256 devices in a mesh: gx: 16 (over z_hi, x), gy: 4 (over z_lo, core), gz: 4 (over y).
Axes of the slice: x: 4, y: 4, z: 8 (z_hi: 4, z_lo: 2; z = z_hi * 2 + z_lo), core: 2. Of those that a mesh axis runs over, the one named last changes fastest.
Arguments:
- density: float32 [256, 64, 512], P('gx', 'gy', 'gz'), may hold values from 0.8 to 1.2
- momentum: float32 [3, 256, 64, 512], P(None, 'gx', 'gy', 'gz'), may hold values from -1.5 to 1.5
- energy: float32 [256, 64, 512], P('gx', 'gy', 'gz'), may hold values from 2.5 to 3.5
- acoustic: float32 [4, 32, 16, 16, 512], P(None, 'gx', 'gy', 'gz'), may hold values from -3 to 3
- tile_slot: int32 [16, 4, 4, 8], P('gx', 'gy', 'gz'), may hold values from 0 to 63, as said below
- tile_element: int32 [16, 4, 4, 8], P('gx', 'gy', 'gz'), may hold values from 0 to 31
Outputs:
- density_next: float32 [256, 64, 512], P('gx', 'gy', 'gz')
- momentum_next: float32 [3, 256, 64, 512], P(None, 'gx', 'gy', 'gz')
- energy_next: float32 [256, 64, 512], P('gx', 'gy', 'gz')
- acoustic_next: float32 [4, 32, 16, 16, 512], P(None, 'gx', 'gy', 'gz')
The draws below stay inside these ranges and needn't reach their ends.
Inputs may be any that keep to these rules, and one draw needn't show every extreme that they name: `tile_slot`: within one device's list the slots are distinct, so at most 4 tiles of one device go to any one device; every device sends exactly 4 of its 8 tiles to one device along gx; its other 4 tiles go to distinct slots of other devices.
All inputs are finite; a program needn't handle non-finite values.
Results may differ from the reference program's by a relative error of at most 0.0001.
Values sent between devices are 32-bit elements; how exact they have to be, the bound alone decides.
A program may use at most 128 MiB of HBM per device.

```python
import jax
import jax.numpy as jnp
import numpy as np
from jax import lax

CX = 16
CY = 16
CZ = 128
EX = 2
EY = 4
EZ = 4
ELEMENT_NODES = 512
NX = 256
NY = 64
NZ = 512
STREAM_ELEMENTS = 32
CROSS_ELEMENTS = 16
SPAN_ELEMENTS = 16
ELEM_DEV = 32
TILES_DEV = 8
CAP = 4
N_GX = 16
N_GY = 4
N_GZ = 4


def draw_tile_slot(key, part):
    slots = N_GX * CAP
    keys = jax.random.split(key, N_GX * N_GY * N_GZ)

    def single(device_key):
        first_key, second_key, third_key = jax.random.split(device_key, 3)
        leading = jax.random.randint(first_key, (), 0, N_GX)
        ranking = jax.random.permutation(second_key, slots)
        number = jnp.arange(slots)
        owned = number // CAP == leading
        scores = jnp.where(owned, number % CAP, ranking + CAP)
        chosen = jnp.argsort(scores, stable=True)[:TILES_DEV]
        return jax.random.permutation(third_key, chosen).astype(jnp.int32)
    return jax.vmap(single)(keys).reshape(N_GX, N_GY, N_GZ, TILES_DEV)


def plant(values, own_key, smallest, high):
    longest = values.shape.index(max(values.shape))
    spots = []
    for shift in (0, 1):
        where = [jax.random.randint(jax.random.fold_in(own_key, axis), (), 0, length) for axis, length in enumerate(values.shape)]
        where[longest] = (where[longest] + shift) % values.shape[longest]
        spots.append(tuple(where))
    return values.at[spots[0]].set(smallest).at[spots[1]].set(high)


def block_levels(rng, shape, cuts, least, largest):
    level, own = 1.0, jax.random.fold_in(rng, 6)
    for axis_at, parts in cuts:
        heights = jnp.exp(jax.random.uniform(jax.random.fold_in(own, axis_at), (parts,), jnp.float32, least / len(cuts), largest / len(cuts)))
        level = level * jnp.repeat(heights, shape[axis_at] // parts).reshape([-1 if axis == axis_at else 1 for axis in range(len(shape))])
    return level


def gaussian(key, dims, spread, bound, cuts=(), kind=jnp.bfloat16):
    gain = block_levels(key, dims, cuts, -0.22, 0.18) if cuts else 1.0
    entries = jax.random.normal(key, dims, jnp.float32) * spread * gain
    return jnp.minimum(jnp.maximum(entries, -bound), bound).astype(kind)


def setup_inputs(seed: int = 0) -> dict:
    key_of = jax.random.split(jax.random.key(seed), 7)
    return {
        "density": jnp.clip(0.8 + 0.40000004 * jax.random.uniform(key_of[0], (NX, NY, NZ), jnp.float32) ** block_levels(key_of[0], (NX, NY, NZ), ((0, 16), (1, 4), (2, 4)), -0.2, 0.2), 0.8, 1.2),
        "momentum": gaussian(key_of[1], (3, NX, NY, NZ), 0.3, 1.5, ((1, 16), (2, 4), (3, 4)), jnp.float32),
        "energy": jnp.clip(2.5 + 1.0 * jax.random.uniform(key_of[2], (NX, NY, NZ), jnp.float32) ** block_levels(key_of[2], (NX, NY, NZ), ((0, 16), (1, 4), (2, 4)), -0.2, 0.2), 2.5, 3.5),
        "acoustic": gaussian(key_of[3], (4, STREAM_ELEMENTS, CROSS_ELEMENTS, SPAN_ELEMENTS, ELEMENT_NODES), 0.5, 3.0, ((1, 16), (2, 4), (3, 4)), jnp.float32),
        "tile_slot": draw_tile_slot(jax.random.fold_in(key_of[6], 71), 0),
        "tile_element": plant(jax.random.randint(key_of[5], (N_GX, N_GY, N_GZ, TILES_DEV), 0, ELEM_DEV), jax.random.fold_in(key_of[5], 1), 0, ELEM_DEV - 1).astype(jnp.int32),
    }


heat_ratio = 1.4
flow_step = 0.05
viscosity = 0.2
sound_step = 0.02
lift_factor = 28.0
source_gain = 40.0


def derivative_numbers():
    order = 7
    points = np.array([-1.0, -0.8717401485096066, -0.5917001814331423, -0.2092992179024789,
                       0.2092992179024789, 0.5917001814331423, 0.8717401485096066, 1.0])
    previous = np.ones(8)
    current = points * 1.0
    for degree in range(1, order):
        following = ((2 * degree + 1) * points * current - degree * previous) / (degree + 1)
        previous = current
        current = following
    values = current
    table = np.zeros((8, 8))
    for row in range(8):
        for column_strip in range(8):
            if row != column_strip:
                table[row, column_strip] = values[row] / (values[column_strip] * (points[row] - points[column_strip]))
    table[0, 0] = -order * (order + 1) / 4.0
    table[order, order] = order * (order + 1) / 4.0
    return table


def node_tables():
    table = derivative_numbers()
    identity = np.eye(8)
    along_tables = [np.kron(np.kron(table, identity), identity).T,
                    np.kron(np.kron(identity, table), identity).T,
                    np.kron(np.kron(identity, identity), table).T]
    numbers = np.arange(512).reshape(8, 8, 8)
    face_nodes = [numbers[0, :, :], numbers[7, :, :], numbers[:, 0, :],
                  numbers[:, 7, :], numbers[:, :, 0], numbers[:, :, 7]]
    selector = np.zeros((512, 384))
    for face in range(6):
        flat = face_nodes[face].reshape(-1)
        selector[flat, face * 64 + np.arange(64)] = 1.0
    derivs = [jnp.asarray(item, dtype=jnp.float32) for item in along_tables]
    return derivs, jnp.asarray(selector, dtype=jnp.float32), jnp.asarray(selector.T, dtype=jnp.float32)


def strip(padded, axis_dim):
    index = [slice(None), slice(1, -1), slice(1, -1), slice(1, -1)]
    index[axis_dim + 1] = slice(None)
    return padded[tuple(index)]


def shifted(array, axis_dim, upper):
    index = [slice(None)] * 4
    index[axis_dim + 1] = slice(2, None) if upper else slice(None, -2)
    return array[tuple(index)]


def tendency(padded):
    interior = padded[:, 1:-1, 1:-1, 1:-1]
    divergence = jnp.zeros_like(interior)
    laplace = jnp.zeros_like(interior)
    for axis_dim in range(3):
        section = strip(padded, axis_dim)
        mass = section[0]
        moment = section[1:4]
        energy_s = section[4]
        along = moment[axis_dim] / mass
        pressure = (heat_ratio - 1.0) * (energy_s - 0.5 * jnp.sum(moment * moment, axis=0) / mass)
        moment_flux = moment * along
        moment_flux = moment_flux.at[axis_dim].add(pressure)
        flux_terms = jnp.concatenate([moment[axis_dim][None], moment_flux, ((energy_s + pressure) * along)[None]], axis=0)
        divergence = divergence + 0.5 * (shifted(flux_terms, axis_dim, True) - shifted(flux_terms, axis_dim, False))
        laplace = laplace + shifted(section, axis_dim, True) + shifted(section, axis_dim, False)
    return -divergence + viscosity * (laplace - 6.0 * interior)


def velocity_of(portion):
    return portion[1:4] / portion[0]


def lamb_vector(padded):
    grads = []
    for axis_dim in range(3):
        speeds = velocity_of(strip(padded[:4], axis_dim))
        grads.append(0.5 * (shifted(speeds, axis_dim, True) - shifted(speeds, axis_dim, False)))
    centre = velocity_of(padded[:4, 1:-1, 1:-1, 1:-1])
    vort_x = grads[1][2] - grads[2][1]
    vort_y = grads[2][0] - grads[0][2]
    vort_z = grads[0][1] - grads[1][0]
    return jnp.stack([vort_y * centre[2] - vort_z * centre[1],
                      vort_z * centre[0] - vort_x * centre[2],
                      vort_x * centre[1] - vort_y * centre[0]], axis=0)


def advance_inner_steps(padded):
    first = padded[:, 1:-1, 1:-1, 1:-1] + flow_step * tendency(padded)
    second = 0.5 * (padded[:, 2:-2, 2:-2, 2:-2] + first[:, 1:-1, 1:-1, 1:-1] + flow_step * tendency(first))
    return second[:, 1:-1, 1:-1, 1:-1], lamb_vector(second)


def apply_table(field, table):
    return jnp.einsum("...n,nm->...m", field, table, precision=lax.Precision.HIGHEST)


def acoustic_tendency(state, source_term, extend):
    derivs, selector, lifting = node_tables()
    pressure = state[0]
    rate_p = -(apply_table(state[1], derivs[0]) + apply_table(state[2], derivs[1]) + apply_table(state[3], derivs[2]))
    rate_vel = [-apply_table(pressure, derivs[axis_dim]) - source_gain * source_term[axis_dim] for axis_dim in range(3)]
    faces = apply_table(state, selector)
    wide = extend(faces)
    upper_nb = [wide[:, 2:, 1:-1, 1:-1, 0:64], wide[:, 1:-1, 2:, 1:-1, 128:192], wide[:, 1:-1, 1:-1, 2:, 256:320]]
    lower_nb = [wide[:, :-2, 1:-1, 1:-1, 64:128], wide[:, 1:-1, :-2, 1:-1, 192:256], wide[:, 1:-1, 1:-1, :-2, 320:384]]
    p_parts = []
    for axis_dim in range(3):
        comp = axis_dim + 1
        own_low = faces[..., 128 * axis_dim:128 * axis_dim + 64]
        own_high = faces[..., 128 * axis_dim + 64:128 * axis_dim + 128]
        right = upper_nb[axis_dim]
        left = lower_nb[axis_dim]
        p_high = 0.5 * (own_high[0] + right[0]) + 0.5 * (own_high[comp] - right[comp])
        u_high = 0.5 * (own_high[comp] + right[comp]) + 0.5 * (own_high[0] - right[0])
        p_low = 0.5 * (left[0] + own_low[0]) + 0.5 * (left[comp] - own_low[comp])
        u_low = 0.5 * (left[comp] + own_low[comp]) + 0.5 * (left[0] - own_low[0])
        p_parts.append(lift_factor * (u_low - own_low[comp]))
        p_parts.append(-lift_factor * (u_high - own_high[comp]))
        vel_pair = jnp.concatenate([lift_factor * (p_low - own_low[0]), -lift_factor * (p_high - own_high[0])], axis=-1)
        rate_vel[axis_dim] = rate_vel[axis_dim] + apply_table(vel_pair, lifting[128 * axis_dim:128 * axis_dim + 128])
    rate_p = rate_p + apply_table(jnp.concatenate(p_parts, axis=-1), lifting)
    return jnp.stack([rate_p] + rate_vel, axis=0)


def acoustic_step(state, source_term, extend):
    middle = state + sound_step * acoustic_tendency(state, source_term, extend)
    return 0.5 * (state + middle + sound_step * acoustic_tendency(middle, source_term, extend))


def wrap_faces(faces):
    return jnp.pad(faces, ((0, 0), (1, 1), (1, 1), (1, 1), (0, 0)), mode="wrap")


def reference(density, momentum, energy, acoustic, tile_slot, tile_element):
    state = jnp.concatenate([density[None], momentum, energy[None]], axis=0)
    padded = jnp.pad(state, ((0, 0), (3, 3), (3, 3), (3, 3)), mode="wrap")

    def slab_window(index):
        portion = lax.dynamic_slice_in_dim(padded, index * CX, CX + 6, axis=1)
        new_state, lamb_field = advance_inner_steps(portion)
        coarse = lamb_field.reshape(3, CX // 2, 2, NY // 2, 2, NZ // 2, 2).mean(axis=(2, 4, 6))
        grouped = coarse.reshape(3, CX // 16, 8, N_GY, CY // 16, 8, N_GZ, CZ // 16, 8)
        grouped = grouped.transpose(3, 6, 1, 4, 7, 0, 2, 5, 8).reshape(N_GY, N_GZ, TILES_DEV, 1536)
        return new_state, grouped

    slabs, tiles = lax.map(slab_window, jnp.arange(N_GX, dtype=jnp.int32))
    new_state = slabs.transpose(1, 0, 2, 3, 4).reshape(5, NX, NY, NZ)
    shape_ids = (N_GX, N_GY, N_GZ, TILES_DEV)
    peer = (tile_slot // CAP).astype(jnp.int32)
    row_y = jnp.broadcast_to(jnp.arange(N_GY, dtype=jnp.int32)[None, :, None, None], shape_ids)
    row_z = jnp.broadcast_to(jnp.arange(N_GZ, dtype=jnp.int32)[None, None, :, None], shape_ids)
    sources = jnp.zeros((N_GX, N_GY, N_GZ, ELEM_DEV, 1536), jnp.float32)
    sources = sources.at[peer, row_y, row_z, tile_element.astype(jnp.int32)].add(tiles)
    source_term = sources.reshape(N_GX, N_GY, N_GZ, EX, EY, EZ, 3, 512).transpose(6, 0, 3, 1, 4, 2, 5, 7)
    source_term = source_term.reshape(3, STREAM_ELEMENTS, CROSS_ELEMENTS, SPAN_ELEMENTS, 512)
    acoustic_next = acoustic_step(acoustic, source_term, wrap_faces)
    return new_state[0], new_state[1:4], new_state[4], acoustic_next
```

```python
import functools

import jax
import jax.numpy as jnp
import ml_dtypes
import numpy as np
from jax import lax
from jax.experimental import pallas as pl
from jax.experimental.pallas import tpu as pltpu
from jax.sharding import PartitionSpec as P

MESH = pl.DeviceIdType.MESH
F32 = jnp.float32
BF16 = jnp.bfloat16

flow_step = 0.05
viscosity = 0.2
sound_step = 0.02
lift_factor = 28.0
source_gain = 40.0
TILE_LANES = 1664


def derivative_numbers():
    order = 7
    points = np.array(
        [
            -1.0,
            -0.8717401485096066,
            -0.5917001814331423,
            -0.2092992179024789,
            0.2092992179024789,
            0.5917001814331423,
            0.8717401485096066,
            1.0,
        ]
    )
    previous = np.ones(8)
    current = points * 1.0
    for degree in range(1, order):
        following = ((2 * degree + 1) * points * current - degree * previous) / (degree + 1)
        previous = current
        current = following
    table = np.zeros((8, 8))
    for row in range(8):
        for column in range(8):
            if row != column:
                table[row, column] = current[row] / (
                    current[column] * (points[row] - points[column])
                )
    table[0, 0] = -order * (order + 1) / 4.0
    table[order, order] = order * (order + 1) / 4.0
    return table


def split_table(table):
    table = table.astype(np.float32)
    high = table.astype(ml_dtypes.bfloat16)
    low = (table - high.astype(np.float32)).astype(ml_dtypes.bfloat16)
    return high, low


def tables():
    table = derivative_numbers()
    eye = np.eye(8)
    along_x = np.kron(np.kron(table, eye), eye).T
    along_y = np.kron(np.kron(np.eye(4), table), eye).T
    along_z = np.kron(np.kron(np.eye(4), eye), table).T
    order = np.zeros((512, 512), ml_dtypes.bfloat16)
    for c in range(8):
        for ab in range(64):
            order[c * 64 + ab, ab * 8 + c] = 1.0
    return (*split_table(along_x), *split_table(along_y), *split_table(along_z), order)


def iota(shape, dim):
    return lax.broadcasted_iota(jnp.int32, shape, dim)


def fluxes(state):
    rho, mx, my, mz, energy = state
    inverse = 1.0 / rho
    vx, vy, vz = mx * inverse, my * inverse, mz * inverse
    pressure = 0.4 * (energy - 0.5 * (mx * vx + my * vy + mz * vz))
    total = energy + pressure
    xy, xz, yz = mx * vy, mx * vz, my * vz
    return (
        [mx, mx * vx + pressure, xy, xz, total * vx],
        [my, xy, my * vy + pressure, yz, total * vy],
        [mz, xz, yz, mz * vz + pressure, total * vz],
    )


def halves(value):
    high = value.astype(BF16).astype(F32)
    return high, value - high


def kernel(
    zh_count, x_count, gy_count, gz_count,
    rho_hbm, mom_hbm, energy_hbm, sound_hbm, slot_ref, element_ref,
    dxh_hbm, dxl_hbm, dyh_hbm, dyl_hbm, dzh_hbm, dzl_hbm, order_hbm,
    rho_out, mom_out, energy_out, sound_out,
    s0, s1, s2, vel, vort, mref, fref, tiles,
    hx, hy, hz, sy, sz, ax, ay, az, axs, ays, azs,
    stage, q0, q1, n0, chars, near,
    dxh, dxl, dyh, dyl, dzh, dzl, order,
    in_sem, out_sem, flow_send, flow_recv, face_send, face_recv, tile_send, tile_recv,
):
    gx, gy, gz = lax.axis_index("gx"), lax.axis_index("gy"), lax.axis_index("gz")
    gx_count = zh_count * x_count
    zh, xi = gx // x_count, lax.rem(gx, x_count)

    def at_x(step):
        return (lax.rem(gx + step + gx_count, gx_count), gy, gz)

    def at_y(step):
        return (gx, lax.rem(gy + step + gy_count, gy_count), gz)

    def at_z(step):
        return (gx, gy, lax.rem(gz + step + gz_count, gz_count))

    def at_zh(step):
        return (lax.rem(zh + step, zh_count) * x_count + xi, gy, gz)

    def at_xi(step):
        return (zh * x_count + lax.rem(xi + step, x_count), gy, gz)

    loads = [
        (rho_hbm, s0.at[0]), (mom_hbm, s0.at[1:4]), (energy_hbm, s0.at[4]), (sound_hbm, stage),
        (order_hbm, order), (dxh_hbm, dxh), (dxl_hbm, dxl), (dyh_hbm, dyh), (dyl_hbm, dyl),
        (dzh_hbm, dzh), (dzl_hbm, dzl),
    ]
    loads = [pltpu.make_async_copy(a, b, in_sem.at[i]) for i, (a, b) in enumerate(loads)]
    for load in loads:
        load.start()

    barrier = pltpu.get_barrier_semaphore()
    partners = [at_x(-1), at_x(1), at_y(-1), at_y(1), at_z(-1), at_z(1)]
    partners += [at_zh(k) for k in range(1, zh_count)] + [at_xi(j) for j in range(1, x_count)]
    for partner in partners:
        pl.semaphore_signal(barrier, inc=1, device_id=partner, device_id_type=MESH)

    lane = iota((16, 128), 1)
    row = iota((16, 128), 0)
    odd = lax.rem(lane, 2) == 1
    edge = (lane == 0) | (lane == 127)
    pair = lane // 2

    pending = []

    def send(src, dst, send_sem, recv_sem, device):
        copy = pltpu.make_async_remote_copy(
            src_ref=src, dst_ref=dst, send_sem=send_sem, recv_sem=recv_sem,
            device_id=device, device_id_type=MESH,
        )
        copy.start()
        pending.append(copy)
        return copy

    def flow_sends(turn, x_source, comps):
        def go(i, src, dst, device):
            return send(src, dst, flow_send.at[turn, i], flow_recv.at[turn, i], device)

        return [
            go(0, x_source(240), hx.at[turn, 0, comps], at_x(1)),
            go(1, x_source(0), hx.at[turn, 1, comps], at_x(-1)),
            go(2, sy.at[turn, 0, comps], hy.at[turn, 0, comps], at_y(1)),
            go(3, sy.at[turn, 1, comps], hy.at[turn, 1, comps], at_y(-1)),
            go(4, sz.at[turn, comps], hz.at[turn, 0, comps], at_z(1)),
            go(5, sz.at[turn, comps], hz.at[turn, 1, comps], at_z(-1)),
        ]

    def slab(x):
        return pl.ds(pl.multiple_of(x * 16, 16), 16)

    def pack_lanes(packed, values, x):
        here = pair == x
        return [jnp.where(here, pltpu.roll(v, 2 * x + 1, 1), p) for p, v in zip(packed, values)]

    def pack_rows(turn, ref, comps):
        for c in comps:
            sy[turn, 0, c] = ref[c, pl.ds(15, 16, stride=16), :]
            sy[turn, 1, c] = ref[c, pl.ds(0, 16, stride=16), :]

    for load in loads[:3]:
        load.wait()
    pack_rows(0, s0, range(5))

    def pack_first(x, packed):
        return pack_lanes(packed, [s0[c, slab(x), :] for c in range(5)], x)

    first_slab = [s0[c, 0:16, :] for c in range(5)]
    for c, value in enumerate(lax.fori_loop(0, 16, pack_first, first_slab)):
        sz[0, c] = value
    pl.semaphore_wait(barrier, len(partners))
    every = pl.ds(0, 5)
    round_0 = flow_sends(0, lambda r: s0.at[:, r : r + 16, :], every)

    def face_sends(turn, q):
        for d in range(3):
            for j in range(4):
                block = slice(128 * j, 128 * j + 128)
                chars[0, d, j] = q[0, :, block] - q[1 + d, :, block]
                chars[1, d, j] = q[0, :, block] + q[1 + d, :, block]
        axs[turn, 0] = chars[0, 0, 0, 0:16, :]
        axs[turn, 1] = chars[1, 0, 3, 16:32, :]
        for side, top in ((0, 0), (1, 12)):
            for j in range(4):
                block = slice(128 * j, 128 * j + 128)
                ays[turn, side, 0:4, block] = chars[side, 1, j, top : top + 4, :]
                ays[turn, side, 4:8, block] = chars[side, 1, j, top + 16 : top + 20, :]
                azs[turn, side, :, block] = chars[side, 2, j, pl.ds(3 * side, 8, stride=4), :]

        def go(i, src, dst, device):
            return send(src, dst, face_send.at[turn, i], face_recv.at[turn, i], device)

        return [
            go(0, axs.at[turn, 0], ax.at[turn, 0], at_x(-1)),
            go(1, axs.at[turn, 1], ax.at[turn, 1], at_x(1)),
            go(2, ays.at[turn, 0], ay.at[turn, 0], at_y(-1)),
            go(3, ays.at[turn, 1], ay.at[turn, 1], at_y(1)),
            go(4, azs.at[turn, 0], az.at[turn, 0], at_z(-1)),
            go(5, azs.at[turn, 1], az.at[turn, 1], at_z(1)),
        ]

    def apply3(value, high, low):
        rows = value.shape[0]
        top, rest = halves(value)
        both = jnp.concatenate([top, rest], axis=0).astype(BF16)
        part = jnp.dot(both, high, preferred_element_type=F32)
        return (
            part[:rows] + part[rows:]
            + jnp.dot(top.astype(BF16), low, preferred_element_type=F32)
        )

    def derivative(d, value):
        if d == 0:
            return apply3(value, dxh[...], dxl[...])
        high, low = (dyh, dyl) if d == 1 else (dzh, dzl)
        split = [apply3(value[:, s : s + 256], high[...], low[...]) for s in (0, 256)]
        return jnp.concatenate(split, axis=1)

    lane32 = iota((32, 128), 1)

    def rates(q, out, gain, base, copies, turn, with_pressure):
        total = None
        for d in range(3):
            if with_pressure:
                both = derivative(d, jnp.concatenate([q[0], q[1 + d]], axis=0))
                out[1 + d] = base(1 + d) - gain * both[:32]
                both = both[32:]
            else:
                both = derivative(d, q[1 + d])
                out[1 + d] = base(1 + d)
            total = both if total is None else total + both
        out[0] = base(0) - gain * total
        for side, d, move in ((0, 1, 28), (1, 1, 4), (0, 2, 31), (1, 2, 1)):
            for j in range(4):
                near[side, d - 1, j] = pltpu.roll(chars[side, d, j], move, 0)
        for copy in copies:
            copy.wait_recv()
        for side, top in ((0, 12), (1, 0)):
            for j in range(4):
                block = slice(128 * j, 128 * j + 128)
                near[side, 0, j, top : top + 4, :] = ay[turn, side, 0:4, block]
                near[side, 0, j, top + 16 : top + 20, :] = ay[turn, side, 4:8, block]
                near[side, 1, j, pl.ds(3 - 3 * side, 8, stride=4), :] = az[turn, side, :, block]
        k = 0.5 * lift_factor * gain
        other = jnp.concatenate([chars[0, 0, 0, 16:32, :], ax[turn, 0]], axis=0)
        jump = pltpu.roll(other, 64, 1) - chars[0, 0, 3]
        jump = jnp.where(lane32 >= 64, k * jump, 0.0)
        out[0, :, 384:512] += jump
        out[1, :, 384:512] -= jump
        other = jnp.concatenate([ax[turn, 1], chars[1, 0, 3, 0:16, :]], axis=0)
        jump = chars[1, 0, 0] - pltpu.roll(other, 64, 1)
        jump = jnp.where(lane32 < 64, k * jump, 0.0)
        out[0, :, 0:128] -= jump
        out[1, :, 0:128] -= jump
        for d, period, move in ((1, 64, 56), (2, 8, 7)):
            place = lax.rem(lane32, period)
            span = period - move
            for j in range(4):
                block = slice(128 * j, 128 * j + 128)
                high = pltpu.roll(near[0, d - 1, j], move, 1) - chars[0, d, j]
                high = jnp.where(place >= move, k * high, 0.0)
                low = chars[1, d, j] - pltpu.roll(near[1, d - 1, j], 128 - move, 1)
                low = jnp.where(place < span, k * low, 0.0)
                out[0, :, block] += high - low
                out[1 + d, :, block] -= high + low

    loads[3].wait()
    for i in range(32):
        c, part = i // 8, i % 8
        q0[c, 4 * part : 4 * part + 4, :] = stage[i]
    faces_0 = face_sends(0, q0)

    def interior(source, target, gain, base):
        half, visc = 0.5 * gain, viscosity * gain

        def update(x, before, first):
            state = [source[c, slab(x), :] for c in range(5)]
            along_x, along_y, along_z = fluxes(state)
            sums, later = [], []
            for c in range(5):
                soft = visc * state[c]
                acc = base(c, x, state[c]) - 6.0 * soft
                part = half * along_z[c]
                acc += pltpu.roll(jnp.where(lane == 0, 0.0, soft - part), 127, 1)
                acc += pltpu.roll(jnp.where(lane == 127, 0.0, soft + part), 1, 1)
                part = half * along_y[c]
                acc += pltpu.roll(jnp.where(row == 0, 0.0, soft - part), 15, 0)
                acc += pltpu.roll(jnp.where(row == 15, 0.0, soft + part), 1, 0)
                part = half * along_x[c]
                if not first:
                    target[c, slab(x - 1), :] = before[c] + (soft - part)
                    acc += before[5 + c]
                sums.append(acc)
                later.append(soft + part)
            return sums + later

        carry = update(0, None, True)
        carry = lax.fori_loop(1, 16, lambda x, b: update(x, b, False), carry)
        for c in range(5):
            target[c, 240:256, :] = carry[c]

    def boundary(turn, target, gain, copies):
        half, visc = 0.5 * gain, viscosity * gain
        for copy in copies:
            copy.wait_recv()
        lower, upper = [hx[turn, 0, c] for c in range(5)], [hx[turn, 1, c] for c in range(5)]
        low_flux, up_flux = fluxes(lower)[0], fluxes(upper)[0]
        for c in range(5):
            target[c, 0:16, :] += visc * lower[c] + half * low_flux[c]
            target[c, 240:256, :] += visc * upper[c] - half * up_flux[c]
        lower, upper = [hy[turn, 0, c] for c in range(5)], [hy[turn, 1, c] for c in range(5)]
        low_flux, up_flux = fluxes(lower)[1], fluxes(upper)[1]
        for c in range(5):
            target[c, pl.ds(0, 16, stride=16), :] += visc * lower[c] + half * low_flux[c]
            target[c, pl.ds(15, 16, stride=16), :] += visc * upper[c] - half * up_flux[c]
        both = [
            jnp.where(odd, pltpu.roll(hz[turn, 0, c], 1, 1), pltpu.roll(hz[turn, 1, c], 127, 1))
            for c in range(5)
        ]
        flux = fluxes(both)[2]
        return [
            visc * both[c] + jnp.where(odd, half * flux[c], -half * flux[c]) for c in range(5)
        ]

    def add_edges(target, terms, x):
        values = []
        for c in range(5):
            moved = pltpu.roll(terms[c], 127 - 2 * x, 1)
            value = target[c, slab(x), :] + jnp.where(edge, moved, 0.0)
            target[c, slab(x), :] = value
            values.append(value)
        return values

    interior(s0, s1, flow_step, lambda c, x, u: u)
    terms = boundary(0, s1, flow_step, round_0)
    pack_first_slab = [s1[c, 0:16, :] for c in range(5)]

    def finish_first(x, packed):
        return pack_lanes(packed, add_edges(s1, terms, x), x)

    packed = lax.fori_loop(0, 16, finish_first, pack_first_slab)
    for c in range(5):
        sz[1, c] = packed[c]
    pack_rows(1, s1, range(5))
    round_1 = flow_sends(1, lambda r: s1.at[:, r : r + 16, :], every)

    interior(s1, s2, 0.5 * flow_step, lambda c, x, u: 0.5 * (s0[c, slab(x), :] + u))
    terms_2 = boundary(1, s2, 0.5 * flow_step, round_1)

    def finish_second(x, packed):
        values = add_edges(s2, terms_2, x)
        inverse = 1.0 / values[0]
        vx, vy, vz = (values[d] * inverse for d in (1, 2, 3))
        vel[0, slab(x), :], vel[1, slab(x), :], vel[2, slab(x), :] = vy, vz, vx
        return pack_lanes(packed, [vy, vx], x)

    zero = jnp.zeros((16, 128), F32)
    packed = lax.fori_loop(0, 16, finish_second, [zero, zero])
    sz[2, 0], sz[2, 1] = packed
    for i, comp in enumerate((1, 2)):
        sy[2, 0, i] = vel[comp, pl.ds(15, 16, stride=16), :]
        sy[2, 1, i] = vel[comp, pl.ds(0, 16, stride=16), :]
    round_2 = flow_sends(2, lambda r: vel.at[0:2, r : r + 16, :], pl.ds(0, 2))

    stores = [
        pltpu.make_async_copy(s2.at[0], rho_out, out_sem.at[0]),
        pltpu.make_async_copy(s2.at[1:4], mom_out, out_sem.at[1]),
        pltpu.make_async_copy(s2.at[4], energy_out, out_sem.at[2]),
    ]
    for store in stores:
        store.start()

    def dy(f):
        up = pltpu.roll(jnp.where(row == 0, 0.0, f), 15, 0)
        return up - pltpu.roll(jnp.where(row == 15, 0.0, f), 1, 0)

    def dz(f):
        up = pltpu.roll(jnp.where(lane == 0, 0.0, f), 127, 1)
        return up - pltpu.roll(jnp.where(lane == 127, 0.0, f), 1, 1)

    def curl(x, carry):
        vy, vz, vx = (vel[i, slab(x), :] for i in range(3))
        after = slab(jnp.minimum(x + 1, 15))
        before = slab(jnp.maximum(x - 1, 0))
        dx_vy, dx_vz = (
            jnp.where(x < 15, vel[i, after, :], 0.0) - jnp.where(x > 0, vel[i, before, :], 0.0)
            for i in range(2)
        )
        vort[0, slab(x), :] = dy(vz) - dz(vy)
        vort[1, slab(x), :] = dz(vx) - dx_vz
        vort[2, slab(x), :] = dx_vy - dy(vx)
        return carry

    lax.fori_loop(0, 16, curl, 0)
    for copy in round_2:
        copy.wait_recv()
    vort[1, 0:16, :] += hx[2, 0, 1]
    vort[2, 0:16, :] -= hx[2, 0, 0]
    vort[1, 240:256, :] -= hx[2, 1, 1]
    vort[2, 240:256, :] += hx[2, 1, 0]
    vort[0, pl.ds(0, 16, stride=16), :] -= hy[2, 0, 0]
    vort[2, pl.ds(0, 16, stride=16), :] += hy[2, 0, 1]
    vort[0, pl.ds(15, 16, stride=16), :] += hy[2, 1, 0]
    vort[2, pl.ds(15, 16, stride=16), :] -= hy[2, 1, 1]
    side_y, side_x = (
        jnp.where(odd, pltpu.roll(hz[2, 0, i], 1, 1), pltpu.roll(hz[2, 1, i], 127, 1))
        for i in range(2)
    )
    side_y = jnp.where(odd, side_y, -side_y)
    side_x = jnp.where(odd, -side_x, side_x)

    def lamb_pair(a, carry):
        sums = [None] * 3
        for x in (2 * a, 2 * a + 1):
            wx = vort[0, slab(x), :] + jnp.where(edge, pltpu.roll(side_y, 127 - 2 * x, 1), 0.0)
            wy = vort[1, slab(x), :] + jnp.where(edge, pltpu.roll(side_x, 127 - 2 * x, 1), 0.0)
            wz = vort[2, slab(x), :]
            vy, vz, vx = (vel[i, slab(x), :] for i in range(3))
            parts = (wy * vz - wz * vy, wz * vx - wx * vz, wx * vy - wy * vx)
            sums = [p if s is None else s + p for s, p in zip(sums, parts)]
        for d in range(3):
            mref[d, slab(a), :] = 0.0625 * sums[d]
        return carry

    lax.fori_loop(0, 8, lamb_pair, 0)
    coarse = [
        mref[d, pl.ds(0, 64, stride=2), :] + mref[d, pl.ds(1, 64, stride=2), :] for d in range(3)
    ]
    fref[0] = jnp.transpose(jnp.concatenate([coarse[0], coarse[1]], axis=0))
    fref[1] = jnp.transpose(jnp.concatenate([coarse[2], coarse[2]], axis=0))
    pieces = [
        [
            fref[i, pl.ds(2 * c, 8, stride=16), :] + fref[i, pl.ds(2 * c + 1, 8, stride=16), :]
            for c in range(8)
        ]
        for i in range(2)
    ]
    left = iota((8, 128), 1) < 64
    rows = [[], [], []]
    for j in range(4):
        a, b = pieces[0][2 * j], pieces[0][2 * j + 1]
        rows[0].append(jnp.where(left, a, pltpu.roll(b, 64, 1)))
        rows[1].append(jnp.where(left, pltpu.roll(a, 64, 1), b))
        rows[2].append(jnp.where(left, pieces[1][2 * j], pieces[1][2 * j + 1]))
    own = jnp.concatenate([jnp.concatenate(r, axis=1) for r in rows], axis=0)
    high, rest = halves(own)
    middle, low = halves(rest)
    loads[4].wait()
    parts = jnp.concatenate([high, middle, low], axis=0).astype(BF16)
    parts = jnp.dot(parts, order[...], preferred_element_type=F32)
    own = parts[0:24] + parts[24:48] + parts[48:72]
    for d in range(3):
        tiles[gx, :, 512 * d : 512 * d + 512] = own[8 * d : 8 * d + 8]
    row8 = iota((8, 128), 0)
    target = jnp.zeros((8, 128), jnp.int32)
    for t in range(8):
        address = lax.div(slot_ref[0, 0, 0, t], 4) * 32 + element_ref[0, 0, 0, t]
        target = jnp.where(row8 == t, address, target)
    tiles[gx, :, 1536:1664] = target.astype(F32)

    def tile_copy(i, source, device):
        return send(tiles.at[source], tiles.at[source], tile_send.at[i], tile_recv.at[i], device)

    down = [tile_copy(k - 1, gx, at_zh(k)) for k in range(1, zh_count)]
    across = []

    def pass_on(k):
        source = lax.rem(zh - k + zh_count, zh_count) * x_count + xi
        for j in range(1, x_count):
            i = zh_count - 1 + k * (x_count - 1) + j - 1
            across.append(tile_copy(i, source, at_xi(j)))

    pass_on(0)

    for load in loads[5:]:
        load.wait()
    rates(q0, q1, sound_step, lambda c: q0[c], faces_0, 0, True)
    for k in range(1, zh_count):
        down[k - 1].wait_recv()
        pass_on(k)
    faces_1 = face_sends(1, q1)
    rates(q1, n0, 0.5 * sound_step, lambda c: 0.5 * (q0[c] + q1[c]), faces_1, 1, True)

    for copy in across:
        copy.wait_recv()
    gx_tiles = 8 * gx_count
    address = tiles[:, :, 1536:1664].reshape(gx_tiles, 128)
    wanted = (gx * 32 + iota((gx_tiles, 128), 1)).astype(F32)
    picking = jnp.where(address == wanted, 1.0, 0.0)
    picking = jnp.transpose(picking)[0:32].astype(BF16)
    for d in range(3):
        block = tiles[:, :, 512 * d : 512 * d + 512].reshape(gx_tiles, 512)
        high, low = halves(block)
        both = jnp.dot(picking, high.astype(BF16), preferred_element_type=F32)
        both += jnp.dot(picking, low.astype(BF16), preferred_element_type=F32)
        q1[1 + d] = -source_gain * sound_step * both
    q1[0] = jnp.zeros((32, 512), F32)
    faces_2 = face_sends(2, q1)
    rates(q1, q0, 0.5 * sound_step, lambda c: n0[c] + q1[c], faces_2, 2, False)
    for i in range(32):
        c, part = i // 8, i % 8
        stage[i] = q0[c, 4 * part : 4 * part + 4, :]
    stores.append(pltpu.make_async_copy(stage, sound_out, out_sem.at[3]))
    stores[-1].start()
    for copy in pending:
        copy.wait_send()
    for store in stores:
        store.wait()


def solution(mesh):
    gx_count, gy_count, gz_count = (mesh.shape[a] for a in ("gx", "gy", "gz"))
    x_count = 4 if gx_count == 16 else 2
    zh_count = gx_count // x_count
    tile_sends = (zh_count - 1) + zh_count * (x_count - 1)
    consts = tables()

    def on_device(density, momentum, energy, acoustic, tile_slot, tile_element):
        anywhere = pl.BlockSpec(memory_space=pl.ANY)
        scalars = pl.BlockSpec(memory_space=pltpu.SMEM)
        out_shape = (
            jax.ShapeDtypeStruct((256, 128), F32),
            jax.ShapeDtypeStruct((3, 256, 128), F32),
            jax.ShapeDtypeStruct((256, 128), F32),
            jax.ShapeDtypeStruct((32, 4, 512), F32),
        )
        vmem = pltpu.VMEM
        scratch = [
            vmem((5, 256, 128), F32), vmem((5, 256, 128), F32), vmem((5, 256, 128), F32),
            vmem((3, 256, 128), F32), vmem((3, 256, 128), F32), vmem((3, 128, 128), F32),
            vmem((2, 128, 128), F32), vmem((gx_count, 8, TILE_LANES), F32),
            vmem((3, 2, 5, 16, 128), F32), vmem((3, 2, 5, 16, 128), F32),
            vmem((3, 2, 5, 16, 128), F32), vmem((3, 2, 5, 16, 128), F32),
            vmem((3, 5, 16, 128), F32),
            vmem((3, 2, 16, 128), F32), vmem((3, 2, 8, 512), F32), vmem((3, 2, 8, 512), F32),
            vmem((3, 2, 16, 128), F32), vmem((3, 2, 8, 512), F32), vmem((3, 2, 8, 512), F32),
            vmem((32, 4, 512), F32), vmem((4, 32, 512), F32), vmem((4, 32, 512), F32),
            vmem((4, 32, 512), F32), vmem((2, 3, 4, 32, 128), F32), vmem((2, 2, 4, 32, 128), F32),
            vmem((512, 512), BF16), vmem((512, 512), BF16), vmem((256, 256), BF16),
            vmem((256, 256), BF16), vmem((256, 256), BF16), vmem((256, 256), BF16),
            vmem((512, 512), BF16),
            pltpu.SemaphoreType.DMA((11,)), pltpu.SemaphoreType.DMA((4,)),
            pltpu.SemaphoreType.DMA((3, 6)), pltpu.SemaphoreType.DMA((3, 6)),
            pltpu.SemaphoreType.DMA((3, 6)), pltpu.SemaphoreType.DMA((3, 6)),
            pltpu.SemaphoreType.DMA((tile_sends,)), pltpu.SemaphoreType.DMA((tile_sends,)),
        ]
        outs = pl.pallas_call(
            functools.partial(kernel, zh_count, x_count, gy_count, gz_count),
            out_shape=out_shape,
            in_specs=[anywhere] * 4 + [scalars] * 2 + [anywhere] * 7,
            out_specs=[anywhere] * 4,
            scratch_shapes=scratch,
            compiler_params=pltpu.CompilerParams(
                collective_id=0, has_side_effects=True, vmem_limit_bytes=60 * 2**20
            ),
            cost_estimate=pl.CostEstimate(
                flops=10**9, bytes_accessed=4 * 2**20, transcendentals=0
            ),
        )(
            density.reshape(256, 128), momentum.reshape(3, 256, 128), energy.reshape(256, 128),
            acoustic.reshape(32, 4, 512), tile_slot, tile_element,
            *[jnp.asarray(c) for c in consts],
        )
        return (
            outs[0].reshape(16, 16, 128), outs[1].reshape(3, 16, 16, 128),
            outs[2].reshape(16, 16, 128), outs[3].reshape(4, 2, 4, 4, 512),
        )

    in_specs = (
        P("gx", "gy", "gz"), P(None, "gx", "gy", "gz"), P("gx", "gy", "gz"),
        P(None, "gx", "gy", "gz", None), P("gx", "gy", "gz", None), P("gx", "gy", "gz", None),
    )
    out_specs = (
        P("gx", "gy", "gz"), P(None, "gx", "gy", "gz"), P("gx", "gy", "gz"),
        P(None, "gx", "gy", "gz", None),
    )
    return jax.shard_map(
        on_device, mesh=mesh, in_specs=in_specs, out_specs=out_specs, check_vma=False
    )
```

```python
import functools

import jax
import jax.numpy as jnp
import ml_dtypes
import numpy as np
from jax import lax
from jax.experimental import pallas as pl
from jax.experimental.pallas import tpu as pltpu
from jax.sharding import PartitionSpec as P

MESH = pl.DeviceIdType.MESH
F32 = jnp.float32
BF16 = jnp.bfloat16

flow_step = 0.05
viscosity = 0.2
sound_step = 0.02
lift_factor = 28.0
source_gain = 40.0
TILE_LANES = 1664


def derivative_numbers():
    order = 7
    points = np.array(
        [
            -1.0,
            -0.8717401485096066,
            -0.5917001814331423,
            -0.2092992179024789,
            0.2092992179024789,
            0.5917001814331423,
            0.8717401485096066,
            1.0,
        ]
    )
    previous = np.ones(8)
    current = points * 1.0
    for degree in range(1, order):
        following = ((2 * degree + 1) * points * current - degree * previous) / (degree + 1)
        previous = current
        current = following
    table = np.zeros((8, 8))
    for row in range(8):
        for column in range(8):
            if row != column:
                table[row, column] = current[row] / (
                    current[column] * (points[row] - points[column])
                )
    table[0, 0] = -order * (order + 1) / 4.0
    table[order, order] = order * (order + 1) / 4.0
    return table


def split_table(table):
    table = table.astype(np.float32)
    high = table.astype(ml_dtypes.bfloat16)
    low = (table - high.astype(np.float32)).astype(ml_dtypes.bfloat16)
    return high, low


def tables():
    table = derivative_numbers()
    eye = np.eye(8)
    along_x = np.kron(np.kron(table, eye), eye).T
    along_y = np.kron(np.kron(np.eye(4), table), eye).T
    along_z = np.kron(np.kron(np.eye(4), eye), table).T
    order = np.zeros((512, 512), ml_dtypes.bfloat16)
    for c in range(8):
        for ab in range(64):
            order[c * 64 + ab, ab * 8 + c] = 1.0
    return (*split_table(along_x), *split_table(along_y), *split_table(along_z), order)


def iota(shape, dim):
    return lax.broadcasted_iota(jnp.int32, shape, dim)


def fluxes(state):
    rho, mx, my, mz, energy = state
    inverse = 1.0 / rho
    vx, vy, vz = mx * inverse, my * inverse, mz * inverse
    pressure = 0.4 * (energy - 0.5 * (mx * vx + my * vy + mz * vz))
    total = energy + pressure
    xy, xz, yz = mx * vy, mx * vz, my * vz
    return (
        [mx, mx * vx + pressure, xy, xz, total * vx],
        [my, xy, my * vy + pressure, yz, total * vy],
        [mz, xz, yz, mz * vz + pressure, total * vz],
    )


def halves(value):
    high = value.astype(BF16).astype(F32)
    return high, value - high


def kernel(
    zh_count, x_count, gy_count, gz_count,
    rho_hbm, mom_hbm, energy_hbm, sound_hbm, slot_ref, element_ref,
    dxh_hbm, dxl_hbm, dyh_hbm, dyl_hbm, dzh_hbm, dzl_hbm, order_hbm,
    rho_out, mom_out, energy_out, sound_out,
    s0, s1, s2, vel, vort, mref, fref, tiles,
    hx, hy, hz, sy, sz, ax, ay, az, axs, ays, azs,
    stage, q0, q1, n0, chars, near,
    dxh, dxl, dyh, dyl, dzh, dzl, order,
    in_sem, out_sem, flow_send, flow_recv, face_send, face_recv, tile_send, tile_recv,
):
    gx, gy, gz = lax.axis_index("gx"), lax.axis_index("gy"), lax.axis_index("gz")
    gx_count = zh_count * x_count
    zh, xi = gx // x_count, lax.rem(gx, x_count)

    def at_x(step):
        return (lax.rem(gx + step + gx_count, gx_count), gy, gz)

    def at_y(step):
        return (gx, lax.rem(gy + step + gy_count, gy_count), gz)

    def at_z(step):
        return (gx, gy, lax.rem(gz + step + gz_count, gz_count))

    def at_zh(step):
        return (lax.rem(zh + step, zh_count) * x_count + xi, gy, gz)

    def at_xi(step):
        return (zh * x_count + lax.rem(xi + step, x_count), gy, gz)

    barrier = pltpu.get_barrier_semaphore()
    partners = [at_x(-1), at_x(1), at_y(-1), at_y(1), at_z(-1), at_z(1)]
    partners += [at_zh(k) for k in range(1, zh_count)] + [at_xi(j) for j in range(1, x_count)]
    for partner in partners:
        pl.semaphore_signal(barrier, inc=1, device_id=partner, device_id_type=MESH)

    loads = [
        (rho_hbm, s0.at[0]), (mom_hbm, s0.at[1:4]), (energy_hbm, s0.at[4]), (sound_hbm, stage),
        (order_hbm, order), (dxh_hbm, dxh), (dxl_hbm, dxl), (dyh_hbm, dyh), (dyl_hbm, dyl),
        (dzh_hbm, dzh), (dzl_hbm, dzl),
    ]
    loads = [pltpu.make_async_copy(a, b, in_sem.at[i]) for i, (a, b) in enumerate(loads)]
    for load in loads:
        load.start()

    lane = iota((16, 128), 1)
    row = iota((16, 128), 0)
    odd = lax.rem(lane, 2) == 1
    edge = (lane == 0) | (lane == 127)
    pair = lane // 2

    pending = []

    def send(src, dst, send_sem, recv_sem, device):
        copy = pltpu.make_async_remote_copy(
            src_ref=src, dst_ref=dst, send_sem=send_sem, recv_sem=recv_sem,
            device_id=device, device_id_type=MESH,
        )
        copy.start()
        pending.append(copy)
        return copy

    def flow_go(turn, i, src, dst, device):
        return send(src, dst, flow_send.at[turn, i], flow_recv.at[turn, i], device)

    def sends_x(turn, x_source, comps):
        return [
            flow_go(turn, 0, x_source(240), hx.at[turn, 0, comps], at_x(1)),
            flow_go(turn, 1, x_source(0), hx.at[turn, 1, comps], at_x(-1)),
        ]

    def sends_yz(turn, comps):
        return [
            flow_go(turn, 2, sz.at[turn, comps], hz.at[turn, 0, comps], at_z(1)),
            flow_go(turn, 3, sz.at[turn, comps], hz.at[turn, 1, comps], at_z(-1)),
            flow_go(turn, 4, sy.at[turn, 0, comps], hy.at[turn, 0, comps], at_y(1)),
            flow_go(turn, 5, sy.at[turn, 1, comps], hy.at[turn, 1, comps], at_y(-1)),
        ]

    def slab(x):
        return pl.ds(pl.multiple_of(x * 16, 16), 16)

    def pack_lanes(packed, values, x):
        here = pair == x
        return [jnp.where(here, pltpu.roll(v, 2 * x + 1, 1), p) for p, v in zip(packed, values)]

    def pack_rows(turn, ref, comps):
        for c in comps:
            sy[turn, 0, c] = ref[c, pl.ds(15, 16, stride=16), :]
            sy[turn, 1, c] = ref[c, pl.ds(0, 16, stride=16), :]

    for load in loads[:3]:
        load.wait()
    pack_rows(0, s0, range(5))

    def pack_first(x, packed):
        return pack_lanes(packed, [s0[c, slab(x), :] for c in range(5)], x)

    first_slab = [s0[c, 0:16, :] for c in range(5)]
    for c, value in enumerate(lax.fori_loop(0, 16, pack_first, first_slab)):
        sz[0, c] = value
    pl.semaphore_wait(barrier, len(partners))
    every = pl.ds(0, 5)
    round_x = sends_x(0, lambda r: s0.at[:, r : r + 16, :], every)
    round_yz = sends_yz(0, every)

    def face_sends(turn, q):
        for d in range(3):
            for j in range(4):
                block = slice(128 * j, 128 * j + 128)
                chars[0, d, j] = q[0, :, block] - q[1 + d, :, block]
                chars[1, d, j] = q[0, :, block] + q[1 + d, :, block]
        axs[turn, 0] = chars[0, 0, 0, 0:16, :]
        axs[turn, 1] = chars[1, 0, 3, 16:32, :]
        for side, top in ((0, 0), (1, 12)):
            for j in range(4):
                block = slice(128 * j, 128 * j + 128)
                ays[turn, side, 0:4, block] = chars[side, 1, j, top : top + 4, :]
                ays[turn, side, 4:8, block] = chars[side, 1, j, top + 16 : top + 20, :]
                azs[turn, side, :, block] = chars[side, 2, j, pl.ds(3 * side, 8, stride=4), :]

        def go(i, src, dst, device):
            return send(src, dst, face_send.at[turn, i], face_recv.at[turn, i], device)

        return [
            go(0, axs.at[turn, 0], ax.at[turn, 0], at_x(-1)),
            go(1, axs.at[turn, 1], ax.at[turn, 1], at_x(1)),
            go(2, ays.at[turn, 0], ay.at[turn, 0], at_y(-1)),
            go(3, ays.at[turn, 1], ay.at[turn, 1], at_y(1)),
            go(4, azs.at[turn, 0], az.at[turn, 0], at_z(-1)),
            go(5, azs.at[turn, 1], az.at[turn, 1], at_z(1)),
        ]

    def apply3(value, high, low):
        rows = value.shape[0]
        top, rest = halves(value)
        both = jnp.concatenate([top, rest], axis=0).astype(BF16)
        part = jnp.dot(both, high, preferred_element_type=F32)
        return (
            part[:rows] + part[rows:]
            + jnp.dot(top.astype(BF16), low, preferred_element_type=F32)
        )

    def derivative(d, value):
        if d == 0:
            return apply3(value, dxh[...], dxl[...])
        high, low = (dyh, dyl) if d == 1 else (dzh, dzl)
        split = [apply3(value[:, s : s + 256], high[...], low[...]) for s in (0, 256)]
        return jnp.concatenate(split, axis=1)

    lane32 = iota((32, 128), 1)

    def rates(q, out, gain, base, copies, turn, with_pressure):
        total = None
        for d in range(3):
            if with_pressure:
                both = derivative(d, jnp.concatenate([q[0], q[1 + d]], axis=0))
                out[1 + d] = base(1 + d) - gain * both[:32]
                both = both[32:]
            else:
                both = derivative(d, q[1 + d])
                out[1 + d] = base(1 + d)
            total = both if total is None else total + both
        out[0] = base(0) - gain * total
        for side, d, move in ((0, 1, 28), (1, 1, 4), (0, 2, 31), (1, 2, 1)):
            for j in range(4):
                near[side, d - 1, j] = pltpu.roll(chars[side, d, j], move, 0)
        for copy in copies[2:6]:
            copy.wait_recv()
        for side, top in ((0, 12), (1, 0)):
            for j in range(4):
                block = slice(128 * j, 128 * j + 128)
                near[side, 0, j, top : top + 4, :] = ay[turn, side, 0:4, block]
                near[side, 0, j, top + 16 : top + 20, :] = ay[turn, side, 4:8, block]
                near[side, 1, j, pl.ds(3 - 3 * side, 8, stride=4), :] = az[turn, side, :, block]
        k = 0.5 * lift_factor * gain
        for d, period, move in ((1, 64, 56), (2, 8, 7)):
            place = lax.rem(lane32, period)
            span = period - move
            for j in range(4):
                block = slice(128 * j, 128 * j + 128)
                high = pltpu.roll(near[0, d - 1, j], move, 1) - chars[0, d, j]
                high = jnp.where(place >= move, k * high, 0.0)
                low = chars[1, d, j] - pltpu.roll(near[1, d - 1, j], 128 - move, 1)
                low = jnp.where(place < span, k * low, 0.0)
                out[0, :, block] += high - low
                out[1 + d, :, block] -= high + low
        for copy in copies[0:2]:
            copy.wait_recv()
        other = jnp.concatenate([chars[0, 0, 0, 16:32, :], ax[turn, 0]], axis=0)
        jump = pltpu.roll(other, 64, 1) - chars[0, 0, 3]
        jump = jnp.where(lane32 >= 64, k * jump, 0.0)
        out[0, :, 384:512] += jump
        out[1, :, 384:512] -= jump
        other = jnp.concatenate([ax[turn, 1], chars[1, 0, 3, 0:16, :]], axis=0)
        jump = chars[1, 0, 0] - pltpu.roll(other, 64, 1)
        jump = jnp.where(lane32 < 64, k * jump, 0.0)
        out[0, :, 0:128] -= jump
        out[1, :, 0:128] -= jump

    loads[3].wait()
    for i in range(32):
        c, part = i // 8, i % 8
        q0[c, 4 * part : 4 * part + 4, :] = stage[i]
    faces_0 = face_sends(0, q0)

    def interior(source, target, gain, base):
        half, visc = 0.5 * gain, viscosity * gain

        def update(x, before, first):
            state = [source[c, slab(x), :] for c in range(5)]
            along_x, along_y, along_z = fluxes(state)
            sums, later = [], []
            for c in range(5):
                soft = visc * state[c]
                acc = base(c, x, state[c]) - 6.0 * soft
                part = half * along_z[c]
                acc += pltpu.roll(jnp.where(lane == 0, 0.0, soft - part), 127, 1)
                acc += pltpu.roll(jnp.where(lane == 127, 0.0, soft + part), 1, 1)
                part = half * along_y[c]
                acc += pltpu.roll(jnp.where(row == 0, 0.0, soft - part), 15, 0)
                acc += pltpu.roll(jnp.where(row == 15, 0.0, soft + part), 1, 0)
                part = half * along_x[c]
                if not first:
                    target[c, slab(x - 1), :] = before[c] + (soft - part)
                    acc += before[5 + c]
                sums.append(acc)
                later.append(soft + part)
            return sums + later

        carry = update(0, None, True)
        carry = lax.fori_loop(1, 16, lambda x, b: update(x, b, False), carry)
        for c in range(5):
            target[c, 240:256, :] = carry[c]

    def boundary_yz(turn, target, gain, copies):
        half, visc = 0.5 * gain, viscosity * gain
        for copy in copies:
            copy.wait_recv()
        lower, upper = [hy[turn, 0, c] for c in range(5)], [hy[turn, 1, c] for c in range(5)]
        low_flux, up_flux = fluxes(lower)[1], fluxes(upper)[1]
        for c in range(5):
            target[c, pl.ds(0, 16, stride=16), :] += visc * lower[c] + half * low_flux[c]
            target[c, pl.ds(15, 16, stride=16), :] += visc * upper[c] - half * up_flux[c]
        both = [
            jnp.where(odd, pltpu.roll(hz[turn, 0, c], 1, 1), pltpu.roll(hz[turn, 1, c], 127, 1))
            for c in range(5)
        ]
        flux = fluxes(both)[2]
        return [
            visc * both[c] + jnp.where(odd, half * flux[c], -half * flux[c]) for c in range(5)
        ]

    def boundary_x(turn, target, gain, copies):
        half, visc = 0.5 * gain, viscosity * gain
        outer = []
        for side, rows, copy in ((0, slice(0, 16), copies[0]), (1, slice(240, 256), copies[1])):
            copy.wait_recv()
            state = [hx[turn, side, c] for c in range(5)]
            flux = fluxes(state)[0]
            values = []
            for c in range(5):
                term = half * flux[c] if side == 0 else -half * flux[c]
                value = target[c, rows, :] + (visc * state[c] + term)
                target[c, rows, :] = value
                values.append(value)
            outer.append(values)
        return outer

    def add_edges(target, terms, x):
        values = []
        for c in range(5):
            moved = pltpu.roll(terms[c], 127 - 2 * x, 1)
            value = target[c, slab(x), :] + jnp.where(edge, moved, 0.0)
            target[c, slab(x), :] = value
            values.append(value)
        return values

    interior(s0, s1, flow_step, lambda c, x, u: u)
    terms = boundary_yz(0, s1, flow_step, round_yz)
    packed = [s1[c, 16:32, :] for c in range(5)]
    packed = lax.fori_loop(1, 15, lambda x, p: pack_lanes(p, add_edges(s1, terms, x), x), packed)
    for x in (0, 15):
        add_edges(s1, terms, x)
    outer = boundary_x(0, s1, flow_step, round_x)
    round_x = sends_x(1, lambda r: s1.at[:, r : r + 16, :], every)
    packed = pack_lanes(pack_lanes(packed, outer[0], 0), outer[1], 15)
    for c in range(5):
        sz[1, c] = packed[c]
    pack_rows(1, s1, range(5))
    round_yz = sends_yz(1, every)

    interior(s1, s2, 0.5 * flow_step, lambda c, x, u: 0.5 * (s0[c, slab(x), :] + u))
    terms_2 = boundary_yz(1, s2, 0.5 * flow_step, round_yz)

    def velocity(x, values):
        inverse = 1.0 / values[0]
        vx, vy, vz = (values[d] * inverse for d in (1, 2, 3))
        vel[0, slab(x), :], vel[1, slab(x), :], vel[2, slab(x), :] = vy, vz, vx
        return [vy, vx]

    zero = jnp.zeros((16, 128), F32)
    packed = lax.fori_loop(
        1, 15, lambda x, p: pack_lanes(p, velocity(x, add_edges(s2, terms_2, x)), x), [zero, zero]
    )
    for x in (0, 15):
        add_edges(s2, terms_2, x)
    outer = boundary_x(1, s2, 0.5 * flow_step, round_x)
    outer = [velocity(0, outer[0]), velocity(15, outer[1])]
    round_x = sends_x(2, lambda r: vel.at[0:2, r : r + 16, :], pl.ds(0, 2))
    sz[2, 0], sz[2, 1] = pack_lanes(pack_lanes(packed, outer[0], 0), outer[1], 15)
    for i, comp in enumerate((1, 2)):
        sy[2, 0, i] = vel[comp, pl.ds(15, 16, stride=16), :]
        sy[2, 1, i] = vel[comp, pl.ds(0, 16, stride=16), :]
    round_yz = sends_yz(2, pl.ds(0, 2))

    stores = [
        pltpu.make_async_copy(s2.at[0], rho_out, out_sem.at[0]),
        pltpu.make_async_copy(s2.at[1:4], mom_out, out_sem.at[1]),
        pltpu.make_async_copy(s2.at[4], energy_out, out_sem.at[2]),
    ]
    for store in stores:
        store.start()

    def dy(f):
        up = pltpu.roll(jnp.where(row == 0, 0.0, f), 15, 0)
        return up - pltpu.roll(jnp.where(row == 15, 0.0, f), 1, 0)

    def dz(f):
        up = pltpu.roll(jnp.where(lane == 0, 0.0, f), 127, 1)
        return up - pltpu.roll(jnp.where(lane == 127, 0.0, f), 1, 1)

    def curl(x, carry):
        vy, vz, vx = (vel[i, slab(x), :] for i in range(3))
        after = slab(jnp.minimum(x + 1, 15))
        before = slab(jnp.maximum(x - 1, 0))
        dx_vy, dx_vz = (
            jnp.where(x < 15, vel[i, after, :], 0.0) - jnp.where(x > 0, vel[i, before, :], 0.0)
            for i in range(2)
        )
        vort[0, slab(x), :] = dy(vz) - dz(vy)
        vort[1, slab(x), :] = dz(vx) - dx_vz
        vort[2, slab(x), :] = dx_vy - dy(vx)
        return carry

    lax.fori_loop(0, 16, curl, 0)
    for copy in round_yz:
        copy.wait_recv()
    vort[0, pl.ds(0, 16, stride=16), :] -= hy[2, 0, 0]
    vort[2, pl.ds(0, 16, stride=16), :] += hy[2, 0, 1]
    vort[0, pl.ds(15, 16, stride=16), :] += hy[2, 1, 0]
    vort[2, pl.ds(15, 16, stride=16), :] -= hy[2, 1, 1]
    side_y, side_x = (
        jnp.where(odd, pltpu.roll(hz[2, 0, i], 1, 1), pltpu.roll(hz[2, 1, i], 127, 1))
        for i in range(2)
    )
    side_y = jnp.where(odd, side_y, -side_y)
    side_x = jnp.where(odd, -side_x, side_x)

    def lamb_pair(a, carry):
        sums = [None] * 3
        for x in (2 * a, 2 * a + 1):
            wx = vort[0, slab(x), :] + jnp.where(edge, pltpu.roll(side_y, 127 - 2 * x, 1), 0.0)
            wy = vort[1, slab(x), :] + jnp.where(edge, pltpu.roll(side_x, 127 - 2 * x, 1), 0.0)
            wz = vort[2, slab(x), :]
            vy, vz, vx = (vel[i, slab(x), :] for i in range(3))
            parts = (wy * vz - wz * vy, wz * vx - wx * vz, wx * vy - wy * vx)
            sums = [p if s is None else s + p for s, p in zip(sums, parts)]
        for d in range(3):
            mref[d, slab(a), :] = 0.0625 * sums[d]
        return carry

    lax.fori_loop(1, 7, lamb_pair, 0)
    round_x[0].wait_recv()
    vort[1, 0:16, :] += hx[2, 0, 1]
    vort[2, 0:16, :] -= hx[2, 0, 0]
    lamb_pair(0, 0)
    round_x[1].wait_recv()
    vort[1, 240:256, :] -= hx[2, 1, 1]
    vort[2, 240:256, :] += hx[2, 1, 0]
    lamb_pair(7, 0)
    coarse = [
        mref[d, pl.ds(0, 64, stride=2), :] + mref[d, pl.ds(1, 64, stride=2), :] for d in range(3)
    ]
    fref[0] = jnp.transpose(jnp.concatenate([coarse[0], coarse[1]], axis=0))
    fref[1] = jnp.transpose(jnp.concatenate([coarse[2], coarse[2]], axis=0))
    pieces = [
        [
            fref[i, pl.ds(2 * c, 8, stride=16), :] + fref[i, pl.ds(2 * c + 1, 8, stride=16), :]
            for c in range(8)
        ]
        for i in range(2)
    ]
    left = iota((8, 128), 1) < 64
    rows = [[], [], []]
    for j in range(4):
        a, b = pieces[0][2 * j], pieces[0][2 * j + 1]
        rows[0].append(jnp.where(left, a, pltpu.roll(b, 64, 1)))
        rows[1].append(jnp.where(left, pltpu.roll(a, 64, 1), b))
        rows[2].append(jnp.where(left, pieces[1][2 * j], pieces[1][2 * j + 1]))
    own = jnp.concatenate([jnp.concatenate(r, axis=1) for r in rows], axis=0)
    high, rest = halves(own)
    middle, low = halves(rest)
    loads[4].wait()
    parts = jnp.concatenate([high, middle, low], axis=0).astype(BF16)
    parts = jnp.dot(parts, order[...], preferred_element_type=F32)
    own = parts[0:24] + parts[24:48] + parts[48:72]
    for d in range(3):
        tiles[gx, :, 512 * d : 512 * d + 512] = own[8 * d : 8 * d + 8]
    row8 = iota((8, 128), 0)
    target = jnp.zeros((8, 128), jnp.int32)
    for t in range(8):
        address = lax.div(slot_ref[0, 0, 0, t], 4) * 32 + element_ref[0, 0, 0, t]
        target = jnp.where(row8 == t, address, target)
    tiles[gx, :, 1536:1664] = target.astype(F32)

    def tile_copy(i, source, device):
        return send(tiles.at[source], tiles.at[source], tile_send.at[i], tile_recv.at[i], device)

    down = [tile_copy(k - 1, gx, at_zh(k)) for k in range(1, zh_count)]
    across = []

    def pass_on(k):
        source = lax.rem(zh - k + zh_count, zh_count) * x_count + xi
        for j in range(1, x_count):
            i = zh_count - 1 + k * (x_count - 1) + j - 1
            across.append(tile_copy(i, source, at_xi(j)))

    pass_on(0)

    for load in loads[5:]:
        load.wait()
    rates(q0, q1, sound_step, lambda c: q0[c], faces_0, 0, True)
    for k in range(1, zh_count):
        down[k - 1].wait_recv()
        pass_on(k)
    faces_1 = face_sends(1, q1)
    rates(q1, n0, 0.5 * sound_step, lambda c: 0.5 * (q0[c] + q1[c]), faces_1, 1, True)

    for copy in across:
        copy.wait_recv()
    gx_tiles = 8 * gx_count
    address = tiles[:, :, 1536:1664].reshape(gx_tiles, 128)
    wanted = (gx * 32 + iota((gx_tiles, 128), 1)).astype(F32)
    picking = jnp.where(address == wanted, 1.0, 0.0)
    picking = jnp.transpose(picking)[0:32].astype(BF16)
    for d in range(3):
        block = tiles[:, :, 512 * d : 512 * d + 512].reshape(gx_tiles, 512)
        high, low = halves(block)
        both = jnp.dot(picking, high.astype(BF16), preferred_element_type=F32)
        both += jnp.dot(picking, low.astype(BF16), preferred_element_type=F32)
        q1[1 + d] = -source_gain * sound_step * both
    q1[0] = jnp.zeros((32, 512), F32)
    faces_2 = face_sends(2, q1)
    rates(q1, q0, 0.5 * sound_step, lambda c: n0[c] + q1[c], faces_2, 2, False)
    for i in range(32):
        c, part = i // 8, i % 8
        stage[i] = q0[c, 4 * part : 4 * part + 4, :]
    stores.append(pltpu.make_async_copy(stage, sound_out, out_sem.at[3]))
    stores[-1].start()
    for copy in pending:
        copy.wait_send()
    for store in stores:
        store.wait()


def hand_over(*refs):
    sources, targets, held, sem = refs[0:4], refs[4:8], refs[8:12], refs[12]
    loads = [pltpu.make_async_copy(sources[i], held[i], sem.at[0, i]) for i in range(4)]
    stores = [pltpu.make_async_copy(held[i], targets[i], sem.at[1, i]) for i in range(4)]
    for load in loads:
        load.start()
    for load, store in zip(loads, stores):
        load.wait()
        store.start()
    for store in stores:
        store.wait()


def solution(mesh):
    gx_count, gy_count, gz_count = (mesh.shape[a] for a in ("gx", "gy", "gz"))
    x_count = 4 if gx_count == 16 else 2
    zh_count = gx_count // x_count
    tile_sends = (zh_count - 1) + zh_count * (x_count - 1)
    consts = tables()

    def on_device(density, momentum, energy, acoustic, tile_slot, tile_element):
        anywhere = pl.BlockSpec(memory_space=pl.ANY)
        scalars = pl.BlockSpec(memory_space=pltpu.SMEM)
        out_shape = (
            jax.ShapeDtypeStruct((256, 128), F32),
            jax.ShapeDtypeStruct((3, 256, 128), F32),
            jax.ShapeDtypeStruct((256, 128), F32),
            jax.ShapeDtypeStruct((32, 4, 512), F32),
        )
        vmem = pltpu.VMEM
        scratch = [
            vmem((5, 256, 128), F32), vmem((5, 256, 128), F32), vmem((5, 256, 128), F32),
            vmem((3, 256, 128), F32), vmem((3, 256, 128), F32), vmem((3, 128, 128), F32),
            vmem((2, 128, 128), F32), vmem((gx_count, 8, TILE_LANES), F32),
            vmem((3, 2, 5, 16, 128), F32), vmem((3, 2, 5, 16, 128), F32),
            vmem((3, 2, 5, 16, 128), F32), vmem((3, 2, 5, 16, 128), F32),
            vmem((3, 5, 16, 128), F32),
            vmem((3, 2, 16, 128), F32), vmem((3, 2, 8, 512), F32), vmem((3, 2, 8, 512), F32),
            vmem((3, 2, 16, 128), F32), vmem((3, 2, 8, 512), F32), vmem((3, 2, 8, 512), F32),
            vmem((32, 4, 512), F32), vmem((4, 32, 512), F32), vmem((4, 32, 512), F32),
            vmem((4, 32, 512), F32), vmem((2, 3, 4, 32, 128), F32), vmem((2, 2, 4, 32, 128), F32),
            vmem((512, 512), BF16), vmem((512, 512), BF16), vmem((256, 256), BF16),
            vmem((256, 256), BF16), vmem((256, 256), BF16), vmem((256, 256), BF16),
            vmem((512, 512), BF16),
            pltpu.SemaphoreType.DMA((11,)), pltpu.SemaphoreType.DMA((4,)),
            pltpu.SemaphoreType.DMA((3, 6)), pltpu.SemaphoreType.DMA((3, 6)),
            pltpu.SemaphoreType.DMA((3, 6)), pltpu.SemaphoreType.DMA((3, 6)),
            pltpu.SemaphoreType.DMA((tile_sends,)), pltpu.SemaphoreType.DMA((tile_sends,)),
        ]
        outs = pl.pallas_call(
            functools.partial(kernel, zh_count, x_count, gy_count, gz_count),
            out_shape=out_shape,
            in_specs=[anywhere] * 4 + [scalars] * 2 + [anywhere] * 7,
            out_specs=[anywhere] * 4,
            scratch_shapes=scratch,
            compiler_params=pltpu.CompilerParams(
                collective_id=0, has_side_effects=True, vmem_limit_bytes=60 * 2**20
            ),
            cost_estimate=pl.CostEstimate(
                flops=10**9, bytes_accessed=4 * 2**20, transcendentals=0
            ),
        )(
            density.reshape(256, 128), momentum.reshape(3, 256, 128), energy.reshape(256, 128),
            acoustic.reshape(32, 4, 512), tile_slot, tile_element,
            *[jnp.asarray(c) for c in consts],
        )
        outs = pl.pallas_call(
            hand_over,
            out_shape=out_shape,
            in_specs=[anywhere] * 4,
            out_specs=[anywhere] * 4,
            scratch_shapes=[vmem(o.shape, F32) for o in out_shape]
            + [pltpu.SemaphoreType.DMA((2, 4))],
            compiler_params=pltpu.CompilerParams(vmem_limit_bytes=60 * 2**20),
        )(*outs)
        return (
            outs[0].reshape(16, 16, 128), outs[1].reshape(3, 16, 16, 128),
            outs[2].reshape(16, 16, 128), outs[3].reshape(4, 2, 4, 4, 512),
        )

    in_specs = (
        P("gx", "gy", "gz"), P(None, "gx", "gy", "gz"), P("gx", "gy", "gz"),
        P(None, "gx", "gy", "gz", None), P("gx", "gy", "gz", None), P("gx", "gy", "gz", None),
    )
    out_specs = (
        P("gx", "gy", "gz"), P(None, "gx", "gy", "gz"), P("gx", "gy", "gz"),
        P(None, "gx", "gy", "gz", None),
    )
    return jax.shard_map(
        on_device, mesh=mesh, in_specs=in_specs, out_specs=out_specs, check_vma=False
    )
```

```python
import functools

import jax
import jax.numpy as jnp
import ml_dtypes
import numpy as np
from jax import lax
from jax.experimental import pallas as pl
from jax.experimental.pallas import tpu as pltpu
from jax.sharding import PartitionSpec as P

MESH = pl.DeviceIdType.MESH
F32 = jnp.float32
BF16 = jnp.bfloat16

flow_step = 0.05
viscosity = 0.2
sound_step = 0.02
lift_factor = 28.0
source_gain = 40.0
TILE_LANES = 1664


def derivative_numbers():
    order = 7
    points = np.array(
        [
            -1.0,
            -0.8717401485096066,
            -0.5917001814331423,
            -0.2092992179024789,
            0.2092992179024789,
            0.5917001814331423,
            0.8717401485096066,
            1.0,
        ]
    )
    previous = np.ones(8)
    current = points * 1.0
    for degree in range(1, order):
        following = ((2 * degree + 1) * points * current - degree * previous) / (degree + 1)
        previous = current
        current = following
    table = np.zeros((8, 8))
    for row in range(8):
        for column in range(8):
            if row != column:
                table[row, column] = current[row] / (
                    current[column] * (points[row] - points[column])
                )
    table[0, 0] = -order * (order + 1) / 4.0
    table[order, order] = order * (order + 1) / 4.0
    return table


def split_table(table):
    table = table.astype(np.float32)
    high = table.astype(ml_dtypes.bfloat16)
    low = (table - high.astype(np.float32)).astype(ml_dtypes.bfloat16)
    return high, low


def tables():
    table = derivative_numbers()
    eye = np.eye(8)
    along_x = np.kron(np.kron(table, eye), eye).T
    along_y = np.kron(np.kron(np.eye(4), table), eye).T
    along_z = np.kron(np.kron(np.eye(4), eye), table).T
    order = np.zeros((512, 512), ml_dtypes.bfloat16)
    for c in range(8):
        for ab in range(64):
            order[c * 64 + ab, ab * 8 + c] = 1.0
    return (*split_table(along_x), *split_table(along_y), *split_table(along_z), order)


def iota(shape, dim):
    return lax.broadcasted_iota(jnp.int32, shape, dim)


def fluxes(state):
    rho, mx, my, mz, energy = state
    inverse = 1.0 / rho
    vx, vy, vz = mx * inverse, my * inverse, mz * inverse
    pressure = 0.4 * (energy - 0.5 * (mx * vx + my * vy + mz * vz))
    total = energy + pressure
    xy, xz, yz = mx * vy, mx * vz, my * vz
    return (
        [mx, mx * vx + pressure, xy, xz, total * vx],
        [my, xy, my * vy + pressure, yz, total * vy],
        [mz, xz, yz, mz * vz + pressure, total * vz],
    )


def halves(value):
    high = value.astype(BF16).astype(F32)
    return high, value - high


def kernel(
    zh_count, x_count, gy_count, gz_count,
    rho_hbm, mom_hbm, energy_hbm, sound_hbm, slot_ref, element_ref,
    dxh_hbm, dxl_hbm, dyh_hbm, dyl_hbm, dzh_hbm, dzl_hbm, order_hbm,
    rho_out, mom_out, energy_out, sound_out,
    s0, s1, s2, vel, vort, mref, fref, tiles, parcel, arrived, full,
    hx, hy, hz, sy, sz, ax, ay, az, axs, ays, azs,
    stage, q0, q1, n0, chars, near,
    dxh, dxl, dyh, dyl, dzh, dzl, order,
    in_sem, out_sem, flow_send, flow_recv, face_send, face_recv, tile_send, tile_recv,
):
    gx, gy, gz = lax.axis_index("gx"), lax.axis_index("gy"), lax.axis_index("gz")
    gx_count = zh_count * x_count
    zh, xi = gx // x_count, lax.rem(gx, x_count)

    def at_x(step):
        return (lax.rem(gx + step + gx_count, gx_count), gy, gz)

    def at_y(step):
        return (gx, lax.rem(gy + step + gy_count, gy_count), gz)

    def at_z(step):
        return (gx, gy, lax.rem(gz + step + gz_count, gz_count))

    def at_zh(step):
        return (lax.rem(zh + step, zh_count) * x_count + xi, gy, gz)

    def at_xi(step):
        return (zh * x_count + lax.rem(xi + step, x_count), gy, gz)

    barrier = pltpu.get_barrier_semaphore()
    partners = [at_x(-1), at_x(1), at_y(-1), at_y(1), at_z(-1), at_z(1)]
    partners += [at_zh(k) for k in range(1, zh_count)] + [at_xi(j) for j in range(1, x_count)]
    for partner in partners:
        pl.semaphore_signal(barrier, inc=1, device_id=partner, device_id_type=MESH)

    loads = [
        (rho_hbm, s0.at[0]), (mom_hbm, s0.at[1:4]), (energy_hbm, s0.at[4]), (sound_hbm, stage),
        (order_hbm, order), (dxh_hbm, dxh), (dxl_hbm, dxl), (dyh_hbm, dyh), (dyl_hbm, dyl),
        (dzh_hbm, dzh), (dzl_hbm, dzl),
    ]
    loads = [pltpu.make_async_copy(a, b, in_sem.at[i]) for i, (a, b) in enumerate(loads)]
    for load in loads:
        load.start()

    lane = iota((16, 128), 1)
    row = iota((16, 128), 0)
    odd = lax.rem(lane, 2) == 1
    edge = (lane == 0) | (lane == 127)
    pair = lane // 2

    pending = []

    def send(src, dst, send_sem, recv_sem, device):
        copy = pltpu.make_async_remote_copy(
            src_ref=src, dst_ref=dst, send_sem=send_sem, recv_sem=recv_sem,
            device_id=device, device_id_type=MESH,
        )
        copy.start()
        pending.append(copy)
        return copy

    def flow_go(turn, i, src, dst, device):
        return send(src, dst, flow_send.at[turn, i], flow_recv.at[turn, i], device)

    def sends_x(turn, x_source, comps):
        return [
            flow_go(turn, 0, x_source(240), hx.at[turn, 0, comps], at_x(1)),
            flow_go(turn, 1, x_source(0), hx.at[turn, 1, comps], at_x(-1)),
        ]

    def sends_yz(turn, comps):
        return [
            flow_go(turn, 2, sz.at[turn, comps], hz.at[turn, 0, comps], at_z(1)),
            flow_go(turn, 3, sz.at[turn, comps], hz.at[turn, 1, comps], at_z(-1)),
            flow_go(turn, 4, sy.at[turn, 0, comps], hy.at[turn, 0, comps], at_y(1)),
            flow_go(turn, 5, sy.at[turn, 1, comps], hy.at[turn, 1, comps], at_y(-1)),
        ]

    def slab(x):
        return pl.ds(pl.multiple_of(x * 16, 16), 16)

    def pack_lanes(packed, values, x):
        here = pair == x
        return [jnp.where(here, pltpu.roll(v, 2 * x + 1, 1), p) for p, v in zip(packed, values)]

    def pack_rows(turn, ref, comps):
        for c in comps:
            sy[turn, 0, c] = ref[c, pl.ds(15, 16, stride=16), :]
            sy[turn, 1, c] = ref[c, pl.ds(0, 16, stride=16), :]

    for load in loads[:3]:
        load.wait()
    pack_rows(0, s0, range(5))

    def pack_first(x, packed):
        return pack_lanes(packed, [s0[c, slab(x), :] for c in range(5)], x)

    first_slab = [s0[c, 0:16, :] for c in range(5)]
    for c, value in enumerate(lax.fori_loop(0, 16, pack_first, first_slab)):
        sz[0, c] = value
    pl.semaphore_wait(barrier, len(partners))
    every = pl.ds(0, 5)
    round_x = sends_x(0, lambda r: s0.at[:, r : r + 16, :], every)
    round_yz = sends_yz(0, every)

    def face_sends(turn, q):
        for d in range(3):
            for j in range(4):
                block = slice(128 * j, 128 * j + 128)
                chars[0, d, j] = q[0, :, block] - q[1 + d, :, block]
                chars[1, d, j] = q[0, :, block] + q[1 + d, :, block]
        axs[turn, 0] = chars[0, 0, 0, 0:16, :]
        axs[turn, 1] = chars[1, 0, 3, 16:32, :]
        for side, top in ((0, 0), (1, 12)):
            for j in range(4):
                block = slice(128 * j, 128 * j + 128)
                ays[turn, side, 0:4, block] = chars[side, 1, j, top : top + 4, :]
                ays[turn, side, 4:8, block] = chars[side, 1, j, top + 16 : top + 20, :]
                azs[turn, side, :, block] = chars[side, 2, j, pl.ds(3 * side, 8, stride=4), :]

        def go(i, src, dst, device):
            return send(src, dst, face_send.at[turn, i], face_recv.at[turn, i], device)

        return [
            go(0, axs.at[turn, 0], ax.at[turn, 0], at_x(-1)),
            go(1, axs.at[turn, 1], ax.at[turn, 1], at_x(1)),
            go(2, ays.at[turn, 0], ay.at[turn, 0], at_y(-1)),
            go(3, ays.at[turn, 1], ay.at[turn, 1], at_y(1)),
            go(4, azs.at[turn, 0], az.at[turn, 0], at_z(-1)),
            go(5, azs.at[turn, 1], az.at[turn, 1], at_z(1)),
        ]

    def apply3(value, high, low):
        rows = value.shape[0]
        top, rest = halves(value)
        both = jnp.concatenate([top, rest], axis=0).astype(BF16)
        part = jnp.dot(both, high, preferred_element_type=F32)
        return (
            part[:rows] + part[rows:]
            + jnp.dot(top.astype(BF16), low, preferred_element_type=F32)
        )

    def derivative(d, value):
        if d == 0:
            return apply3(value, dxh[...], dxl[...])
        high, low = (dyh, dyl) if d == 1 else (dzh, dzl)
        split = [apply3(value[:, s : s + 256], high[...], low[...]) for s in (0, 256)]
        return jnp.concatenate(split, axis=1)

    lane32 = iota((32, 128), 1)

    def rates(q, out, gain, base, copies, turn, with_pressure):
        total = None
        for d in range(3):
            if with_pressure:
                both = derivative(d, jnp.concatenate([q[0], q[1 + d]], axis=0))
                out[1 + d] = base(1 + d) - gain * both[:32]
                both = both[32:]
            else:
                both = derivative(d, q[1 + d])
                out[1 + d] = base(1 + d)
            total = both if total is None else total + both
        out[0] = base(0) - gain * total
        for side, d, move in ((0, 1, 28), (1, 1, 4), (0, 2, 31), (1, 2, 1)):
            for j in range(4):
                near[side, d - 1, j] = pltpu.roll(chars[side, d, j], move, 0)
        for copy in copies[2:6]:
            copy.wait_recv()
        for side, top in ((0, 12), (1, 0)):
            for j in range(4):
                block = slice(128 * j, 128 * j + 128)
                near[side, 0, j, top : top + 4, :] = ay[turn, side, 0:4, block]
                near[side, 0, j, top + 16 : top + 20, :] = ay[turn, side, 4:8, block]
                near[side, 1, j, pl.ds(3 - 3 * side, 8, stride=4), :] = az[turn, side, :, block]
        k = 0.5 * lift_factor * gain
        for d, period, move in ((1, 64, 56), (2, 8, 7)):
            place = lax.rem(lane32, period)
            span = period - move
            for j in range(4):
                block = slice(128 * j, 128 * j + 128)
                high = pltpu.roll(near[0, d - 1, j], move, 1) - chars[0, d, j]
                high = jnp.where(place >= move, k * high, 0.0)
                low = chars[1, d, j] - pltpu.roll(near[1, d - 1, j], 128 - move, 1)
                low = jnp.where(place < span, k * low, 0.0)
                out[0, :, block] += high - low
                out[1 + d, :, block] -= high + low
        for copy in copies[0:2]:
            copy.wait_recv()
        other = jnp.concatenate([chars[0, 0, 0, 16:32, :], ax[turn, 0]], axis=0)
        jump = pltpu.roll(other, 64, 1) - chars[0, 0, 3]
        jump = jnp.where(lane32 >= 64, k * jump, 0.0)
        out[0, :, 384:512] += jump
        out[1, :, 384:512] -= jump
        other = jnp.concatenate([ax[turn, 1], chars[1, 0, 3, 0:16, :]], axis=0)
        jump = chars[1, 0, 0] - pltpu.roll(other, 64, 1)
        jump = jnp.where(lane32 < 64, k * jump, 0.0)
        out[0, :, 0:128] -= jump
        out[1, :, 0:128] -= jump

    loads[3].wait()
    for i in range(32):
        c, part = i // 8, i % 8
        q0[c, 4 * part : 4 * part + 4, :] = stage[i]
    faces_0 = face_sends(0, q0)

    def interior(source, target, gain, base):
        half, visc = 0.5 * gain, viscosity * gain

        def update(x, before, first):
            state = [source[c, slab(x), :] for c in range(5)]
            along_x, along_y, along_z = fluxes(state)
            sums, later = [], []
            for c in range(5):
                soft = visc * state[c]
                acc = base(c, x, state[c]) - 6.0 * soft
                part = half * along_z[c]
                acc += pltpu.roll(jnp.where(lane == 0, 0.0, soft - part), 127, 1)
                acc += pltpu.roll(jnp.where(lane == 127, 0.0, soft + part), 1, 1)
                part = half * along_y[c]
                acc += pltpu.roll(jnp.where(row == 0, 0.0, soft - part), 15, 0)
                acc += pltpu.roll(jnp.where(row == 15, 0.0, soft + part), 1, 0)
                part = half * along_x[c]
                if not first:
                    target[c, slab(x - 1), :] = before[c] + (soft - part)
                    acc += before[5 + c]
                sums.append(acc)
                later.append(soft + part)
            return sums + later

        carry = update(0, None, True)
        carry = lax.fori_loop(1, 16, lambda x, b: update(x, b, False), carry)
        for c in range(5):
            target[c, 240:256, :] = carry[c]

    def boundary_yz(turn, target, gain, copies):
        half, visc = 0.5 * gain, viscosity * gain
        for copy in copies:
            copy.wait_recv()
        lower, upper = [hy[turn, 0, c] for c in range(5)], [hy[turn, 1, c] for c in range(5)]
        low_flux, up_flux = fluxes(lower)[1], fluxes(upper)[1]
        for c in range(5):
            target[c, pl.ds(0, 16, stride=16), :] += visc * lower[c] + half * low_flux[c]
            target[c, pl.ds(15, 16, stride=16), :] += visc * upper[c] - half * up_flux[c]
        both = [
            jnp.where(odd, pltpu.roll(hz[turn, 0, c], 1, 1), pltpu.roll(hz[turn, 1, c], 127, 1))
            for c in range(5)
        ]
        flux = fluxes(both)[2]
        return [
            visc * both[c] + jnp.where(odd, half * flux[c], -half * flux[c]) for c in range(5)
        ]

    def boundary_x(turn, target, gain, copies):
        half, visc = 0.5 * gain, viscosity * gain
        outer = []
        for side, rows, copy in ((0, slice(0, 16), copies[0]), (1, slice(240, 256), copies[1])):
            copy.wait_recv()
            state = [hx[turn, side, c] for c in range(5)]
            flux = fluxes(state)[0]
            values = []
            for c in range(5):
                term = half * flux[c] if side == 0 else -half * flux[c]
                value = target[c, rows, :] + (visc * state[c] + term)
                target[c, rows, :] = value
                values.append(value)
            outer.append(values)
        return outer

    def add_edges(target, terms, x):
        values = []
        for c in range(5):
            moved = pltpu.roll(terms[c], 127 - 2 * x, 1)
            value = target[c, slab(x), :] + jnp.where(edge, moved, 0.0)
            target[c, slab(x), :] = value
            values.append(value)
        return values

    interior(s0, s1, flow_step, lambda c, x, u: u)
    terms = boundary_yz(0, s1, flow_step, round_yz)
    packed = [s1[c, 16:32, :] for c in range(5)]
    packed = lax.fori_loop(1, 15, lambda x, p: pack_lanes(p, add_edges(s1, terms, x), x), packed)
    for x in (0, 15):
        add_edges(s1, terms, x)
    outer = boundary_x(0, s1, flow_step, round_x)
    round_x = sends_x(1, lambda r: s1.at[:, r : r + 16, :], every)
    packed = pack_lanes(pack_lanes(packed, outer[0], 0), outer[1], 15)
    for c in range(5):
        sz[1, c] = packed[c]
    pack_rows(1, s1, range(5))
    round_yz = sends_yz(1, every)

    interior(s1, s2, 0.5 * flow_step, lambda c, x, u: 0.5 * (s0[c, slab(x), :] + u))
    terms_2 = boundary_yz(1, s2, 0.5 * flow_step, round_yz)

    def velocity(x, values):
        inverse = 1.0 / values[0]
        vx, vy, vz = (values[d] * inverse for d in (1, 2, 3))
        vel[0, slab(x), :], vel[1, slab(x), :], vel[2, slab(x), :] = vy, vz, vx
        return [vy, vx]

    zero = jnp.zeros((16, 128), F32)
    packed = lax.fori_loop(
        1, 15, lambda x, p: pack_lanes(p, velocity(x, add_edges(s2, terms_2, x)), x), [zero, zero]
    )
    for x in (0, 15):
        add_edges(s2, terms_2, x)
    outer = boundary_x(1, s2, 0.5 * flow_step, round_x)
    outer = [velocity(0, outer[0]), velocity(15, outer[1])]
    round_x = sends_x(2, lambda r: vel.at[0:2, r : r + 16, :], pl.ds(0, 2))
    sz[2, 0], sz[2, 1] = pack_lanes(pack_lanes(packed, outer[0], 0), outer[1], 15)
    for i, comp in enumerate((1, 2)):
        sy[2, 0, i] = vel[comp, pl.ds(15, 16, stride=16), :]
        sy[2, 1, i] = vel[comp, pl.ds(0, 16, stride=16), :]
    round_yz = sends_yz(2, pl.ds(0, 2))

    stores = [
        pltpu.make_async_copy(s2.at[0], rho_out, out_sem.at[0]),
        pltpu.make_async_copy(s2.at[1:4], mom_out, out_sem.at[1]),
        pltpu.make_async_copy(s2.at[4], energy_out, out_sem.at[2]),
    ]
    for store in stores:
        store.start()

    def dy(f):
        up = pltpu.roll(jnp.where(row == 0, 0.0, f), 15, 0)
        return up - pltpu.roll(jnp.where(row == 15, 0.0, f), 1, 0)

    def dz(f):
        up = pltpu.roll(jnp.where(lane == 0, 0.0, f), 127, 1)
        return up - pltpu.roll(jnp.where(lane == 127, 0.0, f), 1, 1)

    def curl(x, carry):
        vy, vz, vx = (vel[i, slab(x), :] for i in range(3))
        after = slab(jnp.minimum(x + 1, 15))
        before = slab(jnp.maximum(x - 1, 0))
        dx_vy, dx_vz = (
            jnp.where(x < 15, vel[i, after, :], 0.0) - jnp.where(x > 0, vel[i, before, :], 0.0)
            for i in range(2)
        )
        vort[0, slab(x), :] = dy(vz) - dz(vy)
        vort[1, slab(x), :] = dz(vx) - dx_vz
        vort[2, slab(x), :] = dx_vy - dy(vx)
        return carry

    lax.fori_loop(0, 16, curl, 0)
    for copy in round_yz:
        copy.wait_recv()
    vort[0, pl.ds(0, 16, stride=16), :] -= hy[2, 0, 0]
    vort[2, pl.ds(0, 16, stride=16), :] += hy[2, 0, 1]
    vort[0, pl.ds(15, 16, stride=16), :] += hy[2, 1, 0]
    vort[2, pl.ds(15, 16, stride=16), :] -= hy[2, 1, 1]
    side_y, side_x = (
        jnp.where(odd, pltpu.roll(hz[2, 0, i], 1, 1), pltpu.roll(hz[2, 1, i], 127, 1))
        for i in range(2)
    )
    side_y = jnp.where(odd, side_y, -side_y)
    side_x = jnp.where(odd, -side_x, side_x)

    def lamb_pair(a, carry):
        sums = [None] * 3
        for x in (2 * a, 2 * a + 1):
            wx = vort[0, slab(x), :] + jnp.where(edge, pltpu.roll(side_y, 127 - 2 * x, 1), 0.0)
            wy = vort[1, slab(x), :] + jnp.where(edge, pltpu.roll(side_x, 127 - 2 * x, 1), 0.0)
            wz = vort[2, slab(x), :]
            vy, vz, vx = (vel[i, slab(x), :] for i in range(3))
            parts = (wy * vz - wz * vy, wz * vx - wx * vz, wx * vy - wy * vx)
            sums = [p if s is None else s + p for s, p in zip(sums, parts)]
        for d in range(3):
            mref[d, slab(a), :] = 0.0625 * sums[d]
        return carry

    lax.fori_loop(1, 7, lamb_pair, 0)
    round_x[0].wait_recv()
    vort[1, 0:16, :] += hx[2, 0, 1]
    vort[2, 0:16, :] -= hx[2, 0, 0]
    lamb_pair(0, 0)
    round_x[1].wait_recv()
    vort[1, 240:256, :] -= hx[2, 1, 1]
    vort[2, 240:256, :] += hx[2, 1, 0]
    lamb_pair(7, 0)
    coarse = [
        mref[d, pl.ds(0, 64, stride=2), :] + mref[d, pl.ds(1, 64, stride=2), :] for d in range(3)
    ]
    fref[0] = jnp.transpose(jnp.concatenate([coarse[0], coarse[1]], axis=0))
    fref[1] = jnp.transpose(jnp.concatenate([coarse[2], coarse[2]], axis=0))
    pieces = [
        [
            fref[i, pl.ds(2 * c, 8, stride=16), :] + fref[i, pl.ds(2 * c + 1, 8, stride=16), :]
            for c in range(8)
        ]
        for i in range(2)
    ]
    left = iota((8, 128), 1) < 64
    rows = [[], [], []]
    for j in range(4):
        a, b = pieces[0][2 * j], pieces[0][2 * j + 1]
        rows[0].append(jnp.where(left, a, pltpu.roll(b, 64, 1)))
        rows[1].append(jnp.where(left, pltpu.roll(a, 64, 1), b))
        rows[2].append(jnp.where(left, pieces[1][2 * j], pieces[1][2 * j + 1]))
    own = jnp.concatenate([jnp.concatenate(r, axis=1) for r in rows], axis=0)
    high, rest = halves(own)
    middle, low = halves(rest)
    loads[4].wait()
    parts = jnp.concatenate([high, middle, low], axis=0).astype(BF16)
    parts = jnp.dot(parts, order[...], preferred_element_type=F32)
    own = parts[0:24] + parts[24:48] + parts[48:72]
    for d in range(3):
        tiles[0, :, 512 * d : 512 * d + 512] = own[8 * d : 8 * d + 8]
    row8, lane8 = iota((8, 128), 0), iota((8, 128), 1)
    label = jnp.full((8, 128), -1, jnp.int32)
    for t in range(8):
        label = jnp.where((lane8 < 24) & (lax.rem(lane8, 8) == t), slot_ref[0, 0, 0, t], label)
        label = jnp.where((lane8 >= 64) & (row8 == t), element_ref[0, 0, 0, t], label)
    tiles[0, :, 1536:1664] = label.astype(F32)

    down = [
        send(tiles.at[0], tiles.at[k], tile_send.at[k - 1], tile_recv.at[k - 1], at_zh(k))
        for k in range(1, zh_count)
    ]
    across = []
    slots = 4 * x_count
    place = iota((slots, 24), 0)
    wanted = zh * slots + lax.rem(xi + place // 4, x_count) * 4 + lax.rem(place, 4)
    wanted = wanted.astype(F32)

    def pass_on(k):
        listed = jnp.broadcast_to(tiles[k, 0:1, 1536:1560], (slots, 24))
        choice = jnp.where(listed == wanted, 1.0, 0.0).astype(BF16)
        for first in range(0, TILE_LANES, 512):
            block = slice(first, min(first + 512, TILE_LANES))
            high, rest = halves(tiles[k, :, block])
            middle, low = halves(rest)
            parts = jnp.concatenate([high, middle, low], axis=0).astype(BF16)
            chosen = jnp.dot(choice, parts, preferred_element_type=F32)
            full[k * slots : k * slots + 4, block] = chosen[0:4]
            for j in range(1, x_count):
                parcel[k, j - 1, :, block] = chosen[4 * j : 4 * j + 4]
        for j in range(1, x_count):
            i = zh_count - 1 + k * (x_count - 1) + j - 1
            across.append(
                send(
                    parcel.at[k, j - 1], arrived.at[k, j - 1], tile_send.at[i], tile_recv.at[i],
                    at_xi(j),
                )
            )

    pass_on(0)

    for load in loads[5:]:
        load.wait()
    rates(q0, q1, sound_step, lambda c: q0[c], faces_0, 0, True)
    faces_1 = face_sends(1, q1)
    for k in sorted(range(1, zh_count), key=lambda k: min(k, zh_count - k)):
        down[k - 1].wait_recv()
        pass_on(k)
    rates(q1, n0, 0.5 * sound_step, lambda c: 0.5 * (q0[c] + q1[c]), faces_1, 1, True)

    for i, copy in enumerate(across):
        copy.wait_recv()
    for k in range(zh_count):
        for j in range(1, x_count):
            top = k * slots + 4 * j
            full[top : top + 4, :] = arrived[k, j - 1]
    count = zh_count * slots
    element = (iota((count, 128), 1) - 64).astype(F32)
    picking = jnp.where(full[:, 1536:1664] == element, 1.0, 0.0)
    picking = jnp.concatenate([picking, picking], axis=0)
    picking = jnp.transpose(picking)[64:96].astype(BF16)
    for d in range(3):
        high, low = halves(full[:, 512 * d : 512 * d + 512])
        parts = jnp.concatenate([high, low], axis=0).astype(BF16)
        both = jnp.dot(picking, parts, preferred_element_type=F32)
        q1[1 + d] = -source_gain * sound_step * both
    q1[0] = jnp.zeros((32, 512), F32)
    faces_2 = face_sends(2, q1)
    rates(q1, q0, 0.5 * sound_step, lambda c: n0[c] + q1[c], faces_2, 2, False)
    for i in range(32):
        c, part = i // 8, i % 8
        stage[i] = q0[c, 4 * part : 4 * part + 4, :]
    stores.append(pltpu.make_async_copy(stage, sound_out, out_sem.at[3]))
    stores[-1].start()
    for copy in pending:
        copy.wait_send()
    for store in stores:
        store.wait()


def hand_over(*refs):
    sources, targets, held, sem = refs[0:4], refs[4:8], refs[8:12], refs[12]
    loads = [pltpu.make_async_copy(sources[i], held[i], sem.at[0, i]) for i in range(4)]
    stores = [pltpu.make_async_copy(held[i], targets[i], sem.at[1, i]) for i in range(4)]
    for load in loads:
        load.start()
    for load, store in zip(loads, stores):
        load.wait()
        store.start()
    for store in stores:
        store.wait()


def solution(mesh):
    gx_count, gy_count, gz_count = (mesh.shape[a] for a in ("gx", "gy", "gz"))
    x_count = 4 if gx_count == 16 else 2
    zh_count = gx_count // x_count
    tile_sends = (zh_count - 1) + zh_count * (x_count - 1)
    consts = tables()

    def on_device(density, momentum, energy, acoustic, tile_slot, tile_element):
        anywhere = pl.BlockSpec(memory_space=pl.ANY)
        scalars = pl.BlockSpec(memory_space=pltpu.SMEM)
        out_shape = (
            jax.ShapeDtypeStruct((256, 128), F32),
            jax.ShapeDtypeStruct((3, 256, 128), F32),
            jax.ShapeDtypeStruct((256, 128), F32),
            jax.ShapeDtypeStruct((32, 4, 512), F32),
        )
        vmem = pltpu.VMEM
        scratch = [
            vmem((5, 256, 128), F32), vmem((5, 256, 128), F32), vmem((5, 256, 128), F32),
            vmem((3, 256, 128), F32), vmem((3, 256, 128), F32), vmem((3, 128, 128), F32),
            vmem((2, 128, 128), F32), vmem((zh_count, 8, TILE_LANES), F32),
            vmem((zh_count, x_count - 1, 4, TILE_LANES), F32),
            vmem((zh_count, x_count - 1, 4, TILE_LANES), F32),
            vmem((4 * gx_count, TILE_LANES), F32),
            vmem((3, 2, 5, 16, 128), F32), vmem((3, 2, 5, 16, 128), F32),
            vmem((3, 2, 5, 16, 128), F32), vmem((3, 2, 5, 16, 128), F32),
            vmem((3, 5, 16, 128), F32),
            vmem((3, 2, 16, 128), F32), vmem((3, 2, 8, 512), F32), vmem((3, 2, 8, 512), F32),
            vmem((3, 2, 16, 128), F32), vmem((3, 2, 8, 512), F32), vmem((3, 2, 8, 512), F32),
            vmem((32, 4, 512), F32), vmem((4, 32, 512), F32), vmem((4, 32, 512), F32),
            vmem((4, 32, 512), F32), vmem((2, 3, 4, 32, 128), F32), vmem((2, 2, 4, 32, 128), F32),
            vmem((512, 512), BF16), vmem((512, 512), BF16), vmem((256, 256), BF16),
            vmem((256, 256), BF16), vmem((256, 256), BF16), vmem((256, 256), BF16),
            vmem((512, 512), BF16),
            pltpu.SemaphoreType.DMA((11,)), pltpu.SemaphoreType.DMA((4,)),
            pltpu.SemaphoreType.DMA((3, 6)), pltpu.SemaphoreType.DMA((3, 6)),
            pltpu.SemaphoreType.DMA((3, 6)), pltpu.SemaphoreType.DMA((3, 6)),
            pltpu.SemaphoreType.DMA((tile_sends,)), pltpu.SemaphoreType.DMA((tile_sends,)),
        ]
        outs = pl.pallas_call(
            functools.partial(kernel, zh_count, x_count, gy_count, gz_count),
            out_shape=out_shape,
            in_specs=[anywhere] * 4 + [scalars] * 2 + [anywhere] * 7,
            out_specs=[anywhere] * 4,
            scratch_shapes=scratch,
            compiler_params=pltpu.CompilerParams(
                collective_id=0, has_side_effects=True, vmem_limit_bytes=60 * 2**20
            ),
            cost_estimate=pl.CostEstimate(
                flops=10**9, bytes_accessed=4 * 2**20, transcendentals=0
            ),
        )(
            density.reshape(256, 128), momentum.reshape(3, 256, 128), energy.reshape(256, 128),
            acoustic.reshape(32, 4, 512), tile_slot, tile_element,
            *[jnp.asarray(c) for c in consts],
        )
        outs = pl.pallas_call(
            hand_over,
            out_shape=out_shape,
            in_specs=[anywhere] * 4,
            out_specs=[anywhere] * 4,
            scratch_shapes=[vmem(o.shape, F32) for o in out_shape]
            + [pltpu.SemaphoreType.DMA((2, 4))],
            compiler_params=pltpu.CompilerParams(vmem_limit_bytes=60 * 2**20),
        )(*outs)
        return (
            outs[0].reshape(16, 16, 128), outs[1].reshape(3, 16, 16, 128),
            outs[2].reshape(16, 16, 128), outs[3].reshape(4, 2, 4, 4, 512),
        )

    in_specs = (
        P("gx", "gy", "gz"), P(None, "gx", "gy", "gz"), P("gx", "gy", "gz"),
        P(None, "gx", "gy", "gz", None), P("gx", "gy", "gz", None), P("gx", "gy", "gz", None),
    )
    out_specs = (
        P("gx", "gy", "gz"), P(None, "gx", "gy", "gz"), P("gx", "gy", "gz"),
        P(None, "gx", "gy", "gz", None),
    )
    return jax.shard_map(
        on_device, mesh=mesh, in_specs=in_specs, out_specs=out_specs, check_vma=False
    )
```

```python
import functools

import jax
import jax.numpy as jnp
import ml_dtypes
import numpy as np
from jax import lax
from jax.experimental import pallas as pl
from jax.experimental.pallas import tpu as pltpu
from jax.sharding import PartitionSpec as P

MESH = pl.DeviceIdType.MESH
F32 = jnp.float32
BF16 = jnp.bfloat16

flow_step = 0.05
viscosity = 0.2
sound_step = 0.02
lift_factor = 28.0
source_gain = 40.0
TILE_LANES = 1664
PARCEL_LANES = 1920


def derivative_numbers():
    order = 7
    points = np.array(
        [
            -1.0,
            -0.8717401485096066,
            -0.5917001814331423,
            -0.2092992179024789,
            0.2092992179024789,
            0.5917001814331423,
            0.8717401485096066,
            1.0,
        ]
    )
    previous = np.ones(8)
    current = points * 1.0
    for degree in range(1, order):
        following = ((2 * degree + 1) * points * current - degree * previous) / (degree + 1)
        previous = current
        current = following
    table = np.zeros((8, 8))
    for row in range(8):
        for column in range(8):
            if row != column:
                table[row, column] = current[row] / (
                    current[column] * (points[row] - points[column])
                )
    table[0, 0] = -order * (order + 1) / 4.0
    table[order, order] = order * (order + 1) / 4.0
    return table


def split_table(table):
    table = table.astype(np.float32)
    high = table.astype(ml_dtypes.bfloat16)
    low = (table - high.astype(np.float32)).astype(ml_dtypes.bfloat16)
    return high, low


def tables():
    table = derivative_numbers()
    eye = np.eye(8)
    along_x = np.kron(np.kron(table, eye), eye).T
    along_y = np.kron(np.kron(np.eye(4), table), eye).T
    along_z = np.kron(np.kron(np.eye(4), eye), table).T
    order = np.zeros((512, 512), ml_dtypes.bfloat16)
    for c in range(8):
        for ab in range(64):
            order[c * 64 + ab, ab * 8 + c] = 1.0
    return (*split_table(along_x), *split_table(along_y), *split_table(along_z), order)


def iota(shape, dim):
    return lax.broadcasted_iota(jnp.int32, shape, dim)


def fluxes(state):
    rho, mx, my, mz, energy = state
    inverse = 1.0 / rho
    vx, vy, vz = mx * inverse, my * inverse, mz * inverse
    pressure = 0.4 * (energy - 0.5 * (mx * vx + my * vy + mz * vz))
    total = energy + pressure
    xy, xz, yz = mx * vy, mx * vz, my * vz
    return (
        [mx, mx * vx + pressure, xy, xz, total * vx],
        [my, xy, my * vy + pressure, yz, total * vy],
        [mz, xz, yz, mz * vz + pressure, total * vz],
    )


def halves(value):
    high = value.astype(BF16).astype(F32)
    return high, value - high


def kernel(
    zh_count, x_count, gy_count, gz_count,
    rho_hbm, mom_hbm, energy_hbm, sound_hbm, slot_ref, element_ref,
    dxh_hbm, dxl_hbm, dyh_hbm, dyl_hbm, dzh_hbm, dzl_hbm, order_hbm,
    rho_out, mom_out, energy_out, sound_out,
    s0, s1, s2, vel, vort, mref, fref, tiles, parcel, arrived, full,
    hx, hy, hz, sy, sz, ax, ay, az, axs, ays, azs,
    stage, q0, q1, n0, chars, near,
    dxh, dxl, dyh, dyl, dzh, dzl, order,
    in_sem, out_sem, flow_send, flow_recv, face_send, face_recv, tile_send, tile_recv,
):
    gx, gy, gz = lax.axis_index("gx"), lax.axis_index("gy"), lax.axis_index("gz")
    gx_count = zh_count * x_count
    zh, xi = gx // x_count, lax.rem(gx, x_count)

    def at_x(step):
        return (lax.rem(gx + step + gx_count, gx_count), gy, gz)

    def at_y(step):
        return (gx, lax.rem(gy + step + gy_count, gy_count), gz)

    def at_z(step):
        return (gx, gy, lax.rem(gz + step + gz_count, gz_count))

    def at_zh(step):
        return (lax.rem(zh + step, zh_count) * x_count + xi, gy, gz)

    def at_xi(step):
        return (zh * x_count + lax.rem(xi + step, x_count), gy, gz)

    barrier = pltpu.get_barrier_semaphore()
    partners = [at_x(-1), at_x(1), at_y(-1), at_y(1), at_z(-1), at_z(1)]
    partners += [at_zh(k) for k in range(1, zh_count)] + [at_xi(j) for j in range(1, x_count)]
    for partner in partners:
        pl.semaphore_signal(barrier, inc=1, device_id=partner, device_id_type=MESH)

    loads = [
        (rho_hbm, s0.at[0]), (mom_hbm, s0.at[1:4]), (energy_hbm, s0.at[4]), (sound_hbm, stage),
        (order_hbm, order), (dxh_hbm, dxh), (dxl_hbm, dxl), (dyh_hbm, dyh), (dyl_hbm, dyl),
        (dzh_hbm, dzh), (dzl_hbm, dzl),
    ]
    loads = [pltpu.make_async_copy(a, b, in_sem.at[i]) for i, (a, b) in enumerate(loads)]
    for load in loads:
        load.start()

    lane = iota((16, 128), 1)
    row = iota((16, 128), 0)
    odd = lax.rem(lane, 2) == 1
    edge = (lane == 0) | (lane == 127)
    pair = lane // 2

    pending = []

    def send(src, dst, send_sem, recv_sem, device):
        copy = pltpu.make_async_remote_copy(
            src_ref=src, dst_ref=dst, send_sem=send_sem, recv_sem=recv_sem,
            device_id=device, device_id_type=MESH,
        )
        copy.start()
        pending.append(copy)
        return copy

    def flow_go(turn, i, src, dst, device):
        return send(src, dst, flow_send.at[turn, i], flow_recv.at[turn, i], device)

    def sends_x(turn, x_source, comps):
        return [
            flow_go(turn, 0, x_source(240), hx.at[turn, 0, comps], at_x(1)),
            flow_go(turn, 1, x_source(0), hx.at[turn, 1, comps], at_x(-1)),
        ]

    def sends_yz(turn, comps):
        return [
            flow_go(turn, 2, sz.at[turn, comps], hz.at[turn, 0, comps], at_z(1)),
            flow_go(turn, 3, sz.at[turn, comps], hz.at[turn, 1, comps], at_z(-1)),
            flow_go(turn, 4, sy.at[turn, 0, comps], hy.at[turn, 0, comps], at_y(1)),
            flow_go(turn, 5, sy.at[turn, 1, comps], hy.at[turn, 1, comps], at_y(-1)),
        ]

    def slab(x):
        return pl.ds(pl.multiple_of(x * 16, 16), 16)

    def pack_lanes(packed, values, x):
        here = pair == x
        return [jnp.where(here, pltpu.roll(v, 2 * x + 1, 1), p) for p, v in zip(packed, values)]

    def pack_rows(turn, ref, comps):
        for c in comps:
            sy[turn, 0, c] = ref[c, pl.ds(15, 16, stride=16), :]
            sy[turn, 1, c] = ref[c, pl.ds(0, 16, stride=16), :]

    for load in loads[:3]:
        load.wait()
    pack_rows(0, s0, range(5))

    def pack_first(x, packed):
        return pack_lanes(packed, [s0[c, slab(x), :] for c in range(5)], x)

    first_slab = [s0[c, 0:16, :] for c in range(5)]
    for c, value in enumerate(lax.fori_loop(0, 16, pack_first, first_slab)):
        sz[0, c] = value
    pl.semaphore_wait(barrier, len(partners))
    every = pl.ds(0, 5)
    round_x = sends_x(0, lambda r: s0.at[:, r : r + 16, :], every)
    round_yz = sends_yz(0, every)

    def face_sends(turn, q):
        for d in range(3):
            for j in range(4):
                block = slice(128 * j, 128 * j + 128)
                chars[0, d, j] = q[0, :, block] - q[1 + d, :, block]
                chars[1, d, j] = q[0, :, block] + q[1 + d, :, block]
        axs[turn, 0] = chars[0, 0, 0, 0:16, :]
        axs[turn, 1] = chars[1, 0, 3, 16:32, :]
        for side, top in ((0, 0), (1, 12)):
            for j in range(4):
                block = slice(128 * j, 128 * j + 128)
                ays[turn, side, 0:4, block] = chars[side, 1, j, top : top + 4, :]
                ays[turn, side, 4:8, block] = chars[side, 1, j, top + 16 : top + 20, :]
                azs[turn, side, :, block] = chars[side, 2, j, pl.ds(3 * side, 8, stride=4), :]

        def go(i, src, dst, device):
            return send(src, dst, face_send.at[turn, i], face_recv.at[turn, i], device)

        along_x = [
            go(0, axs.at[turn, 0], ax.at[turn, 0], at_x(-1)),
            go(1, axs.at[turn, 1], ax.at[turn, 1], at_x(1)),
        ]
        return along_x + [
            go(2, ays.at[turn, 0], ay.at[turn, 0], at_y(-1)),
            go(3, ays.at[turn, 1], ay.at[turn, 1], at_y(1)),
            go(4, azs.at[turn, 0], az.at[turn, 0], at_z(-1)),
            go(5, azs.at[turn, 1], az.at[turn, 1], at_z(1)),
        ]

    def apply3(value, high, low):
        rows = value.shape[0]
        top, rest = halves(value)
        both = jnp.concatenate([top, rest], axis=0).astype(BF16)
        part = jnp.dot(both, high, preferred_element_type=F32)
        return (
            part[:rows] + part[rows:]
            + jnp.dot(top.astype(BF16), low, preferred_element_type=F32)
        )

    def derivative(d, value):
        if d == 0:
            return apply3(value, dxh[...], dxl[...])
        high, low = (dyh, dyl) if d == 1 else (dzh, dzl)
        split = [apply3(value[:, s : s + 256], high[...], low[...]) for s in (0, 256)]
        return jnp.concatenate(split, axis=1)

    lane32 = iota((32, 128), 1)

    def rates(q, out, gain, base, copies, turn, with_pressure):
        total = None
        for d in range(3):
            if with_pressure:
                both = derivative(d, jnp.concatenate([q[0], q[1 + d]], axis=0))
                out[1 + d] = base(1 + d) - gain * both[:32]
                both = both[32:]
            else:
                both = derivative(d, q[1 + d])
                out[1 + d] = base(1 + d)
            total = both if total is None else total + both
        out[0] = base(0) - gain * total
        for side, d, move in ((0, 1, 28), (1, 1, 4), (0, 2, 31), (1, 2, 1)):
            for j in range(4):
                near[side, d - 1, j] = pltpu.roll(chars[side, d, j], move, 0)
        for copy in copies[2:6]:
            copy.wait_recv()
        for side, top in ((0, 12), (1, 0)):
            for j in range(4):
                block = slice(128 * j, 128 * j + 128)
                near[side, 0, j, top : top + 4, :] = ay[turn, side, 0:4, block]
                near[side, 0, j, top + 16 : top + 20, :] = ay[turn, side, 4:8, block]
                near[side, 1, j, pl.ds(3 - 3 * side, 8, stride=4), :] = az[turn, side, :, block]
        k = 0.5 * lift_factor * gain
        for d, period, move in ((1, 64, 56), (2, 8, 7)):
            place = lax.rem(lane32, period)
            span = period - move
            for j in range(4):
                block = slice(128 * j, 128 * j + 128)
                high = pltpu.roll(near[0, d - 1, j], move, 1) - chars[0, d, j]
                high = jnp.where(place >= move, k * high, 0.0)
                low = chars[1, d, j] - pltpu.roll(near[1, d - 1, j], 128 - move, 1)
                low = jnp.where(place < span, k * low, 0.0)
                out[0, :, block] += high - low
                out[1 + d, :, block] -= high + low
        for copy in copies[0:2]:
            if copy is not None:
                copy.wait_recv()
        other = jnp.concatenate([chars[0, 0, 0, 16:32, :], ax[turn, 0]], axis=0)
        jump = pltpu.roll(other, 64, 1) - chars[0, 0, 3]
        jump = jnp.where(lane32 >= 64, k * jump, 0.0)
        out[0, :, 384:512] += jump
        out[1, :, 384:512] -= jump
        other = jnp.concatenate([ax[turn, 1], chars[1, 0, 3, 0:16, :]], axis=0)
        jump = chars[1, 0, 0] - pltpu.roll(other, 64, 1)
        jump = jnp.where(lane32 < 64, k * jump, 0.0)
        out[0, :, 0:128] -= jump
        out[1, :, 0:128] -= jump

    loads[3].wait()
    for i in range(32):
        c, part = i // 8, i % 8
        q0[c, 4 * part : 4 * part + 4, :] = stage[i]
    faces_0 = face_sends(0, q0)

    def interior(source, target, gain, base):
        half, visc = 0.5 * gain, viscosity * gain

        def update(x, before, first):
            state = [source[c, slab(x), :] for c in range(5)]
            along_x, along_y, along_z = fluxes(state)
            sums, later = [], []
            for c in range(5):
                soft = visc * state[c]
                acc = base(c, x, state[c]) - 6.0 * soft
                part = half * along_z[c]
                acc += pltpu.roll(jnp.where(lane == 0, 0.0, soft - part), 127, 1)
                acc += pltpu.roll(jnp.where(lane == 127, 0.0, soft + part), 1, 1)
                part = half * along_y[c]
                acc += pltpu.roll(jnp.where(row == 0, 0.0, soft - part), 15, 0)
                acc += pltpu.roll(jnp.where(row == 15, 0.0, soft + part), 1, 0)
                part = half * along_x[c]
                if not first:
                    target[c, slab(x - 1), :] = before[c] + (soft - part)
                    acc += before[5 + c]
                sums.append(acc)
                later.append(soft + part)
            return sums + later

        carry = update(0, None, True)
        carry = lax.fori_loop(1, 16, lambda x, b: update(x, b, False), carry)
        for c in range(5):
            target[c, 240:256, :] = carry[c]

    def boundary_yz(turn, target, gain, copies):
        half, visc = 0.5 * gain, viscosity * gain
        for copy in copies:
            copy.wait_recv()
        lower, upper = [hy[turn, 0, c] for c in range(5)], [hy[turn, 1, c] for c in range(5)]
        low_flux, up_flux = fluxes(lower)[1], fluxes(upper)[1]
        for c in range(5):
            target[c, pl.ds(0, 16, stride=16), :] += visc * lower[c] + half * low_flux[c]
            target[c, pl.ds(15, 16, stride=16), :] += visc * upper[c] - half * up_flux[c]
        both = [
            jnp.where(odd, pltpu.roll(hz[turn, 0, c], 1, 1), pltpu.roll(hz[turn, 1, c], 127, 1))
            for c in range(5)
        ]
        flux = fluxes(both)[2]
        return [
            visc * both[c] + jnp.where(odd, half * flux[c], -half * flux[c]) for c in range(5)
        ]

    def boundary_x(turn, target, gain, copies):
        half, visc = 0.5 * gain, viscosity * gain
        outer = []
        for side, rows, copy in ((0, slice(0, 16), copies[0]), (1, slice(240, 256), copies[1])):
            copy.wait_recv()
            state = [hx[turn, side, c] for c in range(5)]
            flux = fluxes(state)[0]
            values = []
            for c in range(5):
                term = half * flux[c] if side == 0 else -half * flux[c]
                value = target[c, rows, :] + (visc * state[c] + term)
                target[c, rows, :] = value
                values.append(value)
            outer.append(values)
        return outer

    def add_edges(target, terms, x):
        values = []
        for c in range(5):
            moved = pltpu.roll(terms[c], 127 - 2 * x, 1)
            value = target[c, slab(x), :] + jnp.where(edge, moved, 0.0)
            target[c, slab(x), :] = value
            values.append(value)
        return values

    interior(s0, s1, flow_step, lambda c, x, u: u)
    terms = boundary_yz(0, s1, flow_step, round_yz)
    packed = [s1[c, 16:32, :] for c in range(5)]
    packed = lax.fori_loop(1, 15, lambda x, p: pack_lanes(p, add_edges(s1, terms, x), x), packed)
    for x in (0, 15):
        add_edges(s1, terms, x)
    outer = boundary_x(0, s1, flow_step, round_x)
    round_x = sends_x(1, lambda r: s1.at[:, r : r + 16, :], every)
    packed = pack_lanes(pack_lanes(packed, outer[0], 0), outer[1], 15)
    for c in range(5):
        sz[1, c] = packed[c]
    pack_rows(1, s1, range(5))
    round_yz = sends_yz(1, every)

    interior(s1, s2, 0.5 * flow_step, lambda c, x, u: 0.5 * (s0[c, slab(x), :] + u))
    for load in loads[5:]:
        load.wait()
    rates(q0, q1, sound_step, lambda c: q0[c], faces_0, 0, True)
    faces_1 = face_sends(1, q1)
    terms_2 = boundary_yz(1, s2, 0.5 * flow_step, round_yz)

    def velocity(x, values):
        inverse = 1.0 / values[0]
        vx, vy, vz = (values[d] * inverse for d in (1, 2, 3))
        vel[0, slab(x), :], vel[1, slab(x), :], vel[2, slab(x), :] = vy, vz, vx
        return [vy, vx]

    zero = jnp.zeros((16, 128), F32)
    packed = lax.fori_loop(
        1, 15, lambda x, p: pack_lanes(p, velocity(x, add_edges(s2, terms_2, x)), x), [zero, zero]
    )
    for x in (0, 15):
        add_edges(s2, terms_2, x)
    outer = boundary_x(1, s2, 0.5 * flow_step, round_x)
    outer = [velocity(0, outer[0]), velocity(15, outer[1])]
    round_x = sends_x(2, lambda r: vel.at[0:2, r : r + 16, :], pl.ds(0, 2))
    sz[2, 0], sz[2, 1] = pack_lanes(pack_lanes(packed, outer[0], 0), outer[1], 15)
    for i, comp in enumerate((1, 2)):
        sy[2, 0, i] = vel[comp, pl.ds(15, 16, stride=16), :]
        sy[2, 1, i] = vel[comp, pl.ds(0, 16, stride=16), :]
    round_yz = sends_yz(2, pl.ds(0, 2))

    stores = [
        pltpu.make_async_copy(s2.at[0], rho_out, out_sem.at[0]),
        pltpu.make_async_copy(s2.at[1:4], mom_out, out_sem.at[1]),
        pltpu.make_async_copy(s2.at[4], energy_out, out_sem.at[2]),
    ]
    for store in stores:
        store.start()

    def dy(f):
        up = pltpu.roll(jnp.where(row == 0, 0.0, f), 15, 0)
        return up - pltpu.roll(jnp.where(row == 15, 0.0, f), 1, 0)

    def dz(f):
        up = pltpu.roll(jnp.where(lane == 0, 0.0, f), 127, 1)
        return up - pltpu.roll(jnp.where(lane == 127, 0.0, f), 1, 1)

    def curl(x, carry):
        vy, vz, vx = (vel[i, slab(x), :] for i in range(3))
        after = slab(jnp.minimum(x + 1, 15))
        before = slab(jnp.maximum(x - 1, 0))
        dx_vy, dx_vz = (
            jnp.where(x < 15, vel[i, after, :], 0.0) - jnp.where(x > 0, vel[i, before, :], 0.0)
            for i in range(2)
        )
        vort[0, slab(x), :] = dy(vz) - dz(vy)
        vort[1, slab(x), :] = dz(vx) - dx_vz
        vort[2, slab(x), :] = dx_vy - dy(vx)
        return carry

    lax.fori_loop(0, 16, curl, 0)
    rates(q1, n0, 0.5 * sound_step, lambda c: 0.5 * (q0[c] + q1[c]), faces_1, 1, True)
    for copy in round_yz:
        copy.wait_recv()
    vort[0, pl.ds(0, 16, stride=16), :] -= hy[2, 0, 0]
    vort[2, pl.ds(0, 16, stride=16), :] += hy[2, 0, 1]
    vort[0, pl.ds(15, 16, stride=16), :] += hy[2, 1, 0]
    vort[2, pl.ds(15, 16, stride=16), :] -= hy[2, 1, 1]
    side_y, side_x = (
        jnp.where(odd, pltpu.roll(hz[2, 0, i], 1, 1), pltpu.roll(hz[2, 1, i], 127, 1))
        for i in range(2)
    )
    side_y = jnp.where(odd, side_y, -side_y)
    side_x = jnp.where(odd, -side_x, side_x)

    def lamb_pair(a, carry):
        sums = [None] * 3
        for x in (2 * a, 2 * a + 1):
            wx = vort[0, slab(x), :] + jnp.where(edge, pltpu.roll(side_y, 127 - 2 * x, 1), 0.0)
            wy = vort[1, slab(x), :] + jnp.where(edge, pltpu.roll(side_x, 127 - 2 * x, 1), 0.0)
            wz = vort[2, slab(x), :]
            vy, vz, vx = (vel[i, slab(x), :] for i in range(3))
            parts = (wy * vz - wz * vy, wz * vx - wx * vz, wx * vy - wy * vx)
            sums = [p if s is None else s + p for s, p in zip(sums, parts)]
        for d in range(3):
            mref[d, slab(a), :] = 0.0625 * sums[d]
        return carry

    lax.fori_loop(1, 7, lamb_pair, 0)
    round_x[0].wait_recv()
    vort[1, 0:16, :] += hx[2, 0, 1]
    vort[2, 0:16, :] -= hx[2, 0, 0]
    lamb_pair(0, 0)
    round_x[1].wait_recv()
    vort[1, 240:256, :] -= hx[2, 1, 1]
    vort[2, 240:256, :] += hx[2, 1, 0]
    lamb_pair(7, 0)
    coarse = [
        mref[d, pl.ds(0, 64, stride=2), :] + mref[d, pl.ds(1, 64, stride=2), :] for d in range(3)
    ]
    fref[0] = jnp.transpose(jnp.concatenate([coarse[0], coarse[1]], axis=0))
    fref[1] = jnp.transpose(jnp.concatenate([coarse[2], coarse[2]], axis=0))
    pieces = [
        [
            fref[i, pl.ds(2 * c, 8, stride=16), :] + fref[i, pl.ds(2 * c + 1, 8, stride=16), :]
            for c in range(8)
        ]
        for i in range(2)
    ]
    left = iota((8, 128), 1) < 64
    rows = [[], [], []]
    for j in range(4):
        a, b = pieces[0][2 * j], pieces[0][2 * j + 1]
        rows[0].append(jnp.where(left, a, pltpu.roll(b, 64, 1)))
        rows[1].append(jnp.where(left, pltpu.roll(a, 64, 1), b))
        rows[2].append(jnp.where(left, pieces[1][2 * j], pieces[1][2 * j + 1]))
    own = jnp.concatenate([jnp.concatenate(r, axis=1) for r in rows], axis=0)
    high, rest = halves(own)
    middle, low = halves(rest)
    loads[4].wait()
    parts = jnp.concatenate([high, middle, low], axis=0).astype(BF16)
    parts = jnp.dot(parts, order[...], preferred_element_type=F32)
    own = parts[0:24] + parts[24:48] + parts[48:72]
    for d in range(3):
        tiles[0, :, 512 * d : 512 * d + 512] = own[8 * d : 8 * d + 8]
    row8, lane8 = iota((8, 128), 0), iota((8, 128), 1)
    label = jnp.zeros((8, 128), jnp.int32)
    for t in range(8):
        both = jnp.where(lane8 < 64, slot_ref[0, 0, 0, t], element_ref[0, 0, 0, t])
        label = jnp.where(row8 == t, both, label)
    tiles[0, :, 1536:1664] = label.astype(F32)

    down = [
        (k, send(tiles.at[0], tiles.at[k], tile_send.at[k - 1], tile_recv.at[k - 1], at_zh(k)))
        for k in sorted(range(1, zh_count), key=lambda k: -min(k, zh_count - k))
    ]
    down.sort(key=lambda item: item[0])
    across = []
    slots = 4 * x_count
    place = iota((slots, 128), 0)
    peer = zh * x_count + lax.rem(xi + place // 4, x_count)

    def slot_of(step):
        owner = lax.rem(peer + step + gx_count, gx_count)
        return (owner * 4 + lax.rem(place, 4)).astype(F32)

    wanted, wanted_after, wanted_before = slot_of(0), slot_of(1), slot_of(-1)

    def pass_on(k):
        marks = tiles[k, :, 1536:1664]
        named = jnp.where(lane8 < 64, marks, pltpu.roll(marks, 64, 1))
        named = [jnp.broadcast_to(named[t : t + 1], (slots, 128)) for t in range(8)]

        def pick(hits, value, block):
            chosen = jnp.zeros((slots, 128), F32)
            for t in range(8):
                row = jnp.broadcast_to(value[t : t + 1], (slots, 128))
                chosen = jnp.where(hits[t], row, chosen)
            full[k * slots : k * slots + 4, block] = chosen[0:4]
            for j in range(1, x_count):
                parcel[k, j - 1, :, block] = chosen[4 * j : 4 * j + 4]

        hits = [n == wanted for n in named]
        for first in range(0, TILE_LANES, 128):
            block = slice(first, first + 128)
            pick(hits, tiles[k, :, block], block)
        low_face = jnp.where(lane8 < 64, tiles[k, :, 0:128], marks)
        pick([n == wanted_after for n in named], low_face, slice(1664, 1792))
        high_face = jnp.where(lane8 < 64, pltpu.roll(marks, 64, 1), tiles[k, :, 384:512])
        pick([n == wanted_before for n in named], high_face, slice(1792, 1920))
        for j in range(1, x_count):
            i = zh_count - 1 + k * (x_count - 1) + j - 1
            across.append(
                send(
                    parcel.at[k, j - 1], arrived.at[k, j - 1], tile_send.at[i], tile_recv.at[i],
                    at_xi(j),
                )
            )

    pass_on(0)

    for k in sorted(range(1, zh_count), key=lambda k: min(k, zh_count - k)):
        down[k - 1][1].wait_recv()
        pass_on(k)
    for i, copy in enumerate(across):
        copy.wait_recv()
    for k in range(zh_count):
        for j in range(1, x_count):
            top = k * slots + 4 * j
            full[top : top + 4, :] = arrived[k, j - 1]
    count = zh_count * slots
    lanes = iota((count, 128), 1)
    element = (lanes - 64).astype(F32)
    picking = jnp.where(full[:, 1536:1664] == element, 1.0, 0.0)
    picking = jnp.concatenate([picking, picking], axis=0)
    picking = jnp.transpose(picking)[64:96].astype(BF16)

    def pick_source(d):
        high, low = halves(full[:, 512 * d : 512 * d + 512])
        parts = jnp.concatenate([high, low], axis=0).astype(BF16)
        both = jnp.dot(picking, parts, preferred_element_type=F32)
        q1[1 + d] = -source_gain * sound_step * both

    pick_source(1)
    pick_source(2)
    faces_2 = []
    for d, (kept, landing, device) in enumerate(((ays, ay, at_y), (azs, az, at_z))):
        for side in (0, 1):
            for j in range(4):
                block = slice(128 * j, 128 * j + 128)
                value = q1[2 + d, :, block] if side else -q1[2 + d, :, block]
                chars[side, 1 + d, j] = value
                if d == 0:
                    top = 12 * side
                    kept[2, side, 0:4, block] = chars[side, 1, j, top : top + 4, :]
                    kept[2, side, 4:8, block] = chars[side, 1, j, top + 16 : top + 20, :]
                else:
                    kept[2, side, :, block] = chars[side, 2, j, pl.ds(3 * side, 8, stride=4), :]
            i = 2 + 2 * d + side
            faces_2.append(
                send(
                    kept.at[2, side], landing.at[2, side], face_send.at[2, i],
                    face_recv.at[2, i], device(2 * side - 1),
                )
            )
    pick_source(0)
    for j in range(4):
        block = slice(128 * j, 128 * j + 128)
        chars[0, 0, j] = -q1[1, :, block]
        chars[1, 0, j] = q1[1, :, block]
    after, before = full[:, 1664:1792], full[:, 1792:1920]
    picking_2 = jnp.concatenate(
        [
            jnp.where((lanes >= 64) & (after == element), 1.0, 0.0),
            jnp.where((lanes < 64) & (before == element + 80.0), 1.0, 0.0),
        ],
        axis=0,
    )
    if 2 * count < 128:
        picking_2 = jnp.concatenate([picking_2, jnp.zeros((128 - 2 * count, 128), F32)], axis=0)
    picking_2 = jnp.transpose(picking_2)[:, 0 : 2 * count]
    picking_2 = jnp.concatenate([picking_2[64:80], picking_2[0:16]], axis=0).astype(BF16)
    high, low = halves(jnp.concatenate([after, before], axis=0))
    sides = jnp.dot(picking_2, high.astype(BF16), preferred_element_type=F32)
    sides += jnp.dot(picking_2, low.astype(BF16), preferred_element_type=F32)
    ax[2, 0] = source_gain * sound_step * sides[0:16]
    ax[2, 1] = -source_gain * sound_step * sides[16:32]
    rates(q1, q0, 0.5 * sound_step, lambda c: n0[c] + (q1[c] if c else 0.0), [None, None] + faces_2, 2, False)
    for i in range(32):
        c, part = i // 8, i % 8
        stage[i] = q0[c, 4 * part : 4 * part + 4, :]
    stores.append(pltpu.make_async_copy(stage, sound_out, out_sem.at[3]))
    stores[-1].start()
    for copy in pending:
        copy.wait_send()
    for store in stores:
        store.wait()


def hand_over(*refs):
    copies = [pltpu.make_async_copy(refs[i], refs[4 + i], refs[8].at[i]) for i in range(4)]
    for copy in copies:
        copy.start()
    for copy in copies:
        copy.wait()


def solution(mesh):
    gx_count, gy_count, gz_count = (mesh.shape[a] for a in ("gx", "gy", "gz"))
    x_count = 4 if gx_count == 16 else 2
    zh_count = gx_count // x_count
    tile_sends = (zh_count - 1) + zh_count * (x_count - 1)
    consts = tables()

    def on_device(density, momentum, energy, acoustic, tile_slot, tile_element):
        anywhere = pl.BlockSpec(memory_space=pl.ANY)
        in_hbm = pl.BlockSpec(memory_space=pltpu.HBM)
        scalars = pl.BlockSpec(memory_space=pltpu.SMEM)
        out_shape = (
            jax.ShapeDtypeStruct((256, 128), F32),
            jax.ShapeDtypeStruct((3, 256, 128), F32),
            jax.ShapeDtypeStruct((256, 128), F32),
            jax.ShapeDtypeStruct((32, 4, 512), F32),
        )
        vmem = pltpu.VMEM
        scratch = [
            vmem((5, 256, 128), F32), vmem((5, 256, 128), F32), vmem((5, 256, 128), F32),
            vmem((3, 256, 128), F32), vmem((3, 256, 128), F32), vmem((3, 128, 128), F32),
            vmem((2, 128, 128), F32), vmem((zh_count, 8, TILE_LANES), F32),
            vmem((zh_count, x_count - 1, 4, PARCEL_LANES), F32),
            vmem((zh_count, x_count - 1, 4, PARCEL_LANES), F32),
            vmem((4 * gx_count, PARCEL_LANES), F32),
            vmem((3, 2, 5, 16, 128), F32), vmem((3, 2, 5, 16, 128), F32),
            vmem((3, 2, 5, 16, 128), F32), vmem((3, 2, 5, 16, 128), F32),
            vmem((3, 5, 16, 128), F32),
            vmem((3, 2, 16, 128), F32), vmem((3, 2, 8, 512), F32), vmem((3, 2, 8, 512), F32),
            vmem((2, 2, 16, 128), F32), vmem((3, 2, 8, 512), F32), vmem((3, 2, 8, 512), F32),
            vmem((32, 4, 512), F32), vmem((4, 32, 512), F32), vmem((4, 32, 512), F32),
            vmem((4, 32, 512), F32), vmem((2, 3, 4, 32, 128), F32), vmem((2, 2, 4, 32, 128), F32),
            vmem((512, 512), BF16), vmem((512, 512), BF16), vmem((256, 256), BF16),
            vmem((256, 256), BF16), vmem((256, 256), BF16), vmem((256, 256), BF16),
            vmem((512, 512), BF16),
            pltpu.SemaphoreType.DMA((11,)), pltpu.SemaphoreType.DMA((4,)),
            pltpu.SemaphoreType.DMA((3, 6)), pltpu.SemaphoreType.DMA((3, 6)),
            pltpu.SemaphoreType.DMA((3, 6)), pltpu.SemaphoreType.DMA((3, 6)),
            pltpu.SemaphoreType.DMA((tile_sends,)), pltpu.SemaphoreType.DMA((tile_sends,)),
        ]
        held_shape = tuple(pltpu.VMEM(o.shape, F32) for o in out_shape)
        outs = pl.pallas_call(
            functools.partial(kernel, zh_count, x_count, gy_count, gz_count),
            out_shape=held_shape,
            in_specs=[anywhere] * 4 + [scalars] * 2 + [anywhere] * 7,
            out_specs=[anywhere] * 4,
            scratch_shapes=scratch,
            compiler_params=pltpu.CompilerParams(
                collective_id=0, has_side_effects=True, vmem_limit_bytes=57 * 2**20
            ),
            cost_estimate=pl.CostEstimate(
                flops=10**9, bytes_accessed=4 * 2**20, transcendentals=0
            ),
        )(
            density.reshape(256, 128), momentum.reshape(3, 256, 128), energy.reshape(256, 128),
            acoustic.reshape(32, 4, 512), tile_slot, tile_element,
            *[jnp.asarray(c) for c in consts],
        )
        outs = pl.pallas_call(
            hand_over,
            out_shape=out_shape,
            in_specs=[anywhere] * 4,
            out_specs=[in_hbm] * 4,
            scratch_shapes=[pltpu.SemaphoreType.DMA((4,))],
            compiler_params=pltpu.CompilerParams(vmem_limit_bytes=8 * 2**20),
        )(*outs)
        return (
            outs[0].reshape(16, 16, 128), outs[1].reshape(3, 16, 16, 128),
            outs[2].reshape(16, 16, 128), outs[3].reshape(4, 2, 4, 4, 512),
        )

    in_specs = (
        P("gx", "gy", "gz"), P(None, "gx", "gy", "gz"), P("gx", "gy", "gz"),
        P(None, "gx", "gy", "gz", None), P("gx", "gy", "gz", None), P("gx", "gy", "gz", None),
    )
    out_specs = (
        P("gx", "gy", "gz"), P(None, "gx", "gy", "gz"), P("gx", "gy", "gz"),
        P(None, "gx", "gy", "gz", None),
    )
    return jax.shard_map(
        on_device, mesh=mesh, in_specs=in_specs, out_specs=out_specs, check_vma=False
    )
```

```python
import functools

import jax
import jax.numpy as jnp
import ml_dtypes
import numpy as np
from jax import lax
from jax.experimental import pallas as pl
from jax.experimental.pallas import tpu as pltpu
from jax.sharding import PartitionSpec as P

MESH = pl.DeviceIdType.MESH
F32 = jnp.float32
BF16 = jnp.bfloat16

flow_step = 0.05
viscosity = 0.2
sound_step = 0.02
lift_factor = 28.0
source_gain = 40.0
TILE_LANES = 1536
PARCEL_LANES = 1664
PARTS = 2


def derivative_numbers():
    order = 7
    points = np.array(
        [
            -1.0,
            -0.8717401485096066,
            -0.5917001814331423,
            -0.2092992179024789,
            0.2092992179024789,
            0.5917001814331423,
            0.8717401485096066,
            1.0,
        ]
    )
    previous = np.ones(8)
    current = points * 1.0
    for degree in range(1, order):
        following = ((2 * degree + 1) * points * current - degree * previous) / (degree + 1)
        previous = current
        current = following
    table = np.zeros((8, 8))
    for row in range(8):
        for column in range(8):
            if row != column:
                table[row, column] = current[row] / (
                    current[column] * (points[row] - points[column])
                )
    table[0, 0] = -order * (order + 1) / 4.0
    table[order, order] = order * (order + 1) / 4.0
    return table


def split_table(table):
    table = table.astype(np.float32)
    high = table.astype(ml_dtypes.bfloat16)
    low = (table - high.astype(np.float32)).astype(ml_dtypes.bfloat16)
    return high, low


def tables():
    table = derivative_numbers()
    eye = np.eye(8)
    along_x = np.kron(np.kron(table, eye), eye).T
    along_y = np.kron(np.kron(np.eye(4), table), eye).T
    along_z = np.kron(np.kron(np.eye(4), eye), table).T
    order = np.zeros((512, 512), ml_dtypes.bfloat16)
    for c in range(8):
        for ab in range(64):
            order[c * 64 + ab, ab * 8 + c] = 1.0
    return (*split_table(along_x), *split_table(along_y), *split_table(along_z), order)


def iota(shape, dim):
    return lax.broadcasted_iota(jnp.int32, shape, dim)


def fluxes(state):
    rho, mx, my, mz, energy = state
    inverse = 1.0 / rho
    vx, vy, vz = mx * inverse, my * inverse, mz * inverse
    pressure = 0.4 * (energy - 0.5 * (mx * vx + my * vy + mz * vz))
    total = energy + pressure
    xy, xz, yz = mx * vy, mx * vz, my * vz
    return (
        [mx, mx * vx + pressure, xy, xz, total * vx],
        [my, xy, my * vy + pressure, yz, total * vy],
        [mz, xz, yz, mz * vz + pressure, total * vz],
    )


def halves(value):
    high = value.astype(BF16).astype(F32)
    return high, value - high


def kernel(
    zh_count, x_count, gy_count, gz_count,
    rho_hbm, mom_hbm, energy_hbm, sound_hbm, slot_ref, element_ref,
    dxh_hbm, dxl_hbm, dyh_hbm, dyl_hbm, dzh_hbm, dzl_hbm, order_hbm,
    rho_out, mom_out, energy_out, sound_out,
    s0, s1, s2, vel, vort, mref, fref, tiles, parcel, arrived, full, labels, named_elements,
    hx, hy, hz, sy, sz, ax, ay, az, axs, ays, azs,
    stage, q0, q1, n0, chars, near,
    dxh, dxl, dyh, dyl, dzh, dzl, order,
    in_sem, out_sem, flow_send, flow_recv, face_send, face_recv, tile_send, tile_recv,
    label_send, label_recv,
):
    gx, gy, gz = lax.axis_index("gx"), lax.axis_index("gy"), lax.axis_index("gz")
    gx_count = zh_count * x_count
    tile_sends = (zh_count - 1) + zh_count * (x_count - 1)
    zh, xi = gx // x_count, lax.rem(gx, x_count)

    def at_x(step):
        return (lax.rem(gx + step + gx_count, gx_count), gy, gz)

    def at_y(step):
        return (gx, lax.rem(gy + step + gy_count, gy_count), gz)

    def at_z(step):
        return (gx, gy, lax.rem(gz + step + gz_count, gz_count))

    def at_zh(step):
        return (lax.rem(zh + step, zh_count) * x_count + xi, gy, gz)

    def at_xi(step):
        return (zh * x_count + lax.rem(xi + step, x_count), gy, gz)

    barrier = pltpu.get_barrier_semaphore()
    partners = [at_x(-1), at_x(1), at_y(-1), at_y(1), at_z(-1), at_z(1)]
    partners += [at_zh(k) for k in range(1, zh_count)] + [at_xi(j) for j in range(1, x_count)]
    for partner in partners:
        pl.semaphore_signal(barrier, inc=1, device_id=partner, device_id_type=MESH)

    loads = [
        (rho_hbm, s0.at[0]), (mom_hbm, s0.at[1:4]), (energy_hbm, s0.at[4]), (sound_hbm, stage),
        (order_hbm, order), (dxh_hbm, dxh), (dxl_hbm, dxl), (dyh_hbm, dyh), (dyl_hbm, dyl),
        (dzh_hbm, dzh), (dzl_hbm, dzl),
    ]
    loads = [pltpu.make_async_copy(a, b, in_sem.at[i]) for i, (a, b) in enumerate(loads)]
    for load in loads:
        load.start()

    lane = iota((16, 128), 1)
    row = iota((16, 128), 0)
    odd = lax.rem(lane, 2) == 1
    edge = (lane == 0) | (lane == 127)
    pair = lane // 2

    pending = []

    def send(src, dst, send_sem, recv_sem, device):
        copy = pltpu.make_async_remote_copy(
            src_ref=src, dst_ref=dst, send_sem=send_sem, recv_sem=recv_sem,
            device_id=device, device_id_type=MESH,
        )
        copy.start()
        pending.append(copy)
        return copy

    def flow_go(turn, i, src, dst, device):
        return send(src, dst, flow_send.at[turn, i], flow_recv.at[turn, i], device)

    def sends_x(turn, x_source, comps):
        return [
            flow_go(turn, 0, x_source(240), hx.at[turn, 0, comps], at_x(1)),
            flow_go(turn, 1, x_source(0), hx.at[turn, 1, comps], at_x(-1)),
        ]

    def sends_yz(turn, comps):
        return [
            flow_go(turn, 2, sz.at[turn, comps], hz.at[turn, 0, comps], at_z(1)),
            flow_go(turn, 3, sz.at[turn, comps], hz.at[turn, 1, comps], at_z(-1)),
            flow_go(turn, 4, sy.at[turn, 0, comps], hy.at[turn, 0, comps], at_y(1)),
            flow_go(turn, 5, sy.at[turn, 1, comps], hy.at[turn, 1, comps], at_y(-1)),
        ]

    def slab(x):
        return pl.ds(pl.multiple_of(x * 16, 16), 16)

    def pack_lanes(packed, values, x):
        here = pair == x
        return [jnp.where(here, pltpu.roll(v, 2 * x + 1, 1), p) for p, v in zip(packed, values)]

    def pack_rows(turn, ref, comps):
        for c in comps:
            sy[turn, 0, c] = ref[c, pl.ds(15, 16, stride=16), :]
            sy[turn, 1, c] = ref[c, pl.ds(0, 16, stride=16), :]

    for load in loads[:3]:
        load.wait()
    pack_rows(0, s0, range(5))

    def pack_first(x, packed):
        return pack_lanes(packed, [s0[c, slab(x), :] for c in range(5)], x)

    first_slab = [s0[c, 0:16, :] for c in range(5)]
    for c, value in enumerate(lax.fori_loop(0, 16, pack_first, first_slab)):
        sz[0, c] = value
    pl.semaphore_wait(barrier, len(partners))
    every = pl.ds(0, 5)
    round_x = sends_x(0, lambda r: s0.at[:, r : r + 16, :], every)
    round_yz = sends_yz(0, every)

    row8, lane8 = iota((8, 128), 0), iota((8, 128), 1)
    label = jnp.zeros((8, 128), jnp.int32)
    for t in range(8):
        both = jnp.where(lane8 < 64, slot_ref[0, 0, 0, t], element_ref[0, 0, 0, t])
        label = jnp.where(row8 == t, both, label)
    labels[0, 0] = label.astype(F32)
    labels_down = [
        send(labels.at[0, 0], labels.at[0, k], label_send.at[k - 1], label_recv.at[k - 1], at_zh(k))
        for k in range(1, zh_count)
    ]

    def face_sends(turn, q):
        for d in range(3):
            for j in range(4):
                block = slice(128 * j, 128 * j + 128)
                chars[0, d, j] = q[0, :, block] - q[1 + d, :, block]
                chars[1, d, j] = q[0, :, block] + q[1 + d, :, block]
        axs[turn, 0] = chars[0, 0, 0, 0:16, :]
        axs[turn, 1] = chars[1, 0, 3, 16:32, :]
        for side, top in ((0, 0), (1, 12)):
            for j in range(4):
                block = slice(128 * j, 128 * j + 128)
                ays[turn, side, 0:4, block] = chars[side, 1, j, top : top + 4, :]
                ays[turn, side, 4:8, block] = chars[side, 1, j, top + 16 : top + 20, :]
                azs[turn, side, :, block] = chars[side, 2, j, pl.ds(3 * side, 8, stride=4), :]

        def go(i, src, dst, device):
            return send(src, dst, face_send.at[turn, i], face_recv.at[turn, i], device)

        along_x = [
            go(0, axs.at[turn, 0], ax.at[turn, 0], at_x(-1)),
            go(1, axs.at[turn, 1], ax.at[turn, 1], at_x(1)),
        ]
        return along_x + [
            go(2, ays.at[turn, 0], ay.at[turn, 0], at_y(-1)),
            go(3, ays.at[turn, 1], ay.at[turn, 1], at_y(1)),
            go(4, azs.at[turn, 0], az.at[turn, 0], at_z(-1)),
            go(5, azs.at[turn, 1], az.at[turn, 1], at_z(1)),
        ]

    def apply3(value, high, low):
        rows = value.shape[0]
        top, rest = halves(value)
        both = jnp.concatenate([top, rest], axis=0).astype(BF16)
        part = jnp.dot(both, high, preferred_element_type=F32)
        return (
            part[:rows] + part[rows:]
            + jnp.dot(top.astype(BF16), low, preferred_element_type=F32)
        )

    def derivative(d, value):
        if d == 0:
            return apply3(value, dxh[...], dxl[...])
        high, low = (dyh, dyl) if d == 1 else (dzh, dzl)
        split = [apply3(value[:, s : s + 256], high[...], low[...]) for s in (0, 256)]
        return jnp.concatenate(split, axis=1)

    lane32 = iota((32, 128), 1)

    def rates(q, out, gain, base, copies, turn, with_pressure):
        total = None
        for d in range(3):
            if with_pressure:
                both = derivative(d, jnp.concatenate([q[0], q[1 + d]], axis=0))
                out[1 + d] = base(1 + d) - gain * both[:32]
                both = both[32:]
            else:
                both = derivative(d, q[1 + d])
                out[1 + d] = base(1 + d)
            total = both if total is None else total + both
        out[0] = base(0) - gain * total
        k = 0.5 * lift_factor * gain

        def lift_x():
            other = jnp.concatenate([chars[0, 0, 0, 16:32, :], ax[turn, 0]], axis=0)
            jump = pltpu.roll(other, 64, 1) - chars[0, 0, 3]
            jump = jnp.where(lane32 >= 64, k * jump, 0.0)
            out[0, :, 384:512] += jump
            out[1, :, 384:512] -= jump
            other = jnp.concatenate([ax[turn, 1], chars[1, 0, 3, 0:16, :]], axis=0)
            jump = chars[1, 0, 0] - pltpu.roll(other, 64, 1)
            jump = jnp.where(lane32 < 64, k * jump, 0.0)
            out[0, :, 0:128] -= jump
            out[1, :, 0:128] -= jump

        if not copies[0]:
            lift_x()
        for side, d, move in ((0, 1, 28), (1, 1, 4), (0, 2, 31), (1, 2, 1)):
            for j in range(4):
                near[side, d - 1, j] = pltpu.roll(chars[side, d, j], move, 0)
        for copy in copies[2:6]:
            copy.wait_recv()
        for side, top in ((0, 12), (1, 0)):
            for j in range(4):
                block = slice(128 * j, 128 * j + 128)
                near[side, 0, j, top : top + 4, :] = ay[turn, side, 0:4, block]
                near[side, 0, j, top + 16 : top + 20, :] = ay[turn, side, 4:8, block]
                near[side, 1, j, pl.ds(3 - 3 * side, 8, stride=4), :] = az[turn, side, :, block]
        for d, period, move in ((1, 64, 56), (2, 8, 7)):
            place = lax.rem(lane32, period)
            span = period - move
            for j in range(4):
                block = slice(128 * j, 128 * j + 128)
                high = pltpu.roll(near[0, d - 1, j], move, 1) - chars[0, d, j]
                high = jnp.where(place >= move, k * high, 0.0)
                low = chars[1, d, j] - pltpu.roll(near[1, d - 1, j], 128 - move, 1)
                low = jnp.where(place < span, k * low, 0.0)
                out[0, :, block] += high - low
                out[1 + d, :, block] -= high + low
        if copies[0]:
            for copy in copies[0:2]:
                copy.wait_recv()
            lift_x()

    loads[3].wait()
    for i in range(32):
        c, part = i // 8, i % 8
        q0[c, 4 * part : 4 * part + 4, :] = stage[i]
    faces_0 = face_sends(0, q0)

    def interior(source, target, gain, base):
        half, visc = 0.5 * gain, viscosity * gain

        def update(x, before, first):
            state = [source[c, slab(x), :] for c in range(5)]
            along_x, along_y, along_z = fluxes(state)
            sums, later = [], []
            for c in range(5):
                soft = visc * state[c]
                acc = base(c, x, state[c]) - 6.0 * soft
                part = half * along_z[c]
                acc += pltpu.roll(jnp.where(lane == 0, 0.0, soft - part), 127, 1)
                acc += pltpu.roll(jnp.where(lane == 127, 0.0, soft + part), 1, 1)
                part = half * along_y[c]
                acc += pltpu.roll(jnp.where(row == 0, 0.0, soft - part), 15, 0)
                acc += pltpu.roll(jnp.where(row == 15, 0.0, soft + part), 1, 0)
                part = half * along_x[c]
                if not first:
                    target[c, slab(x - 1), :] = before[c] + (soft - part)
                    acc += before[5 + c]
                sums.append(acc)
                later.append(soft + part)
            return sums + later

        carry = update(0, None, True)
        carry = lax.fori_loop(1, 16, lambda x, b: update(x, b, False), carry)
        for c in range(5):
            target[c, 240:256, :] = carry[c]

    def boundary_yz(turn, target, gain, copies):
        half, visc = 0.5 * gain, viscosity * gain
        for copy in copies:
            copy.wait_recv()
        lower, upper = [hy[turn, 0, c] for c in range(5)], [hy[turn, 1, c] for c in range(5)]
        low_flux, up_flux = fluxes(lower)[1], fluxes(upper)[1]
        for c in range(5):
            target[c, pl.ds(0, 16, stride=16), :] += visc * lower[c] + half * low_flux[c]
            target[c, pl.ds(15, 16, stride=16), :] += visc * upper[c] - half * up_flux[c]
        both = [
            jnp.where(odd, pltpu.roll(hz[turn, 0, c], 1, 1), pltpu.roll(hz[turn, 1, c], 127, 1))
            for c in range(5)
        ]
        flux = fluxes(both)[2]
        return [
            visc * both[c] + jnp.where(odd, half * flux[c], -half * flux[c]) for c in range(5)
        ]

    def boundary_x(turn, target, gain, copies):
        half, visc = 0.5 * gain, viscosity * gain
        outer = []
        for side, rows, copy in ((0, slice(0, 16), copies[0]), (1, slice(240, 256), copies[1])):
            copy.wait_recv()
            state = [hx[turn, side, c] for c in range(5)]
            flux = fluxes(state)[0]
            values = []
            for c in range(5):
                term = half * flux[c] if side == 0 else -half * flux[c]
                value = target[c, rows, :] + (visc * state[c] + term)
                target[c, rows, :] = value
                values.append(value)
            outer.append(values)
        return outer

    def add_edges(target, terms, x):
        values = []
        for c in range(5):
            moved = pltpu.roll(terms[c], 127 - 2 * x, 1)
            value = target[c, slab(x), :] + jnp.where(edge, moved, 0.0)
            target[c, slab(x), :] = value
            values.append(value)
        return values

    interior(s0, s1, flow_step, lambda c, x, u: u)
    terms = boundary_yz(0, s1, flow_step, round_yz)
    packed = [s1[c, 16:32, :] for c in range(5)]
    packed = lax.fori_loop(1, 15, lambda x, p: pack_lanes(p, add_edges(s1, terms, x), x), packed)
    for x in (0, 15):
        add_edges(s1, terms, x)
    outer = boundary_x(0, s1, flow_step, round_x)
    round_x = sends_x(1, lambda r: s1.at[:, r : r + 16, :], every)
    packed = pack_lanes(pack_lanes(packed, outer[0], 0), outer[1], 15)
    for c in range(5):
        sz[1, c] = packed[c]
    pack_rows(1, s1, range(5))
    round_yz = sends_yz(1, every)

    interior(s1, s2, 0.5 * flow_step, lambda c, x, u: 0.5 * (s0[c, slab(x), :] + u))
    for load in loads[5:]:
        load.wait()
    rates(q0, q1, sound_step, lambda c: q0[c], faces_0, 0, True)
    faces_1 = face_sends(1, q1)
    for copy in labels_down:
        copy.wait_recv()
    labels_across = [
        send(labels.at[0], labels.at[j], label_send.at[i], label_recv.at[i], at_xi(j))
        for j, i in zip(range(1, x_count), range(zh_count - 1, zh_count + x_count - 2))
    ]
    terms_2 = boundary_yz(1, s2, 0.5 * flow_step, round_yz)

    def velocity(x, values):
        inverse = 1.0 / values[0]
        vx, vy, vz = (values[d] * inverse for d in (1, 2, 3))
        vel[0, slab(x), :], vel[1, slab(x), :], vel[2, slab(x), :] = vy, vz, vx
        return [vy, vx]

    zero = jnp.zeros((16, 128), F32)
    packed = lax.fori_loop(
        1, 15, lambda x, p: pack_lanes(p, velocity(x, add_edges(s2, terms_2, x)), x), [zero, zero]
    )
    for x in (0, 15):
        add_edges(s2, terms_2, x)
    outer = boundary_x(1, s2, 0.5 * flow_step, round_x)
    outer = [velocity(0, outer[0]), velocity(15, outer[1])]
    round_x = sends_x(2, lambda r: vel.at[0:2, r : r + 16, :], pl.ds(0, 2))
    sz[2, 0], sz[2, 1] = pack_lanes(pack_lanes(packed, outer[0], 0), outer[1], 15)
    for i, comp in enumerate((1, 2)):
        sy[2, 0, i] = vel[comp, pl.ds(15, 16, stride=16), :]
        sy[2, 1, i] = vel[comp, pl.ds(0, 16, stride=16), :]
    round_yz = sends_yz(2, pl.ds(0, 2))

    stores = [
        pltpu.make_async_copy(s2.at[0], rho_out, out_sem.at[0]),
        pltpu.make_async_copy(s2.at[1:4], mom_out, out_sem.at[1]),
        pltpu.make_async_copy(s2.at[4], energy_out, out_sem.at[2]),
    ]
    for store in stores:
        store.start()

    def dy(f):
        up = pltpu.roll(jnp.where(row == 0, 0.0, f), 15, 0)
        return up - pltpu.roll(jnp.where(row == 15, 0.0, f), 1, 0)

    def dz(f):
        up = pltpu.roll(jnp.where(lane == 0, 0.0, f), 127, 1)
        return up - pltpu.roll(jnp.where(lane == 127, 0.0, f), 1, 1)

    def curl(x, carry):
        vy, vz, vx = (vel[i, slab(x), :] for i in range(3))
        after = slab(jnp.minimum(x + 1, 15))
        before = slab(jnp.maximum(x - 1, 0))
        dx_vy, dx_vz = (
            jnp.where(x < 15, vel[i, after, :], 0.0) - jnp.where(x > 0, vel[i, before, :], 0.0)
            for i in range(2)
        )
        vort[0, slab(x), :] = dy(vz) - dz(vy)
        vort[1, slab(x), :] = dz(vx) - dx_vz
        vort[2, slab(x), :] = dx_vy - dy(vx)
        return carry

    lax.fori_loop(0, 16, curl, 0)
    rates(q1, n0, 0.5 * sound_step, lambda c: 0.5 * (q0[c] + q1[c]), faces_1, 1, True)

    slots = 4 * x_count
    count = zh_count * slots
    for copy in labels_across:
        copy.wait_recv()
    for step, owner in enumerate((gx, lax.rem(gx + 1, gx_count), lax.rem(gx - 1 + gx_count, gx_count))):
        mine = (owner * 4 + lax.rem(row8, 4)).astype(F32)
        for k in range(zh_count):
            for j in range(x_count):
                mark = labels[j, k]
                turned = pltpu.roll(mark, 64, 1)
                slot_names = jnp.where(lane8 < 64, mark, turned)
                elements = jnp.where(lane8 < 64, turned, mark)
                found = jnp.full((8, 128), -1.0, F32)
                for t in range(8):
                    hit = jnp.broadcast_to(slot_names[t : t + 1], (8, 128)) == mine
                    element = jnp.broadcast_to(elements[t : t + 1], (8, 128))
                    found = jnp.where(hit, element, found)
                top = k * slots + 4 * j
                named_elements[step, top : top + 4, :] = found[0:4]
    lanes = iota((count, 128), 1)
    element = lanes.astype(F32)
    picking = jnp.where(named_elements[0] == element, 1.0, 0.0)
    picking = jnp.transpose(jnp.concatenate([picking, picking], axis=0))[0:32].astype(BF16)
    picking_2 = jnp.concatenate(
        [
            jnp.where((lanes < 16) & (named_elements[1] == element), 1.0, 0.0),
            jnp.where((lanes >= 16) & (named_elements[2] == element), 1.0, 0.0),
        ],
        axis=0,
    )
    picking_2 = jnp.transpose(picking_2)[0:32].astype(BF16)
    for copy in round_yz:
        copy.wait_recv()
    vort[0, pl.ds(0, 16, stride=16), :] -= hy[2, 0, 0]
    vort[2, pl.ds(0, 16, stride=16), :] += hy[2, 0, 1]
    vort[0, pl.ds(15, 16, stride=16), :] += hy[2, 1, 0]
    vort[2, pl.ds(15, 16, stride=16), :] -= hy[2, 1, 1]
    side_y, side_x = (
        jnp.where(odd, pltpu.roll(hz[2, 0, i], 1, 1), pltpu.roll(hz[2, 1, i], 127, 1))
        for i in range(2)
    )
    side_y = jnp.where(odd, side_y, -side_y)
    side_x = jnp.where(odd, -side_x, side_x)

    def lamb_pair(a, carry):
        sums = [None] * 3
        for x in (2 * a, 2 * a + 1):
            wx = vort[0, slab(x), :] + jnp.where(edge, pltpu.roll(side_y, 127 - 2 * x, 1), 0.0)
            wy = vort[1, slab(x), :] + jnp.where(edge, pltpu.roll(side_x, 127 - 2 * x, 1), 0.0)
            wz = vort[2, slab(x), :]
            vy, vz, vx = (vel[i, slab(x), :] for i in range(3))
            parts = (wy * vz - wz * vy, wz * vx - wx * vz, wx * vy - wy * vx)
            sums = [p if s is None else s + p for s, p in zip(sums, parts)]
        for d in range(3):
            mref[d, slab(a), :] = 0.0625 * sums[d]
        return carry

    lax.fori_loop(1, 7, lamb_pair, 0)
    round_x[0].wait_recv()
    vort[1, 0:16, :] += hx[2, 0, 1]
    vort[2, 0:16, :] -= hx[2, 0, 0]
    lamb_pair(0, 0)
    round_x[1].wait_recv()
    vort[1, 240:256, :] -= hx[2, 1, 1]
    vort[2, 240:256, :] += hx[2, 1, 0]
    lamb_pair(7, 0)
    coarse = [
        mref[d, pl.ds(0, 64, stride=2), :] + mref[d, pl.ds(1, 64, stride=2), :] for d in range(3)
    ]
    fref[0] = jnp.transpose(jnp.concatenate([coarse[0], coarse[1]], axis=0))
    fref[1] = jnp.transpose(jnp.concatenate([coarse[2], coarse[2]], axis=0))
    pieces = [
        [
            fref[i, pl.ds(2 * c, 8, stride=16), :] + fref[i, pl.ds(2 * c + 1, 8, stride=16), :]
            for c in range(8)
        ]
        for i in range(2)
    ]
    left = iota((8, 128), 1) < 64
    rows = [[], [], []]
    for j in range(4):
        a, b = pieces[0][2 * j], pieces[0][2 * j + 1]
        rows[0].append(jnp.where(left, a, pltpu.roll(b, 64, 1)))
        rows[1].append(jnp.where(left, pltpu.roll(a, 64, 1), b))
        rows[2].append(jnp.where(left, pieces[1][2 * j], pieces[1][2 * j + 1]))
    own = jnp.concatenate([jnp.concatenate(r, axis=1) for r in rows], axis=0)
    high, rest = halves(own)
    middle, low = halves(rest)
    loads[4].wait()
    parts = jnp.concatenate([high, middle, low], axis=0).astype(BF16)
    parts = jnp.dot(parts, order[...], preferred_element_type=F32)
    own = parts[0:24] + parts[24:48] + parts[48:72]
    for d in range(3):
        tiles[0, :, 512 * d : 512 * d + 512] = own[8 * d : 8 * d + 8]
    down = {}
    for part in range(PARTS):
        block = slice(part * TILE_LANES // PARTS, (part + 1) * TILE_LANES // PARTS)
        for k in sorted(range(1, zh_count), key=lambda k: -min(k, zh_count - k)):
            i = part * tile_sends + k - 1
            down[part, k] = send(
                tiles.at[0, :, block], tiles.at[k, :, block], tile_send.at[i], tile_recv.at[i],
                at_zh(k),
            )
    across = []
    place = iota((slots, 128), 0)
    peer = zh * x_count + lax.rem(xi + place // 4, x_count)

    def slot_of(step):
        owner = lax.rem(peer + step + gx_count, gx_count)
        return (owner * 4 + lax.rem(place, 4)).astype(F32)

    wanted, wanted_after, wanted_before = slot_of(0), slot_of(1), slot_of(-1)

    def pass_on(part, k):
        marks = labels[0, k]
        named = jnp.where(lane8 < 64, marks, pltpu.roll(marks, 64, 1))
        named = [jnp.broadcast_to(named[t : t + 1], (slots, 128)) for t in range(8)]

        def pick(hits, value):
            chosen = jnp.zeros((slots, 128), F32)
            for t in range(8):
                row = jnp.broadcast_to(value[t : t + 1], (slots, 128))
                chosen = jnp.where(hits[t], row, chosen)
            return chosen

        def keep(chosen, block):
            full[k * slots : k * slots + 4, block] = chosen[0:4]
            for j in range(1, x_count):
                parcel[k, j - 1, :, block] = chosen[4 * j : 4 * j + 4]

        hits = [n == wanted for n in named]
        start, stop = (n * TILE_LANES // PARTS for n in (part, part + 1))
        for first in range(start, stop, 128):
            value = pick(hits, tiles[k, :, first : first + 128])
            keep(value, slice(first + 128, first + 256))
        if part == 0:
            shared = jnp.where(lane8 < 64, tiles[k, :, 0:128], tiles[k, :, 384:512])
            after = pick([n == wanted_after for n in named], shared)
            before = pick([n == wanted_before for n in named], shared)
            keep(jnp.where(iota((slots, 128), 1) < 64, after, before), slice(0, 128))
        block = slice(start + 128 if part else 0, stop + 128)
        for j in sorted(range(1, x_count), key=lambda j: -min(j, x_count - j)):
            i = part * tile_sends + zh_count - 1 + k * (x_count - 1) + j - 1
            copy = send(
                parcel.at[k, j - 1, :, block], arrived.at[k, j - 1, :, block], tile_send.at[i],
                tile_recv.at[i], at_xi(j),
            )
            across.append((k, j, block, copy))

    for part in range(PARTS):
        pass_on(part, 0)
    for part in range(PARTS):
        for k in sorted(range(1, zh_count), key=lambda k: min(k, zh_count - k)):
            down[part, k].wait_recv()
            pass_on(part, k)
    for k, j, block, copy in across:
        copy.wait_recv()
        top = k * slots + 4 * j
        full[top : top + 4, block] = arrived[k, j - 1, :, block]
    def pick_source(d):
        high, low = halves(full[:, 512 * d + 128 : 512 * d + 640])
        parts = jnp.concatenate([high, low], axis=0).astype(BF16)
        both = jnp.dot(picking, parts, preferred_element_type=F32)
        q1[1 + d] = -source_gain * sound_step * both

    pick_source(1)
    pick_source(2)
    faces_2 = []
    for d, (kept, landing, device) in enumerate(((ays, ay, at_y), (azs, az, at_z))):
        for side in (0, 1):
            for j in range(4):
                block = slice(128 * j, 128 * j + 128)
                value = q1[2 + d, :, block] if side else -q1[2 + d, :, block]
                chars[side, 1 + d, j] = value
                if d == 0:
                    top = 12 * side
                    kept[2, side, 0:4, block] = chars[side, 1, j, top : top + 4, :]
                    kept[2, side, 4:8, block] = chars[side, 1, j, top + 16 : top + 20, :]
                else:
                    kept[2, side, :, block] = chars[side, 2, j, pl.ds(3 * side, 8, stride=4), :]
            i = 2 + 2 * d + side
            faces_2.append(
                send(
                    kept.at[2, side], landing.at[2, side], face_send.at[2, i],
                    face_recv.at[2, i], device(2 * side - 1),
                )
            )
    pick_source(0)
    for j in range(4):
        block = slice(128 * j, 128 * j + 128)
        chars[0, 0, j] = -q1[1, :, block]
        chars[1, 0, j] = q1[1, :, block]
    faces = full[:, 0:128]
    high, low = halves(jnp.concatenate([faces, faces], axis=0))
    sides = jnp.dot(picking_2, high.astype(BF16), preferred_element_type=F32)
    sides += jnp.dot(picking_2, low.astype(BF16), preferred_element_type=F32)
    ax[2, 0] = source_gain * sound_step * sides[0:16]
    ax[2, 1] = -source_gain * sound_step * sides[16:32]
    rates(q1, q0, 0.5 * sound_step, lambda c: n0[c] + (q1[c] if c else 0.0), [None, None] + faces_2, 2, False)
    for i in range(32):
        c, part = i // 8, i % 8
        sound_out[i] = q0[c, 4 * part : 4 * part + 4, :]
    for copy in pending:
        copy.wait_send()
    for store in stores:
        store.wait()


def hand_over(*refs):
    copies = [pltpu.make_async_copy(refs[i], refs[4 + i], refs[8].at[i]) for i in range(4)]
    for copy in copies:
        copy.start()
    for copy in copies:
        copy.wait()


def solution(mesh):
    gx_count, gy_count, gz_count = (mesh.shape[a] for a in ("gx", "gy", "gz"))
    x_count = 4 if gx_count == 16 else 2
    zh_count = gx_count // x_count
    tile_sends = (zh_count - 1) + zh_count * (x_count - 1)
    label_sends = zh_count + x_count - 2
    consts = tables()

    def on_device(density, momentum, energy, acoustic, tile_slot, tile_element):
        anywhere = pl.BlockSpec(memory_space=pl.ANY)
        in_hbm = pl.BlockSpec(memory_space=pltpu.HBM)
        scalars = pl.BlockSpec(memory_space=pltpu.SMEM)
        out_shape = (
            jax.ShapeDtypeStruct((256, 128), F32),
            jax.ShapeDtypeStruct((3, 256, 128), F32),
            jax.ShapeDtypeStruct((256, 128), F32),
            jax.ShapeDtypeStruct((32, 4, 512), F32),
        )
        vmem = pltpu.VMEM
        scratch = [
            vmem((5, 256, 128), F32), vmem((5, 256, 128), F32), vmem((5, 256, 128), F32),
            vmem((3, 256, 128), F32), vmem((3, 256, 128), F32), vmem((3, 128, 128), F32),
            vmem((2, 128, 128), F32), vmem((zh_count, 8, TILE_LANES), F32),
            vmem((zh_count, x_count - 1, 4, PARCEL_LANES), F32),
            vmem((zh_count, x_count - 1, 4, PARCEL_LANES), F32),
            vmem((4 * gx_count, PARCEL_LANES), F32),
            vmem((x_count, zh_count, 8, 128), F32), vmem((3, 4 * gx_count, 128), F32),
            vmem((3, 2, 5, 16, 128), F32), vmem((3, 2, 5, 16, 128), F32),
            vmem((3, 2, 5, 16, 128), F32), vmem((3, 2, 5, 16, 128), F32),
            vmem((3, 5, 16, 128), F32),
            vmem((3, 2, 16, 128), F32), vmem((3, 2, 8, 512), F32), vmem((3, 2, 8, 512), F32),
            vmem((2, 2, 16, 128), F32), vmem((3, 2, 8, 512), F32), vmem((3, 2, 8, 512), F32),
            vmem((32, 4, 512), F32), vmem((4, 32, 512), F32), vmem((4, 32, 512), F32),
            vmem((4, 32, 512), F32), vmem((2, 3, 4, 32, 128), F32), vmem((2, 2, 4, 32, 128), F32),
            vmem((512, 512), BF16), vmem((512, 512), BF16), vmem((256, 256), BF16),
            vmem((256, 256), BF16), vmem((256, 256), BF16), vmem((256, 256), BF16),
            vmem((512, 512), BF16),
            pltpu.SemaphoreType.DMA((11,)), pltpu.SemaphoreType.DMA((3,)),
            pltpu.SemaphoreType.DMA((3, 6)), pltpu.SemaphoreType.DMA((3, 6)),
            pltpu.SemaphoreType.DMA((3, 6)), pltpu.SemaphoreType.DMA((3, 6)),
            pltpu.SemaphoreType.DMA((PARTS * tile_sends,)),
            pltpu.SemaphoreType.DMA((PARTS * tile_sends,)),
            pltpu.SemaphoreType.DMA((label_sends,)), pltpu.SemaphoreType.DMA((label_sends,)),
        ]
        held_shape = tuple(pltpu.VMEM(o.shape, F32) for o in out_shape)
        outs = pl.pallas_call(
            functools.partial(kernel, zh_count, x_count, gy_count, gz_count),
            out_shape=held_shape,
            in_specs=[anywhere] * 4 + [scalars] * 2 + [anywhere] * 7,
            out_specs=[anywhere] * 3 + [pl.BlockSpec(memory_space=pltpu.VMEM)],
            scratch_shapes=scratch,
            compiler_params=pltpu.CompilerParams(
                collective_id=0, has_side_effects=True, vmem_limit_bytes=57 * 2**20
            ),
            cost_estimate=pl.CostEstimate(
                flops=10**9, bytes_accessed=4 * 2**20, transcendentals=0
            ),
        )(
            density.reshape(256, 128), momentum.reshape(3, 256, 128), energy.reshape(256, 128),
            acoustic.reshape(32, 4, 512), tile_slot, tile_element,
            *[jnp.asarray(c) for c in consts],
        )
        outs = pl.pallas_call(
            hand_over,
            out_shape=out_shape,
            in_specs=[anywhere] * 4,
            out_specs=[in_hbm] * 4,
            scratch_shapes=[pltpu.SemaphoreType.DMA((4,))],
            compiler_params=pltpu.CompilerParams(vmem_limit_bytes=8 * 2**20),
        )(*outs)
        return (
            outs[0].reshape(16, 16, 128), outs[1].reshape(3, 16, 16, 128),
            outs[2].reshape(16, 16, 128), outs[3].reshape(4, 2, 4, 4, 512),
        )

    in_specs = (
        P("gx", "gy", "gz"), P(None, "gx", "gy", "gz"), P("gx", "gy", "gz"),
        P(None, "gx", "gy", "gz", None), P("gx", "gy", "gz", None), P("gx", "gy", "gz", None),
    )
    out_specs = (
        P("gx", "gy", "gz"), P(None, "gx", "gy", "gz"), P("gx", "gy", "gz"),
        P(None, "gx", "gy", "gz", None),
    )
    return jax.shard_map(
        on_device, mesh=mesh, in_specs=in_specs, out_specs=out_specs, check_vma=False
    )
```

```python
import functools

import jax
import jax.numpy as jnp
import ml_dtypes
import numpy as np
from jax import lax
from jax.experimental import pallas as pl
from jax.experimental.pallas import tpu as pltpu
from jax.sharding import PartitionSpec as P

MESH = pl.DeviceIdType.MESH
F32 = jnp.float32
BF16 = jnp.bfloat16

flow_step = 0.05
viscosity = 0.2
sound_step = 0.02
lift_factor = 28.0
source_gain = 40.0
TILE_LANES = 1536
PARCEL_LANES = 1664
PARTS = 2


def derivative_numbers():
    order = 7
    points = np.array(
        [
            -1.0,
            -0.8717401485096066,
            -0.5917001814331423,
            -0.2092992179024789,
            0.2092992179024789,
            0.5917001814331423,
            0.8717401485096066,
            1.0,
        ]
    )
    previous = np.ones(8)
    current = points * 1.0
    for degree in range(1, order):
        following = ((2 * degree + 1) * points * current - degree * previous) / (degree + 1)
        previous = current
        current = following
    table = np.zeros((8, 8))
    for row in range(8):
        for column in range(8):
            if row != column:
                table[row, column] = current[row] / (
                    current[column] * (points[row] - points[column])
                )
    table[0, 0] = -order * (order + 1) / 4.0
    table[order, order] = order * (order + 1) / 4.0
    return table


def split_table(table):
    table = table.astype(np.float32)
    high = table.astype(ml_dtypes.bfloat16)
    low = (table - high.astype(np.float32)).astype(ml_dtypes.bfloat16)
    return high, low


def tables():
    table = derivative_numbers()
    eye = np.eye(8)
    along_x = np.kron(np.kron(table, eye), eye).T
    along_y = np.kron(np.kron(np.eye(4), table), eye).T
    along_z = np.kron(np.kron(np.eye(4), eye), table).T
    order = np.zeros((512, 512), ml_dtypes.bfloat16)
    for c in range(8):
        for ab in range(64):
            order[c * 64 + ab, ab * 8 + c] = 1.0
    return (*split_table(along_x), *split_table(along_y), *split_table(along_z), order)


def iota(shape, dim):
    return lax.broadcasted_iota(jnp.int32, shape, dim)


def fluxes(state):
    rho, mx, my, mz, energy = state
    inverse = 1.0 / rho
    vx, vy, vz = mx * inverse, my * inverse, mz * inverse
    pressure = 0.4 * (energy - 0.5 * (mx * vx + my * vy + mz * vz))
    total = energy + pressure
    xy, xz, yz = mx * vy, mx * vz, my * vz
    return (
        [mx, mx * vx + pressure, xy, xz, total * vx],
        [my, xy, my * vy + pressure, yz, total * vy],
        [mz, xz, yz, mz * vz + pressure, total * vz],
    )


def halves(value):
    high = value.astype(BF16).astype(F32)
    return high, value - high


def kernel(
    zh_count, x_count, gy_count, gz_count,
    rho_hbm, mom_hbm, energy_hbm, sound_hbm, slot_ref, element_ref,
    dxh_hbm, dxl_hbm, dyh_hbm, dyl_hbm, dzh_hbm, dzl_hbm, order_hbm,
    rho_out, mom_out, energy_out, sound_out,
    s0, s1, s2, vel, vort, mref, fref, tiles, parcel, arrived, full, labels, named_elements,
    hx, hy, hz, sy, sz, ax, ay, az, axs, ays, azs,
    stage, q0, q1, n0, chars, near,
    dxh, dxl, dyh, dyl, dzh, dzl, order,
    in_sem, out_sem, flow_send, flow_recv, face_send, face_recv, tile_send, tile_recv,
    label_send, label_recv,
):
    gx, gy, gz = lax.axis_index("gx"), lax.axis_index("gy"), lax.axis_index("gz")
    gx_count = zh_count * x_count
    tile_sends = (zh_count - 1) + zh_count * (x_count - 1)
    zh, xi = gx // x_count, lax.rem(gx, x_count)

    def at_x(step):
        return (lax.rem(gx + step + gx_count, gx_count), gy, gz)

    def at_y(step):
        return (gx, lax.rem(gy + step + gy_count, gy_count), gz)

    def at_z(step):
        return (gx, gy, lax.rem(gz + step + gz_count, gz_count))

    def at_zh(step):
        return (lax.rem(zh + step, zh_count) * x_count + xi, gy, gz)

    def at_xi(step):
        return (zh * x_count + lax.rem(xi + step, x_count), gy, gz)

    barrier = pltpu.get_barrier_semaphore()
    partners = [at_x(-1), at_x(1), at_y(-1), at_y(1), at_z(-1), at_z(1)]
    partners += [at_zh(k) for k in range(1, zh_count)] + [at_xi(j) for j in range(1, x_count)]
    for partner in partners:
        pl.semaphore_signal(barrier, inc=1, device_id=partner, device_id_type=MESH)

    loads = [
        (rho_hbm, s0.at[0]), (mom_hbm, s0.at[1:4]), (energy_hbm, s0.at[4]), (sound_hbm, stage),
        (order_hbm, order), (dxh_hbm, dxh), (dxl_hbm, dxl), (dyh_hbm, dyh), (dyl_hbm, dyl),
        (dzh_hbm, dzh), (dzl_hbm, dzl),
    ]
    loads = [pltpu.make_async_copy(a, b, in_sem.at[i]) for i, (a, b) in enumerate(loads)]
    for load in loads:
        load.start()

    lane = iota((16, 128), 1)
    row = iota((16, 128), 0)
    odd = lax.rem(lane, 2) == 1
    edge = (lane == 0) | (lane == 127)
    pair = lane // 2

    pending = []

    def send(src, dst, send_sem, recv_sem, device):
        copy = pltpu.make_async_remote_copy(
            src_ref=src, dst_ref=dst, send_sem=send_sem, recv_sem=recv_sem,
            device_id=device, device_id_type=MESH,
        )
        copy.start()
        pending.append(copy)
        return copy

    def flow_go(turn, i, src, dst, device):
        return send(src, dst, flow_send.at[turn, i], flow_recv.at[turn, i], device)

    def sends_x(turn, x_source, comps):
        return [
            flow_go(turn, 0, x_source(240), hx.at[turn, 0, comps], at_x(1)),
            flow_go(turn, 1, x_source(0), hx.at[turn, 1, comps], at_x(-1)),
        ]

    def sends_yz(turn, comps):
        return [
            flow_go(turn, 2, sz.at[turn, comps], hz.at[turn, 0, comps], at_z(1)),
            flow_go(turn, 3, sz.at[turn, comps], hz.at[turn, 1, comps], at_z(-1)),
            flow_go(turn, 4, sy.at[turn, 0, comps], hy.at[turn, 0, comps], at_y(1)),
            flow_go(turn, 5, sy.at[turn, 1, comps], hy.at[turn, 1, comps], at_y(-1)),
        ]

    def slab(x):
        return pl.ds(pl.multiple_of(x * 16, 16), 16)

    def pack_lanes(packed, values, x):
        here = pair == x
        return [jnp.where(here, pltpu.roll(v, 2 * x + 1, 1), p) for p, v in zip(packed, values)]

    def pack_rows(turn, ref, comps):
        for c in comps:
            sy[turn, 0, c] = ref[c, pl.ds(15, 16, stride=16), :]
            sy[turn, 1, c] = ref[c, pl.ds(0, 16, stride=16), :]

    for load in loads[:3]:
        load.wait()
    pack_rows(0, s0, range(5))

    def pack_first(x, packed):
        return pack_lanes(packed, [s0[c, slab(x), :] for c in range(5)], x)

    first_slab = [s0[c, 0:16, :] for c in range(5)]
    for c, value in enumerate(lax.fori_loop(0, 16, pack_first, first_slab)):
        sz[0, c] = value
    pl.semaphore_wait(barrier, len(partners))
    every = pl.ds(0, 5)
    round_x = sends_x(0, lambda r: s0.at[:, r : r + 16, :], every)
    round_yz = sends_yz(0, every)

    row8, lane8 = iota((8, 128), 0), iota((8, 128), 1)
    label = jnp.zeros((8, 128), jnp.int32)
    for t in range(8):
        both = jnp.where(lane8 < 64, slot_ref[0, 0, 0, t], element_ref[0, 0, 0, t])
        label = jnp.where(row8 == t, both, label)
    labels[0, 0] = label.astype(F32)
    labels_down = [
        send(labels.at[0, 0], labels.at[0, k], label_send.at[k - 1], label_recv.at[k - 1], at_zh(k))
        for k in range(1, zh_count)
    ]

    def face_sends(turn, q):
        for d in range(3):
            for j in range(4):
                block = slice(128 * j, 128 * j + 128)
                chars[0, d, j] = q[0, :, block] - q[1 + d, :, block]
                chars[1, d, j] = q[0, :, block] + q[1 + d, :, block]
        axs[turn, 0] = chars[0, 0, 0, 0:16, :]
        axs[turn, 1] = chars[1, 0, 3, 16:32, :]
        for side, top in ((0, 0), (1, 12)):
            for j in range(4):
                block = slice(128 * j, 128 * j + 128)
                ays[turn, side, 0:4, block] = chars[side, 1, j, top : top + 4, :]
                ays[turn, side, 4:8, block] = chars[side, 1, j, top + 16 : top + 20, :]
                azs[turn, side, :, block] = chars[side, 2, j, pl.ds(3 * side, 8, stride=4), :]

        def go(i, src, dst, device):
            return send(src, dst, face_send.at[turn, i], face_recv.at[turn, i], device)

        along_x = [
            go(0, axs.at[turn, 0], ax.at[turn, 0], at_x(-1)),
            go(1, axs.at[turn, 1], ax.at[turn, 1], at_x(1)),
        ]
        return along_x + [
            go(2, ays.at[turn, 0], ay.at[turn, 0], at_y(-1)),
            go(3, ays.at[turn, 1], ay.at[turn, 1], at_y(1)),
            go(4, azs.at[turn, 0], az.at[turn, 0], at_z(-1)),
            go(5, azs.at[turn, 1], az.at[turn, 1], at_z(1)),
        ]

    def apply3(value, high, low):
        rows = value.shape[0]
        top, rest = halves(value)
        both = jnp.concatenate([top, rest], axis=0).astype(BF16)
        part = jnp.dot(both, high, preferred_element_type=F32)
        return (
            part[:rows] + part[rows:]
            + jnp.dot(top.astype(BF16), low, preferred_element_type=F32)
        )

    def derivative(d, value):
        if d == 0:
            return apply3(value, dxh[...], dxl[...])
        high, low = (dyh, dyl) if d == 1 else (dzh, dzl)
        split = [apply3(value[:, s : s + 256], high[...], low[...]) for s in (0, 256)]
        return jnp.concatenate(split, axis=1)

    lane32 = iota((32, 128), 1)

    def rates(q, out, gain, base, copies, turn, with_pressure):
        total = None
        for d in range(3):
            if with_pressure:
                both = derivative(d, jnp.concatenate([q[0], q[1 + d]], axis=0))
                out[1 + d] = base(1 + d) - gain * both[:32]
                both = both[32:]
            else:
                both = derivative(d, q[1 + d])
                out[1 + d] = base(1 + d)
            total = both if total is None else total + both
        out[0] = base(0) - gain * total
        k = 0.5 * lift_factor * gain

        def lift_x():
            other = jnp.concatenate([chars[0, 0, 0, 16:32, :], ax[turn, 0]], axis=0)
            jump = pltpu.roll(other, 64, 1) - chars[0, 0, 3]
            jump = jnp.where(lane32 >= 64, k * jump, 0.0)
            out[0, :, 384:512] += jump
            out[1, :, 384:512] -= jump
            other = jnp.concatenate([ax[turn, 1], chars[1, 0, 3, 0:16, :]], axis=0)
            jump = chars[1, 0, 0] - pltpu.roll(other, 64, 1)
            jump = jnp.where(lane32 < 64, k * jump, 0.0)
            out[0, :, 0:128] -= jump
            out[1, :, 0:128] -= jump

        if not copies[0]:
            lift_x()
        for side, d, move in ((0, 1, 28), (1, 1, 4), (0, 2, 31), (1, 2, 1)):
            for j in range(4):
                near[side, d - 1, j] = pltpu.roll(chars[side, d, j], move, 0)
        for copy in copies[2:6]:
            copy.wait_recv()
        for side, top in ((0, 12), (1, 0)):
            for j in range(4):
                block = slice(128 * j, 128 * j + 128)
                near[side, 0, j, top : top + 4, :] = ay[turn, side, 0:4, block]
                near[side, 0, j, top + 16 : top + 20, :] = ay[turn, side, 4:8, block]
                near[side, 1, j, pl.ds(3 - 3 * side, 8, stride=4), :] = az[turn, side, :, block]
        for d, period, move in ((1, 64, 56), (2, 8, 7)):
            place = lax.rem(lane32, period)
            span = period - move
            for j in range(4):
                block = slice(128 * j, 128 * j + 128)
                high = pltpu.roll(near[0, d - 1, j], move, 1) - chars[0, d, j]
                high = jnp.where(place >= move, k * high, 0.0)
                low = chars[1, d, j] - pltpu.roll(near[1, d - 1, j], 128 - move, 1)
                low = jnp.where(place < span, k * low, 0.0)
                out[0, :, block] += high - low
                out[1 + d, :, block] -= high + low
        if copies[0]:
            for copy in copies[0:2]:
                copy.wait_recv()
            lift_x()

    loads[3].wait()
    for i in range(32):
        c, part = i // 8, i % 8
        q0[c, 4 * part : 4 * part + 4, :] = stage[i]
    faces_0 = face_sends(0, q0)

    def interior(source, target, gain, base):
        half, visc = 0.5 * gain, viscosity * gain

        def update(x, before, first):
            state = [source[c, slab(x), :] for c in range(5)]
            along_x, along_y, along_z = fluxes(state)
            sums, later = [], []
            for c in range(5):
                soft = visc * state[c]
                acc = base(c, x, state[c]) - 6.0 * soft
                part = half * along_z[c]
                acc += pltpu.roll(jnp.where(lane == 0, 0.0, soft - part), 127, 1)
                acc += pltpu.roll(jnp.where(lane == 127, 0.0, soft + part), 1, 1)
                part = half * along_y[c]
                acc += pltpu.roll(jnp.where(row == 0, 0.0, soft - part), 15, 0)
                acc += pltpu.roll(jnp.where(row == 15, 0.0, soft + part), 1, 0)
                part = half * along_x[c]
                if not first:
                    target[c, slab(x - 1), :] = before[c] + (soft - part)
                    acc += before[5 + c]
                sums.append(acc)
                later.append(soft + part)
            return sums + later

        carry = update(0, None, True)
        carry = lax.fori_loop(1, 16, lambda x, b: update(x, b, False), carry)
        for c in range(5):
            target[c, 240:256, :] = carry[c]

    def boundary_yz(turn, target, gain, copies):
        half, visc = 0.5 * gain, viscosity * gain
        for copy in copies:
            copy.wait_recv()
        lower, upper = [hy[turn, 0, c] for c in range(5)], [hy[turn, 1, c] for c in range(5)]
        low_flux, up_flux = fluxes(lower)[1], fluxes(upper)[1]
        for c in range(5):
            target[c, pl.ds(0, 16, stride=16), :] += visc * lower[c] + half * low_flux[c]
            target[c, pl.ds(15, 16, stride=16), :] += visc * upper[c] - half * up_flux[c]
        both = [
            jnp.where(odd, pltpu.roll(hz[turn, 0, c], 1, 1), pltpu.roll(hz[turn, 1, c], 127, 1))
            for c in range(5)
        ]
        flux = fluxes(both)[2]
        return [
            visc * both[c] + jnp.where(odd, half * flux[c], -half * flux[c]) for c in range(5)
        ]

    def boundary_x(turn, target, gain, copies):
        half, visc = 0.5 * gain, viscosity * gain
        outer = []
        for side, rows, copy in ((0, slice(0, 16), copies[0]), (1, slice(240, 256), copies[1])):
            copy.wait_recv()
            state = [hx[turn, side, c] for c in range(5)]
            flux = fluxes(state)[0]
            values = []
            for c in range(5):
                term = half * flux[c] if side == 0 else -half * flux[c]
                value = target[c, rows, :] + (visc * state[c] + term)
                target[c, rows, :] = value
                values.append(value)
            outer.append(values)
        return outer

    def add_edges(target, terms, x):
        values = []
        for c in range(5):
            moved = pltpu.roll(terms[c], 127 - 2 * x, 1)
            value = target[c, slab(x), :] + jnp.where(edge, moved, 0.0)
            target[c, slab(x), :] = value
            values.append(value)
        return values

    interior(s0, s1, flow_step, lambda c, x, u: u)
    terms = boundary_yz(0, s1, flow_step, round_yz)
    packed = [s1[c, 16:32, :] for c in range(5)]
    packed = lax.fori_loop(1, 15, lambda x, p: pack_lanes(p, add_edges(s1, terms, x), x), packed)
    for x in (0, 15):
        add_edges(s1, terms, x)
    outer = boundary_x(0, s1, flow_step, round_x)
    round_x = sends_x(1, lambda r: s1.at[:, r : r + 16, :], every)
    packed = pack_lanes(pack_lanes(packed, outer[0], 0), outer[1], 15)
    for c in range(5):
        sz[1, c] = packed[c]
    pack_rows(1, s1, range(5))
    round_yz = sends_yz(1, every)

    interior(s1, s2, 0.5 * flow_step, lambda c, x, u: 0.5 * (s0[c, slab(x), :] + u))
    for load in loads[5:]:
        load.wait()
    rates(q0, q1, sound_step, lambda c: q0[c], faces_0, 0, True)
    faces_1 = face_sends(1, q1)
    for copy in labels_down:
        copy.wait_recv()
    labels_across = [
        send(labels.at[0], labels.at[j], label_send.at[i], label_recv.at[i], at_xi(j))
        for j, i in zip(range(1, x_count), range(zh_count - 1, zh_count + x_count - 2))
    ]
    terms_2 = boundary_yz(1, s2, 0.5 * flow_step, round_yz)

    def velocity(x, values):
        inverse = 1.0 / values[0]
        vx, vy, vz = (values[d] * inverse for d in (1, 2, 3))
        vel[0, slab(x), :], vel[1, slab(x), :], vel[2, slab(x), :] = vy, vz, vx
        return [vy, vx]

    zero = jnp.zeros((16, 128), F32)
    packed = lax.fori_loop(
        1, 15, lambda x, p: pack_lanes(p, velocity(x, add_edges(s2, terms_2, x)), x), [zero, zero]
    )
    for x in (0, 15):
        add_edges(s2, terms_2, x)
    outer = boundary_x(1, s2, 0.5 * flow_step, round_x)
    outer = [velocity(0, outer[0]), velocity(15, outer[1])]
    round_x = sends_x(2, lambda r: vel.at[0:2, r : r + 16, :], pl.ds(0, 2))
    sz[2, 0], sz[2, 1] = pack_lanes(pack_lanes(packed, outer[0], 0), outer[1], 15)
    for i, comp in enumerate((1, 2)):
        sy[2, 0, i] = vel[comp, pl.ds(15, 16, stride=16), :]
        sy[2, 1, i] = vel[comp, pl.ds(0, 16, stride=16), :]
    round_yz = sends_yz(2, pl.ds(0, 2))

    stores = [
        pltpu.make_async_copy(s2.at[0], rho_out, out_sem.at[0]),
        pltpu.make_async_copy(s2.at[1:4], mom_out, out_sem.at[1]),
        pltpu.make_async_copy(s2.at[4], energy_out, out_sem.at[2]),
    ]
    for store in stores:
        store.start()

    def dy(f):
        up = pltpu.roll(jnp.where(row == 0, 0.0, f), 15, 0)
        return up - pltpu.roll(jnp.where(row == 15, 0.0, f), 1, 0)

    def dz(f):
        up = pltpu.roll(jnp.where(lane == 0, 0.0, f), 127, 1)
        return up - pltpu.roll(jnp.where(lane == 127, 0.0, f), 1, 1)

    def curl(x, carry):
        vy, vz, vx = (vel[i, slab(x), :] for i in range(3))
        after = slab(jnp.minimum(x + 1, 15))
        before = slab(jnp.maximum(x - 1, 0))
        dx_vy, dx_vz = (
            jnp.where(x < 15, vel[i, after, :], 0.0) - jnp.where(x > 0, vel[i, before, :], 0.0)
            for i in range(2)
        )
        vort[0, slab(x), :] = dy(vz) - dz(vy)
        vort[1, slab(x), :] = dz(vx) - dx_vz
        vort[2, slab(x), :] = dx_vy - dy(vx)
        return carry

    lax.fori_loop(0, 16, curl, 0)

    slots = 4 * x_count
    count = zh_count * slots
    for copy in labels_across:
        copy.wait_recv()
    for step, owner in enumerate((gx, lax.rem(gx + 1, gx_count), lax.rem(gx - 1 + gx_count, gx_count))):
        mine = (owner * 4 + lax.rem(row8, 4)).astype(F32)
        for k in range(zh_count):
            for j in range(x_count):
                mark = labels[j, k]
                turned = pltpu.roll(mark, 64, 1)
                slot_names = jnp.where(lane8 < 64, mark, turned)
                elements = jnp.where(lane8 < 64, turned, mark)
                found = jnp.full((8, 128), -1.0, F32)
                for t in range(8):
                    hit = jnp.broadcast_to(slot_names[t : t + 1], (8, 128)) == mine
                    element = jnp.broadcast_to(elements[t : t + 1], (8, 128))
                    found = jnp.where(hit, element, found)
                top = k * slots + 4 * j
                named_elements[step, top : top + 4, :] = found[0:4]
    lanes = iota((count, 128), 1)
    element = lanes.astype(F32)
    picking = jnp.where(named_elements[0] == element, 1.0, 0.0)
    picking = jnp.transpose(jnp.concatenate([picking, picking], axis=0))[0:32].astype(BF16)
    picking_2 = jnp.concatenate(
        [
            jnp.where((lanes < 16) & (named_elements[1] == element), 1.0, 0.0),
            jnp.where((lanes >= 16) & (named_elements[2] == element), 1.0, 0.0),
        ],
        axis=0,
    )
    picking_2 = jnp.transpose(picking_2)[0:32].astype(BF16)
    for copy in round_yz:
        copy.wait_recv()
    vort[0, pl.ds(0, 16, stride=16), :] -= hy[2, 0, 0]
    vort[2, pl.ds(0, 16, stride=16), :] += hy[2, 0, 1]
    vort[0, pl.ds(15, 16, stride=16), :] += hy[2, 1, 0]
    vort[2, pl.ds(15, 16, stride=16), :] -= hy[2, 1, 1]
    side_y, side_x = (
        jnp.where(odd, pltpu.roll(hz[2, 0, i], 1, 1), pltpu.roll(hz[2, 1, i], 127, 1))
        for i in range(2)
    )
    side_y = jnp.where(odd, side_y, -side_y)
    side_x = jnp.where(odd, -side_x, side_x)

    def lamb_pair(a, carry):
        sums = [None] * 3
        for x in (2 * a, 2 * a + 1):
            wx = vort[0, slab(x), :] + jnp.where(edge, pltpu.roll(side_y, 127 - 2 * x, 1), 0.0)
            wy = vort[1, slab(x), :] + jnp.where(edge, pltpu.roll(side_x, 127 - 2 * x, 1), 0.0)
            wz = vort[2, slab(x), :]
            vy, vz, vx = (vel[i, slab(x), :] for i in range(3))
            parts = (wy * vz - wz * vy, wz * vx - wx * vz, wx * vy - wy * vx)
            sums = [p if s is None else s + p for s, p in zip(sums, parts)]
        for d in range(3):
            mref[d, slab(a), :] = 0.0625 * sums[d]
        return carry

    lax.fori_loop(1, 7, lamb_pair, 0)
    round_x[0].wait_recv()
    vort[1, 0:16, :] += hx[2, 0, 1]
    vort[2, 0:16, :] -= hx[2, 0, 0]
    lamb_pair(0, 0)
    round_x[1].wait_recv()
    vort[1, 240:256, :] -= hx[2, 1, 1]
    vort[2, 240:256, :] += hx[2, 1, 0]
    lamb_pair(7, 0)
    coarse = [
        mref[d, pl.ds(0, 64, stride=2), :] + mref[d, pl.ds(1, 64, stride=2), :] for d in range(3)
    ]
    fref[0] = jnp.transpose(jnp.concatenate([coarse[0], coarse[1]], axis=0))
    fref[1] = jnp.transpose(jnp.concatenate([coarse[2], coarse[2]], axis=0))
    pieces = [
        [
            fref[i, pl.ds(2 * c, 8, stride=16), :] + fref[i, pl.ds(2 * c + 1, 8, stride=16), :]
            for c in range(8)
        ]
        for i in range(2)
    ]
    left = iota((8, 128), 1) < 64
    rows = [[], [], []]
    for j in range(4):
        a, b = pieces[0][2 * j], pieces[0][2 * j + 1]
        rows[0].append(jnp.where(left, a, pltpu.roll(b, 64, 1)))
        rows[1].append(jnp.where(left, pltpu.roll(a, 64, 1), b))
        rows[2].append(jnp.where(left, pieces[1][2 * j], pieces[1][2 * j + 1]))
    own = jnp.concatenate([jnp.concatenate(r, axis=1) for r in rows], axis=0)
    high, rest = halves(own)
    middle, low = halves(rest)
    loads[4].wait()
    parts = jnp.concatenate([high, middle, low], axis=0).astype(BF16)
    parts = jnp.dot(parts, order[...], preferred_element_type=F32)
    own = parts[0:24] + parts[24:48] + parts[48:72]
    for d in range(3):
        tiles[0, :, 512 * d : 512 * d + 512] = own[8 * d : 8 * d + 8]
    down = {}
    for part in range(PARTS):
        block = slice(part * TILE_LANES // PARTS, (part + 1) * TILE_LANES // PARTS)
        for k in sorted(range(1, zh_count), key=lambda k: -min(k, zh_count - k)):
            i = part * tile_sends + k - 1
            down[part, k] = send(
                tiles.at[0, :, block], tiles.at[k, :, block], tile_send.at[i], tile_recv.at[i],
                at_zh(k),
            )
    across = []
    place = iota((slots, 128), 0)
    peer = zh * x_count + lax.rem(xi + place // 4, x_count)

    def slot_of(step):
        owner = lax.rem(peer + step + gx_count, gx_count)
        return (owner * 4 + lax.rem(place, 4)).astype(F32)

    wanted, wanted_after, wanted_before = slot_of(0), slot_of(1), slot_of(-1)

    def pass_on(part, k):
        marks = labels[0, k]
        named = jnp.where(lane8 < 64, marks, pltpu.roll(marks, 64, 1))
        named = [jnp.broadcast_to(named[t : t + 1], (slots, 128)) for t in range(8)]

        def pick(hits, value):
            chosen = jnp.zeros((slots, 128), F32)
            for t in range(8):
                row = jnp.broadcast_to(value[t : t + 1], (slots, 128))
                chosen = jnp.where(hits[t], row, chosen)
            return chosen

        def keep(chosen, block):
            full[k * slots : k * slots + 4, block] = chosen[0:4]
            for j in range(1, x_count):
                parcel[k, j - 1, :, block] = chosen[4 * j : 4 * j + 4]

        hits = [n == wanted for n in named]
        start, stop = (n * TILE_LANES // PARTS for n in (part, part + 1))
        for first in range(start, stop, 128):
            value = pick(hits, tiles[k, :, first : first + 128])
            keep(value, slice(first + 128, first + 256))
        if part == 0:
            shared = jnp.where(lane8 < 64, tiles[k, :, 0:128], tiles[k, :, 384:512])
            after = pick([n == wanted_after for n in named], shared)
            before = pick([n == wanted_before for n in named], shared)
            keep(jnp.where(iota((slots, 128), 1) < 64, after, before), slice(0, 128))
        block = slice(start + 128 if part else 0, stop + 128)
        for j in sorted(range(1, x_count), key=lambda j: -min(j, x_count - j)):
            i = part * tile_sends + zh_count - 1 + k * (x_count - 1) + j - 1
            copy = send(
                parcel.at[k, j - 1, :, block], arrived.at[k, j - 1, :, block], tile_send.at[i],
                tile_recv.at[i], at_xi(j),
            )
            across.append((k, j, block, copy))

    for part in range(PARTS):
        pass_on(part, 0)
    for part in range(PARTS):
        for k in sorted(range(1, zh_count), key=lambda k: min(k, zh_count - k)):
            down[part, k].wait_recv()
            pass_on(part, k)
    rates(q1, n0, 0.5 * sound_step, lambda c: 0.5 * (q0[c] + q1[c]), faces_1, 1, True)
    for k, j, block, copy in across:
        copy.wait_recv()
        top = k * slots + 4 * j
        full[top : top + 4, block] = arrived[k, j - 1, :, block]
    def pick_source(d):
        high, low = halves(full[:, 512 * d + 128 : 512 * d + 640])
        parts = jnp.concatenate([high, low], axis=0).astype(BF16)
        both = jnp.dot(picking, parts, preferred_element_type=F32)
        q1[1 + d] = -source_gain * sound_step * both

    pick_source(1)
    pick_source(2)
    faces_2 = []
    for d, (kept, landing, device) in enumerate(((ays, ay, at_y), (azs, az, at_z))):
        for side in (0, 1):
            for j in range(4):
                block = slice(128 * j, 128 * j + 128)
                value = q1[2 + d, :, block] if side else -q1[2 + d, :, block]
                chars[side, 1 + d, j] = value
                if d == 0:
                    top = 12 * side
                    kept[2, side, 0:4, block] = chars[side, 1, j, top : top + 4, :]
                    kept[2, side, 4:8, block] = chars[side, 1, j, top + 16 : top + 20, :]
                else:
                    kept[2, side, :, block] = chars[side, 2, j, pl.ds(3 * side, 8, stride=4), :]
            i = 2 + 2 * d + side
            faces_2.append(
                send(
                    kept.at[2, side], landing.at[2, side], face_send.at[2, i],
                    face_recv.at[2, i], device(2 * side - 1),
                )
            )
    pick_source(0)
    for j in range(4):
        block = slice(128 * j, 128 * j + 128)
        chars[0, 0, j] = -q1[1, :, block]
        chars[1, 0, j] = q1[1, :, block]
    faces = full[:, 0:128]
    high, low = halves(jnp.concatenate([faces, faces], axis=0))
    sides = jnp.dot(picking_2, high.astype(BF16), preferred_element_type=F32)
    sides += jnp.dot(picking_2, low.astype(BF16), preferred_element_type=F32)
    ax[2, 0] = source_gain * sound_step * sides[0:16]
    ax[2, 1] = -source_gain * sound_step * sides[16:32]
    rates(q1, q0, 0.5 * sound_step, lambda c: n0[c] + (q1[c] if c else 0.0), [None, None] + faces_2, 2, False)
    for i in range(32):
        c, part = i // 8, i % 8
        sound_out[i] = q0[c, 4 * part : 4 * part + 4, :]
    for copy in pending:
        copy.wait_send()
    for store in stores:
        store.wait()


def hand_over(*refs):
    copies = [pltpu.make_async_copy(refs[i], refs[4 + i], refs[8].at[i]) for i in range(4)]
    for copy in copies:
        copy.start()
    for copy in copies:
        copy.wait()


def solution(mesh):
    gx_count, gy_count, gz_count = (mesh.shape[a] for a in ("gx", "gy", "gz"))
    x_count = 4 if gx_count == 16 else 2
    zh_count = gx_count // x_count
    tile_sends = (zh_count - 1) + zh_count * (x_count - 1)
    label_sends = zh_count + x_count - 2
    consts = tables()

    def on_device(density, momentum, energy, acoustic, tile_slot, tile_element):
        anywhere = pl.BlockSpec(memory_space=pl.ANY)
        in_hbm = pl.BlockSpec(memory_space=pltpu.HBM)
        scalars = pl.BlockSpec(memory_space=pltpu.SMEM)
        out_shape = (
            jax.ShapeDtypeStruct((256, 128), F32),
            jax.ShapeDtypeStruct((3, 256, 128), F32),
            jax.ShapeDtypeStruct((256, 128), F32),
            jax.ShapeDtypeStruct((32, 4, 512), F32),
        )
        vmem = pltpu.VMEM
        scratch = [
            vmem((5, 256, 128), F32), vmem((5, 256, 128), F32), vmem((5, 256, 128), F32),
            vmem((3, 256, 128), F32), vmem((3, 256, 128), F32), vmem((3, 128, 128), F32),
            vmem((2, 128, 128), F32), vmem((zh_count, 8, TILE_LANES), F32),
            vmem((zh_count, x_count - 1, 4, PARCEL_LANES), F32),
            vmem((zh_count, x_count - 1, 4, PARCEL_LANES), F32),
            vmem((4 * gx_count, PARCEL_LANES), F32),
            vmem((x_count, zh_count, 8, 128), F32), vmem((3, 4 * gx_count, 128), F32),
            vmem((3, 2, 5, 16, 128), F32), vmem((3, 2, 5, 16, 128), F32),
            vmem((3, 2, 5, 16, 128), F32), vmem((3, 2, 5, 16, 128), F32),
            vmem((3, 5, 16, 128), F32),
            vmem((3, 2, 16, 128), F32), vmem((3, 2, 8, 512), F32), vmem((3, 2, 8, 512), F32),
            vmem((2, 2, 16, 128), F32), vmem((3, 2, 8, 512), F32), vmem((3, 2, 8, 512), F32),
            vmem((32, 4, 512), F32), vmem((4, 32, 512), F32), vmem((4, 32, 512), F32),
            vmem((4, 32, 512), F32), vmem((2, 3, 4, 32, 128), F32), vmem((2, 2, 4, 32, 128), F32),
            vmem((512, 512), BF16), vmem((512, 512), BF16), vmem((256, 256), BF16),
            vmem((256, 256), BF16), vmem((256, 256), BF16), vmem((256, 256), BF16),
            vmem((512, 512), BF16),
            pltpu.SemaphoreType.DMA((11,)), pltpu.SemaphoreType.DMA((3,)),
            pltpu.SemaphoreType.DMA((3, 6)), pltpu.SemaphoreType.DMA((3, 6)),
            pltpu.SemaphoreType.DMA((3, 6)), pltpu.SemaphoreType.DMA((3, 6)),
            pltpu.SemaphoreType.DMA((PARTS * tile_sends,)),
            pltpu.SemaphoreType.DMA((PARTS * tile_sends,)),
            pltpu.SemaphoreType.DMA((label_sends,)), pltpu.SemaphoreType.DMA((label_sends,)),
        ]
        held_shape = tuple(pltpu.VMEM(o.shape, F32) for o in out_shape)
        outs = pl.pallas_call(
            functools.partial(kernel, zh_count, x_count, gy_count, gz_count),
            out_shape=held_shape,
            in_specs=[anywhere] * 4 + [scalars] * 2 + [anywhere] * 7,
            out_specs=[anywhere] * 3 + [pl.BlockSpec(memory_space=pltpu.VMEM)],
            scratch_shapes=scratch,
            compiler_params=pltpu.CompilerParams(
                collective_id=0, has_side_effects=True, vmem_limit_bytes=57 * 2**20
            ),
            cost_estimate=pl.CostEstimate(
                flops=10**9, bytes_accessed=4 * 2**20, transcendentals=0
            ),
        )(
            density.reshape(256, 128), momentum.reshape(3, 256, 128), energy.reshape(256, 128),
            acoustic.reshape(32, 4, 512), tile_slot, tile_element,
            *[jnp.asarray(c) for c in consts],
        )
        outs = pl.pallas_call(
            hand_over,
            out_shape=out_shape,
            in_specs=[anywhere] * 4,
            out_specs=[in_hbm] * 4,
            scratch_shapes=[pltpu.SemaphoreType.DMA((4,))],
            compiler_params=pltpu.CompilerParams(vmem_limit_bytes=8 * 2**20),
        )(*outs)
        return (
            outs[0].reshape(16, 16, 128), outs[1].reshape(3, 16, 16, 128),
            outs[2].reshape(16, 16, 128), outs[3].reshape(4, 2, 4, 4, 512),
        )

    in_specs = (
        P("gx", "gy", "gz"), P(None, "gx", "gy", "gz"), P("gx", "gy", "gz"),
        P(None, "gx", "gy", "gz", None), P("gx", "gy", "gz", None), P("gx", "gy", "gz", None),
    )
    out_specs = (
        P("gx", "gy", "gz"), P(None, "gx", "gy", "gz"), P("gx", "gy", "gz"),
        P(None, "gx", "gy", "gz", None),
    )
    return jax.shard_map(
        on_device, mesh=mesh, in_specs=in_specs, out_specs=out_specs, check_vma=False
    )
```
